32 devices in a mesh: row: 8 (over z, y), col: 4 (over x, core).
Axes of the slice: x: 2, y: 2, z: 4, core: 2. Of those that a mesh axis runs over, the one named last changes fastest.
Arguments:
- features: bfloat16 [4096, 2048], P(('row', 'col')), may hold values from -6 to 6
- neighbours: int32 [4096, 64], P('row', 'col'), may hold values from 0 to 1023
- edge_mask: int32 [4096, 64], P('row', 'col'), may hold values from 0 to 1, as said below
- weight: bfloat16 [2048, 2048], replicated, may hold values from -0.25 to 0.25
- bias: float32 [2048], replicated, may hold values from -4 to 4
- cotangent: bfloat16 [4096, 2048], P(('row', 'col')), may hold values from -6 to 6
Outputs:
- activations: bfloat16 [4096, 2048], P(('row', 'col'))
- feature_grad: float32 [4096, 2048], P(('row', 'col'))
- weight_grad: float32 [2048, 2048], replicated
- bias_grad: float32 [2048], replicated
The draws below stay inside these ranges and needn't reach their ends.
Inputs may be any that keep to these rules, and one draw needn't show every extreme that they name: `edge_mask`: in every row and column block the ones come first; in every draw some rows are full in every block (hubs).
All inputs are finite; a program needn't handle non-finite values.
Results may differ from the reference program's by a relative error of at most 0.012.
Values may be sent and summed in bfloat16 or wider, within the bound.
A program may use at most 128 MiB of HBM per device.

```python
import jax
import jax.numpy as jnp
from jax import lax

FEAT = 2048
SLOTS = 16
NODE_DEV = 128
NODES = 4096
N_ROW = 8
N_COL = 4


def draw_edge_mask(key, part):
    key = jax.random.fold_in(key, 7)
    hub_key, count_key = jax.random.split(key)
    hubs = jax.random.randint(hub_key, (NODES,), 0, 8) == 0
    forced = jnp.arange(NODES, dtype=jnp.int32) % 16 == 0
    counts = jax.random.randint(count_key, (NODES, N_COL), SLOTS // 4, SLOTS + 1)
    counts = jnp.where((hubs | forced)[:, None], SLOTS, counts)
    slot_index = jnp.arange(N_COL * SLOTS, dtype=jnp.int32)
    block_count = counts[:, slot_index // SLOTS]
    return (slot_index[None, :] % SLOTS < block_count).astype(jnp.int32)


def place_ends(array, stream_key, least, largest):
    index_at = [jax.random.randint(jax.random.fold_in(stream_key, axis), (), 0, length) for axis, length in enumerate(array.shape)]
    longest = array.shape.index(max(array.shape))
    next_to = index_at[:longest] + [(index_at[longest] + 1) % array.shape[longest]] + index_at[longest + 1:]
    return array.at[tuple(index_at)].set(least).at[tuple(next_to)].set(largest)


def block_levels(stream_key, extent, cuts, low, top_value):
    loudness, own = 1.0, jax.random.fold_in(stream_key, 6)
    for dim, blocks in cuts:
        draws = jnp.exp(jax.random.uniform(jax.random.fold_in(own, dim), (blocks,), jnp.float32, low / len(cuts), top_value / len(cuts)))
        loudness = loudness * jnp.repeat(draws, extent[dim] // blocks).reshape([-1 if axis == dim else 1 for axis in range(len(extent))])
    return loudness


def scatter_about(own_key, extent, width, bound, cuts=(), kind=jnp.bfloat16):
    result = width * jax.random.normal(own_key, extent, jnp.float32)
    if cuts:
        result = result * block_levels(own_key, extent, cuts, -0.22, 0.18)
    return jnp.clip(result, -bound, bound).astype(kind)


def setup_inputs(seed: int = 0) -> dict:
    seeds = jax.random.split(jax.random.key(seed), 7)
    features = scatter_about(seeds[0], (NODES, FEAT), 1.0, 6.0, ((0, 32),))
    neighbours = place_ends(jax.random.randint(seeds[1], (NODES, N_COL * SLOTS), 0, N_ROW * NODE_DEV), jax.random.fold_in(seeds[1], 1), 0, (N_ROW * NODE_DEV) - 1).astype(jnp.int32)
    edge_mask = draw_edge_mask(jax.random.fold_in(seeds[6], 71), 0)
    weight = scatter_about(seeds[3], (FEAT, FEAT), (FEAT // 4) ** -0.5, 0.25)
    bias = scatter_about(seeds[4], (FEAT,), 1.0, 4.0, (), jnp.float32)
    cotangent = scatter_about(seeds[5], (NODES, FEAT), 1.0, 6.0, ((0, 32),))
    return dict(features=features, neighbours=neighbours, edge_mask=edge_mask, weight=weight, bias=bias, cotangent=cotangent)


@jax.custom_vjp
def low(v):
    return lax.optimization_barrier(v.astype(jnp.bfloat16)).astype(jnp.float32)

@jax.custom_vjp
def low_back(v):
    return v

def low_keep(v):
    return (low(v), None)

def low_pass(kept, grad):
    return (grad,)

def back_keep(v):
    return (v, None)

def back_low(kept, grad):
    return (low(grad),)
low.defvjp(low_keep, low_pass)
low_back.defvjp(back_keep, back_low)

def aggregate(inputs_f, neighbours, edge_mask):
    column_block = jnp.arange(N_COL * SLOTS, dtype=jnp.int32) // SLOTS
    global_index = (neighbours // NODE_DEV * N_COL + column_block[None, :]) * NODE_DEV + neighbours % NODE_DEV
    weights = edge_mask.astype(jnp.float32)

    def one_slot(total, pair):
        index_col, weight_col = pair
        return (total + weight_col[:, None] * inputs_f[index_col], None)
    total, unused = lax.scan(jax.checkpoint(one_slot), jnp.zeros(inputs_f.shape, jnp.float32), (global_index.T.astype(jnp.int32), weights.T))
    return total

def reference(features, neighbours, edge_mask, weight, bias, cotangent):
    degree = lax.optimization_barrier(jnp.sum(edge_mask.astype(jnp.float32), axis=1))
    row_scale = 1.0 / (degree + 1.0)

    def forward(inputs_f, weight_f, bias_f):
        gathered = aggregate(inputs_f, neighbours, edge_mask)
        combined = low_back(gathered + 2.0 * inputs_f)
        aggregated = row_scale[:, None] * combined
        preact = jnp.dot(low(aggregated), weight_f, precision=lax.Precision.HIGHEST) + bias_f[None, :]
        preact = low_back(preact)
        return jax.nn.gelu(preact)
    activated, pullback = jax.vjp(forward, features.astype(jnp.float32), weight.astype(jnp.float32), bias)
    feature_grad, weight_grad, bias_grad = pullback(cotangent.astype(jnp.float32))
    return (activated.astype(jnp.bfloat16), feature_grad, weight_grad, bias_grad)
```

```python
import jax
import jax.numpy as jnp
from jax import lax
from jax.sharding import PartitionSpec as P


def slot_matrix(lists, mask_float, width):
    columns = jnp.arange(width, dtype=jnp.int32)
    total = jnp.zeros((lists.shape[0], width), jnp.float32)
    for slot_index in range(lists.shape[1]):
        total = total + jnp.where(
            lists[:, slot_index, None] == columns[None, :], mask_float[:, slot_index, None], 0.0
        )
    return total.astype(jnp.bfloat16)


def on_device(features, neighbours, edge_mask, weight, bias, cotangent):
    mask_float = edge_mask.astype(jnp.float32)
    column_rows = lax.all_gather(features, "row", axis=0, tiled=True)
    adjacency = slot_matrix(neighbours, mask_float, column_rows.shape[0])
    partial_value = jnp.dot(adjacency, column_rows, preferred_element_type=jnp.float32)
    edge_count = jnp.sum(mask_float, axis=1)
    summed, degree = (
        lax.psum_scatter(partial_value.astype(jnp.bfloat16), "col", scatter_dimension=0, tiled=True).astype(jnp.float32),
        lax.psum_scatter(edge_count, "col", scatter_dimension=0, tiled=True),
    )
    row_scale = 1.0 / (degree + 1.0)
    inputs_f = features.astype(jnp.float32)
    aggregated = row_scale[:, None] * (summed + 2.0 * inputs_f)
    aggregated_low = aggregated.astype(jnp.bfloat16)
    preact = jnp.dot(aggregated_low, weight, preferred_element_type=jnp.float32) + bias[None, :]
    activated, gelu_back = jax.vjp(jax.nn.gelu, preact)
    activations = activated.astype(jnp.bfloat16)
    preact_grad = gelu_back(cotangent.astype(jnp.float32))[0].astype(jnp.bfloat16)
    weight_term = lax.dot_general(
        aggregated_low, preact_grad, (((0,), (0,)), ((), ())), preferred_element_type=jnp.float32
    )
    weight_grad = lax.psum(weight_term.astype(jnp.bfloat16), ("row", "col")).astype(jnp.float32)
    bias_grad = lax.psum(jnp.sum(preact_grad.astype(jnp.float32), axis=0), ("row", "col"))
    grad_agg = lax.dot_general(
        preact_grad, weight, (((1,), (1,)), ((), ())), preferred_element_type=jnp.float32
    )
    combined_grad = (row_scale[:, None] * grad_agg).astype(jnp.bfloat16)
    block_grads = lax.all_gather(combined_grad, "col", axis=0, tiled=True)
    target = lax.dot_general(
        adjacency, block_grads, (((0,), (0,)), ((), ())), preferred_element_type=jnp.float32
    )
    returned = lax.psum_scatter(
        target.astype(jnp.bfloat16), "row", scatter_dimension=0, tiled=True
    ).astype(jnp.float32)
    feature_grad = returned + 2.0 * combined_grad.astype(jnp.float32)
    return (activations, feature_grad, weight_grad, bias_grad)


def solution(mesh):
    placed = (
        P(("row", "col"), None),
        P("row", "col"),
        P("row", "col"),
        P(),
        P(),
        P(("row", "col"), None),
    )
    return jax.shard_map(
        on_device,
        mesh=mesh,
        in_specs=placed,
        out_specs=(P(("row", "col"), None), P(("row", "col"), None), P(), P()),
        check_vma=False,
    )
```

```python
import functools

import jax
import jax.numpy as jnp
from jax import lax
from jax.experimental import pallas as pl
from jax.experimental.pallas import tpu as pltpu
from jax.sharding import PartitionSpec as P

MESH = pl.DeviceIdType.MESH
BF16, F32, I32 = jnp.bfloat16, jnp.float32, jnp.int32
NODE = 128
SPLIT = 4
CORES = 2


class Plan:
    def __init__(self, mesh, feat):
        self.rows, self.cols = mesh.shape["row"], mesh.shape["col"]
        self.nz, self.ny = SPLIT, self.rows // SPLIT
        self.nx = self.cols // CORES
        self.feat = feat
        self.slice = feat // self.nz
        self.columns = self.rows * NODE
        self.block = self.cols * NODE
        self.line = self.nz * self.block

    def place(self):
        row, col = lax.axis_index("row"), lax.axis_index("col")
        return row // self.ny, lax.rem(row, self.ny), col // CORES, lax.rem(col, CORES)

    def device(self, z, y, x, k):
        return (z * self.ny + y, x * CORES + k)


class Sends:
    def __init__(self, sems):
        self.sems, self.started = sems, []

    def __call__(self, src, dst, recv, device):
        copy = pltpu.make_async_remote_copy(
            src_ref=src,
            dst_ref=dst,
            send_sem=self.sems.at[len(self.started)],
            recv_sem=recv,
            device_id=device,
            device_id_type=MESH,
        )
        copy.start()
        self.started.append(copy)

    def finish(self):
        for copy in self.started:
            copy.wait_send()


def arrived(ref, recv, device):
    pltpu.make_async_remote_copy(
        src_ref=ref, dst_ref=ref, send_sem=recv, recv_sem=recv, device_id=device, device_id_type=MESH
    ).wait_recv()


def others(index, count):
    return [lax.rem(index + step, count) for step in range(1, count)]


def at(start, size, align=None):
    return pl.ds(pl.multiple_of(start, align or size), size)


def greet(devices):
    barrier = pltpu.get_barrier_semaphore()
    for device in devices:
        pl.semaphore_signal(barrier, inc=1, device_id=device, device_id_type=MESH)
    pl.semaphore_wait(barrier, len(devices))


def forward_kernel(
    plan, chunks, x_ref, codes_ref, w_hbm, bias_ref, cot_ref,
    act_ref, pg_ref, scaled_ref, agg_ref, adj_ref, bias_sum_ref,
    x_t, gathered, codes, count, degrees, w_ref, half_send, half_recv, x_send, x_recv, own, total, summed, agg_rows,
    w_sem, sems, codes_sem, degree_sem, slice_sem, line_sem, half_sem, x_sem, back_sem,
):
    nz, ny, nx, fs = plan.nz, plan.ny, plan.nx, plan.slice
    z, y, x, k = plan.place()
    send = Sends(sems)
    width = fs // chunks
    zs, ys, xs = others(z, nz), others(y, ny), others(x, nx)
    here = plan.device(z, y, x, k)
    mates = [plan.device(z, y, a, k) for a in xs] + [plan.device(z, y, x, 1 - k)] + [plan.device(z, y, a, 1 - k) for a in xs]
    mate_cols = [a * CORES + k for a in xs] + [x * CORES + 1 - k] + [a * CORES + 1 - k for a in xs]

    w_copy = pltpu.make_async_copy(w_hbm, w_ref, w_sem)
    w_copy.start()

    def turn(step, carry):
        cols = at(step * NODE, NODE)
        x_t[cols, :] = x_ref[:, cols].astype(F32).T.astype(BF16)
        return carry

    lax.fori_loop(0, plan.feat // NODE, turn, 0)
    for c in range(plan.cols):
        part = codes_ref[:, c * NODE : (c + 1) * NODE]
        ones = jnp.sum(jnp.where(part >= 0, 1.0, 0.0), axis=0, keepdims=True)
        count[c] = jnp.broadcast_to(ones, (8, NODE))

    greet([plan.device(a, y, x, k) for a in zs] + [plan.device(z, a, x, k) for a in ys] + mates)

    mine = at((y * nz + z) * NODE, NODE)
    for a in zs:
        send(codes_ref, codes.at[z], codes_sem.at[z], plan.device(a, y, x, k))
    for chunk in range(chunks):
        for a in zs:
            send(
                x_t.at[at(a * fs + chunk * width, width)],
                gathered.at[pl.ds(chunk * width, width), mine],
                slice_sem.at[chunk, z],
                plan.device(a, y, x, k),
            )
        for b in ys:
            send(
                x_t.at[at(z * fs + chunk * width, width)],
                gathered.at[pl.ds(chunk * width, width), mine],
                line_sem.at[chunk, z, y],
                plan.device(z, b, x, k),
            )
    col = x * CORES + k
    for device, c in zip(mates, mate_cols):
        send(count.at[c], degrees.at[col], degree_sem.at[col], device)
    gathered[:, mine] = x_t[at(z * fs, fs), :]
    degrees[col] = count[col]

    groups = (plan.rows + 3) // 4
    strip = 64

    def build(a, source):
        for c in range(plan.cols):
            columns = at((((c % CORES) * nx + c // CORES) * nz + a) * NODE, NODE)
            part = source[:, c * NODE : (c + 1) * NODE]
            low = jnp.where(part >= 0, part % NODE, -1)
            high = jnp.where(part >= 0, part // NODE, -1)
            adds = [
                sum(jnp.where(high == 4 * g + i, 1 << (8 * i), 0) for i in range(4) if 4 * g + i < plan.rows)
                for g in range(groups)
            ]
            for start in range(0, NODE, strip):
                lanes = lax.broadcasted_iota(I32, (strip, NODE), 0) + start
                packed = [jnp.zeros((strip, NODE), I32) for _ in range(groups)]
                for s in range(part.shape[0]):
                    hit = low[s : s + 1, :] == lanes
                    packed = [p + jnp.where(hit, v[s : s + 1, :], 0) for p, v in zip(packed, adds)]
                for r in range(plan.rows):
                    row = ((r % ny) * nz + r // ny) * NODE + start
                    number = (packed[r // 4] >> (8 * (r % 4))) & 255
                    adj_ref[row : row + strip, columns] = number.astype(F32).astype(BF16)

    build(z, codes_ref)
    for a in zs:
        arrived(codes.at[a], codes_sem.at[a], here)
        build(a, codes.at[a])

    def block_of(a, b):
        return at((b * nz + a) * NODE, NODE)

    def pass_on(chunk):
        rows = pl.ds(chunk * width, width)
        for a in zs:
            piece = gathered.at[rows, block_of(a, y)]
            arrived(piece, slice_sem.at[chunk, a], here)
            for b in ys:
                send(piece, piece, line_sem.at[chunk, a, y], plan.device(z, b, x, k))

    tile = 256
    half = plan.line // 2
    third = half // nx

    def product(chunk, columns_from, count_, store):
        rows = pl.ds(chunk * width, width)

        def step(i, carry):
            offset = i * tile
            store(
                at(offset, tile),
                jnp.dot(gathered[rows, :], adj_ref[:, at(columns_from + offset, tile)], preferred_element_type=F32),
            )
            return carry

        lax.fori_loop(0, count_ // tile, step, 0)

    def first(chunk):
        rows = pl.ds(chunk * width, width)
        for a in range(nz):
            for b in ys:
                arrived(gathered.at[rows, block_of(a, b)], line_sem.at[chunk, a, b], here)

        def to_half(cols, value):
            half_send[chunk, :, cols] = value.astype(BF16)

        product(chunk, (1 - k) * half, half, to_half)
        send(half_send.at[chunk], half_recv.at[chunk], half_sem.at[chunk], plan.device(z, y, x, 1 - k))

        def to_own(cols, value):
            own[chunk, :, cols] = value

        product(chunk, k * half, half, to_own)

    def second(chunk):
        arrived(half_recv.at[chunk], half_sem.at[chunk], here)
        for a in xs:
            cols = at(a * third, third)
            x_send[chunk, :, cols] = (own[chunk, :, cols] + half_recv[chunk, :, cols].astype(F32)).astype(BF16)
            send(x_send.at[chunk, :, cols], x_recv.at[chunk, x], x_sem.at[chunk, x], plan.device(z, y, a, k))

    def last(chunk):
        cols = at(x * third, third)
        value = own[chunk, :, cols] + half_recv[chunk, :, cols].astype(F32)
        for a in xs:
            arrived(x_recv.at[chunk, a], x_sem.at[chunk, a], here)
            value = value + x_recv[chunk, a].astype(F32)
        total[chunk] = value.astype(BF16)
        rows = at(z * fs + chunk * width, width)
        for a in zs:
            send(total.at[chunk, :, at(a * NODE, NODE)], summed.at[rows], back_sem.at[chunk, z], plan.device(a, y, x, k))
        summed[rows, :] = total[chunk, :, at(z * NODE, NODE)]

    pass_on(0)
    for chunk in range(chunks):
        first(chunk)
        if chunk + 1 < chunks:
            pass_on(chunk + 1)
        second(chunk)
    for chunk in range(chunks):
        last(chunk)

    for device, c in zip(mates, mate_cols):
        arrived(degrees.at[c], degree_sem.at[c], here)
    degree = degrees[0]
    for c in range(1, plan.cols):
        degree = degree + degrees[c]
    scale = 1.0 / (degree[0:1, :] + 1.0)
    scale_col = jnp.broadcast_to(scale, (NODE, NODE)).T[:, 0:1]
    w_copy.wait()
    for chunk in range(chunks):
        for a in zs:
            rows = at(a * fs + chunk * width, width)
            arrived(summed.at[rows], back_sem.at[chunk, a], here)

    def combine(step, carry):
        rows = at(step * NODE, NODE)
        value = scale * (summed[rows, :].astype(F32) + 2.0 * x_t[rows, :].astype(F32))
        agg_ref[rows, :] = value.astype(BF16)
        agg_rows[:, rows] = value.T.astype(BF16)
        return carry

    lax.fori_loop(0, plan.feat // NODE, combine, 0)

    def layer(step, carry):
        cols = at(step * tile, tile)
        pre = jnp.dot(agg_rows[...], w_ref[:, cols], preferred_element_type=F32) + bias_ref[:, cols]
        square = pre * pre
        slope = 0.7978845608028654
        t = jnp.tanh(slope * pre * (1.0 + 0.044715 * square))
        act_ref[:, cols] = (0.5 * pre * (1.0 + t)).astype(BF16)
        grad = 0.5 * (1.0 + t) + 0.5 * pre * (1.0 - t * t) * (slope * (1.0 + 3.0 * 0.044715 * square))
        low = (cot_ref[:, cols].astype(F32) * grad).astype(BF16)
        pg_ref[:, cols] = low
        wide = low.astype(F32)
        scaled_ref[:, cols] = (scale_col * wide).astype(BF16)
        bias_sum_ref[:, cols] = jnp.sum(wide, axis=0, keepdims=True)
        return carry

    lax.fori_loop(0, plan.feat // tile, layer, 0)
    send.finish()


def forward_part(plan, features, codes, weight, bias, cotangent, chunks=2):
    feat, fs = plan.feat, plan.slice
    width = fs // chunks
    half = plan.line // 2
    third = half // plan.nx
    n_sends = (
        (plan.nz - 1) * (1 + 2 * chunks) + plan.cols - 1 + chunks * plan.nz * (plan.ny - 1) + chunks * plan.nx
    )
    dma = pltpu.SemaphoreType.DMA
    vmem = pl.BlockSpec(memory_space=pltpu.VMEM)
    return pl.pallas_call(
        functools.partial(forward_kernel, plan, chunks),
        name="forward",
        out_shape=(
            jax.ShapeDtypeStruct((NODE, feat), BF16),
            jax.ShapeDtypeStruct((NODE, feat), BF16),
            jax.ShapeDtypeStruct((NODE, feat), BF16),
            jax.ShapeDtypeStruct((feat, NODE), BF16),
            jax.ShapeDtypeStruct((plan.columns, plan.line), BF16),
            jax.ShapeDtypeStruct((1, feat), F32),
        ),
        in_specs=[vmem, vmem, pl.BlockSpec(memory_space=pl.ANY), vmem, vmem],
        out_specs=(vmem,) * 6,
        scratch_shapes=[
            pltpu.VMEM((feat, NODE), BF16),
            pltpu.VMEM((fs, plan.columns), BF16),
            pltpu.VMEM((plan.nz,) + codes.shape, I32),
            pltpu.VMEM((plan.cols, 8, NODE), F32),
            pltpu.VMEM((plan.cols, 8, NODE), F32),
            pltpu.VMEM(weight.shape, BF16),
            pltpu.VMEM((chunks, width, half), BF16),
            pltpu.VMEM((chunks, width, half), BF16),
            pltpu.VMEM((chunks, width, half), BF16),
            pltpu.VMEM((chunks, plan.nx, width, third), BF16),
            pltpu.VMEM((chunks, width, half), F32),
            pltpu.VMEM((chunks, width, third), BF16),
            pltpu.VMEM((feat, NODE), BF16),
            pltpu.VMEM((NODE, feat), BF16),
            dma(()),
            dma((n_sends,)),
            dma((plan.nz,)),
            dma((plan.cols,)),
            dma((chunks, plan.nz)),
            dma((chunks, plan.nz, plan.ny)),
            dma((chunks,)),
            dma((chunks, plan.nx)),
            dma((chunks, plan.nz)),
        ],
        compiler_params=pltpu.CompilerParams(
            collective_id=0, has_side_effects=True, vmem_limit_bytes=63 << 20
        ),
    )(features, codes, weight, bias, cotangent)


def backward_kernel(
    plan, wide_chunks, back_chunks, pg_ref, scaled_ref, agg_ref, adj_ref, bias_ref, w_hbm,
    fg_ref, low_hbm, bias_grad_ref,
    w_ref, agg_all, pg_all, grads, half_send, half_recv, own_tile, sum_send, sum_recv, final,
    y_send, y_recv, own_target, back, returned, bias_k, bias_x, bias_y, bias_z, bias_sums,
    local_sem, sems, agg_x_sem, agg_y_sem, pg_y_sem, pg_x_sem, slice_sem, grads_x_sem, grads_k_sem,
    half_sem, sum_sem, gather_sem, y_sem, back_sem, bias_k_sem, bias_x_sem, bias_y_sem, bias_z_sem,
):
    nz, ny, nx, fs, feat = plan.nz, plan.ny, plan.nx, plan.slice, plan.feat
    z, y, x, k = plan.place()
    send = Sends(sems)
    zs, ys, xs = others(z, nz), others(y, ny), others(x, nx)
    here, twin = plan.device(z, y, x, k), plan.device(z, y, x, 1 - k)
    fa, fp = feat // nx, feat // ny
    fh, fw = fa // CORES, fp // wide_chunks
    fz = fh // nz
    group = nz * NODE
    wb = fs // back_chunks

    w_copy = pltpu.make_async_copy(w_hbm, w_ref, local_sem.at[wide_chunks])
    w_copy.start()
    greet(
        [plan.device(a, y, x, k) for a in zs]
        + [plan.device(z, b, x, k) for b in ys]
        + [plan.device(z, y, a, k) for a in xs]
        + [twin]
    )

    def nodes(b, a):
        return at((b * nx + a) * NODE, NODE)

    for a in xs:
        send(agg_ref.at[at(a * fa, fa)], agg_all.at[:, nodes(y, x)], agg_x_sem.at[x], plan.device(z, y, a, k))
    for b in ys:
        send(pg_ref.at[:, at(b * fp, fp)], pg_all.at[nodes(y, x)], pg_y_sem.at[y], plan.device(z, b, x, k))
    for chunk in range(back_chunks):
        for a in zs:
            send(
                scaled_ref.at[:, at(a * fs + chunk * wb, wb)],
                grads.at[at(((k * nx + x) * nz + z) * NODE, NODE), pl.ds(chunk * wb, wb)],
                slice_sem.at[chunk, z],
                plan.device(a, y, x, k),
            )
    for b in ys:
        send(agg_ref.at[at(x * fa, fa)], agg_all.at[:, nodes(y, x)], agg_y_sem.at[y, x], plan.device(z, b, x, k))
    for a in xs:
        send(pg_ref.at[:, at(y * fp, fp)], pg_all.at[nodes(y, x)], pg_x_sem.at[y, x], plan.device(z, y, a, k))
    send(bias_ref, bias_k, bias_k_sem, twin)
    agg_all[:, nodes(y, x)] = agg_ref[at(x * fa, fa), :]
    pg_all[nodes(y, x), :] = pg_ref[:, at(y * fp, fp)]
    grads[at(((k * nx + x) * nz + z) * NODE, NODE), :] = scaled_ref[:, at(z * fs, fs)]

    for a in xs:
        ref = agg_all.at[:, nodes(y, a)]
        arrived(ref, agg_x_sem.at[a], here)
        for b in ys:
            send(ref, ref, agg_y_sem.at[y, a], plan.device(z, b, x, k))
    for b in ys:
        ref = pg_all.at[nodes(b, x)]
        arrived(ref, pg_y_sem.at[b], here)
        for a in xs:
            send(ref, ref, pg_x_sem.at[b, x], plan.device(z, y, a, k))

    arrived(bias_k, bias_k_sem, here)
    bias_sums[0] = bias_ref[...] + bias_k[...]
    for a in xs:
        send(bias_sums.at[0], bias_x.at[x], bias_x_sem.at[x], plan.device(z, y, a, k))
    bias_x[x] = bias_sums[0]

    def line_rows(c, a):
        return at((c * nx + a) * group, group)

    for chunk in range(back_chunks):
        cols = pl.ds(chunk * wb, wb)
        for a in zs:
            arrived(grads.at[at(((k * nx + x) * nz + a) * NODE, NODE), cols], slice_sem.at[chunk, a], here)
        ref = grads.at[line_rows(k, x), cols]
        for a in xs:
            send(ref, ref, grads_x_sem.at[chunk, x], plan.device(z, y, a, k))
        send(ref, ref, grads_k_sem.at[chunk, x], twin)

    for b in ys:
        for a in range(nx):
            arrived(agg_all.at[:, nodes(b, a)], agg_y_sem.at[b, a], here)
    for a in xs:
        for b in range(ny):
            arrived(pg_all.at[nodes(b, a)], pg_x_sem.at[b, a], here)

    tile = min(256, fh)

    def product(rows_from, chunk, store):
        def step(i, carry):
            rows = agg_all[at(rows_from + i * tile, tile), :]
            store(
                at(i * tile, tile),
                jnp.dot(rows, pg_all[:, chunk * fw : (chunk + 1) * fw], preferred_element_type=F32),
            )
            return carry

        lax.fori_loop(0, fh // tile, step, 0)

    for chunk in range(wide_chunks):
        def to_half(rows, value):
            half_send[chunk, rows, :] = value.astype(BF16)

        product((1 - k) * fh, chunk, to_half)
        send(half_send.at[chunk], half_recv.at[chunk], half_sem.at[chunk], twin)
    for chunk in range(wide_chunks):
        def to_own(rows, value):
            own_tile[chunk, rows, :] = value

        product(k * fh, chunk, to_own)
    for chunk in range(wide_chunks):
        arrived(half_recv.at[chunk], half_sem.at[chunk], here)
        for a in zs:
            rows = at(a * fz, fz)
            sum_send[chunk, rows, :] = (own_tile[chunk, rows, :] + half_recv[chunk, rows, :].astype(F32)).astype(BF16)
            send(sum_send.at[chunk, rows], sum_recv.at[chunk, z], sum_sem.at[chunk, z], plan.device(a, y, x, k))

    def bias_stage(ref, sem, count, peers, stage, onward):
        for a in peers:
            arrived(ref.at[a], sem.at[a], here)
        value = ref[0]
        for a in range(1, count):
            value = value + ref[a]
        if onward is None:
            bias_grad_ref[...] = value
        else:
            next_ref, next_sem, index, devices = onward
            bias_sums[stage] = value
            next_ref[index] = value
            for device in devices:
                send(bias_sums.at[stage], next_ref.at[index], next_sem.at[index], device)

    bias_stage(bias_x, bias_x_sem, nx, xs, 1, (bias_y, bias_y_sem, y, [plan.device(z, b, x, k) for b in ys]))

    for chunk in range(back_chunks):
        cols = pl.ds(chunk * wb, wb)
        for a in xs:
            ref = grads.at[line_rows(k, a), cols]
            arrived(ref, grads_x_sem.at[chunk, a], here)
            send(ref, ref, grads_k_sem.at[chunk, a], twin)
    for chunk in range(back_chunks):
        cols = pl.ds(chunk * wb, wb)
        for a in range(nx):
            arrived(grads.at[line_rows(1 - k, a), cols], grads_k_sem.at[chunk, a], here)

        def target(b, store):
            def step(i, carry):
                rows = adj_ref[at(b * group + i * tile, tile), :]
                store(at(i * tile, tile), jnp.dot(rows, grads[:, cols], preferred_element_type=F32))
                return carry

            lax.fori_loop(0, group // tile, step, 0)

        for i, b in enumerate(ys):
            def to_y(rows, value):
                y_send[chunk, i, rows, :] = value.astype(BF16)

            target(b, to_y)
            send(y_send.at[chunk, i], y_recv.at[chunk, ny - 2 - i], y_sem.at[chunk, ny - 2 - i], plan.device(z, b, x, k))

        def to_target(rows, value):
            own_target[chunk, rows, :] = value

        target(y, to_target)
    bias_stage(bias_y, bias_y_sem, ny, ys, 2, (bias_z, bias_z_sem, z, [plan.device(a, y, x, k) for a in zs]))

    def piece(chunk, a_z, a_y, a_x, a_k):
        return low_hbm.at[at(a_x * fa + a_k * fh + a_z * fz, fz), at(a_y * fp + chunk * fw, fw)]

    def gather(source, chunk, origin, devices):
        for device in devices:
            send(source, piece(chunk, *origin), gather_sem.at[(chunk,) + origin], device)

    def await_piece(chunk, *origin):
        arrived(piece(chunk, *origin), gather_sem.at[(chunk,) + origin], here)

    to_z = [plan.device(a, y, x, k) for a in zs]
    to_y_ = [plan.device(z, b, x, k) for b in ys]
    to_x = [plan.device(z, y, a, k) for a in xs]
    locals_ = []
    for chunk in range(wide_chunks):
        rows = at(z * fz, fz)
        value = own_tile[chunk, rows, :] + half_recv[chunk, rows, :].astype(F32)
        for a in zs:
            arrived(sum_recv.at[chunk, a], sum_sem.at[chunk, a], here)
            value = value + sum_recv[chunk, a].astype(F32)
        final[chunk] = value.astype(BF16)
        gather(final.at[chunk], chunk, (z, y, x, k), to_z + to_x + to_y_ + [twin])
        copy = pltpu.make_async_copy(final.at[chunk], piece(chunk, z, y, x, k), local_sem.at[chunk])
        copy.start()
        locals_.append(copy)

    for chunk in range(back_chunks):
        value = own_target[chunk]
        for i in range(ny - 1):
            arrived(y_recv.at[chunk, i], y_sem.at[chunk, i], here)
            value = value + y_recv[chunk, i].astype(F32)
        back[chunk] = value.astype(BF16)
        cols = at(z * fs + chunk * wb, wb)
        for a in zs:
            send(back.at[chunk, at(a * NODE, NODE)], returned.at[:, cols], back_sem.at[chunk, z], plan.device(a, y, x, k))
        returned[:, cols] = back[chunk, at(z * NODE, NODE), :]

    order = [z] + zs
    for chunk in range(wide_chunks):
        for a in zs:
            await_piece(chunk, a, y, x, k)
            gather(piece(chunk, a, y, x, k), chunk, (a, y, x, k), to_x + to_y_ + [twin])
        for step, a in enumerate(order):
            for a_x in xs:
                await_piece(chunk, a, y, a_x, k)
                gather(piece(chunk, a, y, a_x, k), chunk, (a, y, a_x, k), (to_y_ if step % 2 == 0 else []) + [twin])
            for a_y in ys:
                await_piece(chunk, a, a_y, x, k)
                gather(piece(chunk, a, a_y, x, k), chunk, (a, a_y, x, k), (to_x if step % 2 == 1 else []) + [twin])

    w_copy.wait()
    for chunk in range(back_chunks):
        for a in zs:
            cols = at(a * fs + chunk * wb, wb)
            arrived(returned.at[:, cols], back_sem.at[chunk, a], here)
    scaled_ref_value = (returned[...].astype(F32) + 2.0 * scaled_ref[...].astype(F32)).astype(BF16)
    returned[...] = scaled_ref_value

    def through(step, carry):
        rows = at(step * 256, 256)
        fg_ref[:, rows] = lax.dot_general(
            returned[...], w_ref[rows, :], (((1,), (1,)), ((), ())), preferred_element_type=F32
        )
        return carry

    lax.fori_loop(0, feat // 256, through, 0)
    bias_stage(bias_z, bias_z_sem, nz, zs, 3, None)

    for chunk in range(wide_chunks):
        for a in order:
            for a_x in xs:
                for a_y in ys:
                    await_piece(chunk, a, a_y, a_x, k)
                    gather(piece(chunk, a, a_y, a_x, k), chunk, (a, a_y, a_x, k), [twin])
    for chunk in range(wide_chunks):
        for a in range(nz):
            for a_y in range(ny):
                for a_x in range(nx):
                    await_piece(chunk, a, a_y, a_x, 1 - k)
    for copy in locals_:
        copy.wait()
    send.finish()


def backward_part(plan, preact_grad, scaled, agg_t, adjacency, bias_term, weight, wide_chunks=2, back_chunks=2):
    nz, ny, nx, fs, feat = plan.nz, plan.ny, plan.nx, plan.slice, plan.feat
    fa, fp = feat // nx, feat // ny
    fh, fw = fa // CORES, fp // wide_chunks
    fz = fh // nz
    group, wb, depth = nz * NODE, fs // back_chunks, ny * nx * NODE
    dz, dy, dx = nz - 1, ny - 1, nx - 1
    n_sends = (
        dx + dy + back_chunks * dz + dy + dx + 1 + 2 * dx * dy + dx + back_chunks * (dx + 1)
        + wide_chunks * (1 + dz) + dy + back_chunks * dx + back_chunks * dy + dz
        + wide_chunks * (dz + dx + dy + 1) + back_chunks * dz
        + wide_chunks * (dz * (dx + dy + 1) + nz * (dx + dy) + 2 * nz * dx * dy + nz * dx * dy)
    )
    dma = pltpu.SemaphoreType.DMA
    vmem = pl.BlockSpec(memory_space=pltpu.VMEM)
    hbm = pl.BlockSpec(memory_space=pl.ANY)
    return pl.pallas_call(
        functools.partial(backward_kernel, plan, wide_chunks, back_chunks),
        name="backward",
        out_shape=(
            jax.ShapeDtypeStruct((NODE, feat), F32),
            jax.ShapeDtypeStruct((feat, feat), BF16),
            jax.ShapeDtypeStruct((1, feat), F32),
        ),
        in_specs=[vmem] * 5 + [hbm],
        out_specs=(vmem, hbm, vmem),
        scratch_shapes=[
            pltpu.VMEM(weight.shape, BF16),
            pltpu.VMEM((fa, depth), BF16),
            pltpu.VMEM((depth, fp), BF16),
            pltpu.VMEM((plan.line, fs), BF16),
            pltpu.VMEM((wide_chunks, fh, fw), BF16),
            pltpu.VMEM((wide_chunks, fh, fw), BF16),
            pltpu.VMEM((wide_chunks, fh, fw), F32),
            pltpu.VMEM((wide_chunks, fh, fw), BF16),
            pltpu.VMEM((wide_chunks, nz, fz, fw), BF16),
            pltpu.VMEM((wide_chunks, fz, fw), BF16),
            pltpu.VMEM((back_chunks, ny - 1, group, wb), BF16),
            pltpu.VMEM((back_chunks, ny - 1, group, wb), BF16),
            pltpu.VMEM((back_chunks, group, wb), F32),
            pltpu.VMEM((back_chunks, group, wb), BF16),
            pltpu.VMEM((NODE, feat), BF16),
            pltpu.VMEM((1, feat), F32),
            pltpu.VMEM((nx, 1, feat), F32),
            pltpu.VMEM((ny, 1, feat), F32),
            pltpu.VMEM((nz, 1, feat), F32),
            pltpu.VMEM((3, 1, feat), F32),
            dma((wide_chunks + 1,)),
            dma((n_sends,)),
            dma((nx,)),
            dma((ny, nx)),
            dma((ny,)),
            dma((ny, nx)),
            dma((back_chunks, nz)),
            dma((back_chunks, nx)),
            dma((back_chunks, nx)),
            dma((wide_chunks,)),
            dma((wide_chunks, nz)),
            dma((wide_chunks, nz, ny, nx, CORES)),
            dma((back_chunks, ny - 1)),
            dma((back_chunks, nz)),
            dma(()),
            dma((nx,)),
            dma((ny,)),
            dma((nz,)),
        ],
        compiler_params=pltpu.CompilerParams(
            collective_id=1, has_side_effects=True, vmem_limit_bytes=127 << 19
        ),
    )(preact_grad, scaled, agg_t, adjacency, bias_term, weight)


def on_device(plan, features, neighbours, edge_mask, weight, bias, cotangent):
    codes = jnp.where(edge_mask > 0, neighbours, -1).T
    activations, preact_grad, scaled, agg_t, adjacency, bias_term = forward_part(
        plan, features, codes, weight, bias.reshape(1, -1), cotangent
    )
    feature_grad, weight_low, bias_grad = backward_part(
        plan, preact_grad, scaled, agg_t, adjacency, bias_term, weight
    )
    return activations, feature_grad, weight_low.astype(F32), bias_grad.reshape(-1)


def solution(mesh):
    placed = (
        P(("row", "col"), None),
        P("row", "col"),
        P("row", "col"),
        P(),
        P(),
        P(("row", "col"), None),
    )

    def run(*args):
        plan = Plan(mesh, args[0].shape[1])
        return jax.shard_map(
            functools.partial(on_device, plan),
            mesh=mesh,
            in_specs=placed,
            out_specs=(P(("row", "col"), None), P(("row", "col"), None), P(), P()),
            check_vma=False,
        )(*args)

    return run
```

```python
import functools

import jax
import jax.numpy as jnp
from jax import lax
from jax.experimental import pallas as pl
from jax.experimental.pallas import tpu as pltpu
from jax.sharding import PartitionSpec as P

MESH = pl.DeviceIdType.MESH
BF16, F32, I32 = jnp.bfloat16, jnp.float32, jnp.int32
DMA = pltpu.SemaphoreType.DMA
NODE = 128
SPLIT = 4
CORES = 2
CHUNKS = 4
WIDE = 2
BACK = 2


class Plan:
    def __init__(self, mesh, feat, slots):
        rows, cols = mesh.shape["row"], mesh.shape["col"]
        self.rows, self.cols, self.feat, self.slots = rows, cols, feat, slots
        self.nz, self.ny, self.nx = SPLIT, rows // SPLIT, cols // CORES
        self.slice = feat // self.nz
        self.width = self.slice // CHUNKS
        self.columns = rows * NODE
        self.block = cols * NODE
        self.line = self.nz * self.block
        self.half = self.line // CORES
        self.third = self.half // self.nx
        self.fa, self.fp = feat // self.nx, feat // self.ny
        self.fh, self.fw = self.fa // CORES, self.fp // WIDE
        self.fz = self.fh // self.nz
        self.group = self.nz * NODE
        self.wb = self.slice // BACK
        self.depth = self.ny * self.nx * NODE
        self.merged = self.columns * self.line <= 1 << 22

    def place(self):
        row, col = lax.axis_index("row"), lax.axis_index("col")
        return row // self.ny, lax.rem(row, self.ny), col // CORES, lax.rem(col, CORES)

    def device(self, z, y, x, k):
        return (z * self.ny + y, x * CORES + k)


class Refs:
    def __init__(self, names, refs):
        self.__dict__.update(zip(names, refs, strict=True))


def guarded(when, act):
    if when is None:
        act()
    else:
        pl.when(when)(act)


class Sends:
    def __init__(self, sems):
        self.sems, self.started = sems, []

    def __call__(self, src, dst, recv, device, when=None):
        copy = pltpu.make_async_remote_copy(
            src_ref=src,
            dst_ref=dst,
            send_sem=self.sems.at[len(self.started)],
            recv_sem=recv,
            device_id=device,
            device_id_type=MESH,
        )
        guarded(when, copy.start)
        self.started.append((copy, when))

    def finish(self):
        for copy, when in self.started:
            guarded(when, copy.wait_send)


def others(index, count):
    return [lax.rem(index + step, count) for step in range(1, count)]


def at(start, size):
    return pl.ds(pl.multiple_of(start, size), size)


def loop(count, step):
    if count <= 4:
        for i in range(count):
            step(i)
    else:

        def body(i, carry):
            step(i)
            return carry

        lax.fori_loop(0, count, body, 0)


def greet(devices):
    barrier = pltpu.get_barrier_semaphore()
    for device in devices:
        pl.semaphore_signal(barrier, inc=1, device_id=device, device_id_type=MESH)
    pl.semaphore_wait(barrier, len(devices))


class Step:
    def __init__(self, plan, refs):
        self.plan, self.r = plan, refs
        self.z, self.y, self.x, self.k = z, y, x, k = plan.place()
        self.zs, self.ys, self.xs = others(z, plan.nz), others(y, plan.ny), others(x, plan.nx)
        self.here, self.twin = plan.device(z, y, x, k), plan.device(z, y, x, 1 - k)
        self.to_z = [plan.device(a, y, x, k) for a in self.zs]
        self.to_y = [plan.device(z, b, x, k) for b in self.ys]
        self.to_x = [plan.device(z, y, a, k) for a in self.xs]
        self.to_far = [plan.device(z, y, a, 1 - k) for a in self.xs]
        self.send = Sends(refs.sems)

    def arrived(self, ref, sem):
        pltpu.make_async_remote_copy(
            src_ref=ref, dst_ref=ref, send_sem=sem, recv_sem=sem, device_id=self.here, device_id_type=MESH
        ).wait_recv()

    def weight_copies(self):
        plan, r = self.plan, self.r
        copies = []
        for chunk in range(CHUNKS):
            for a in range(plan.nz):
                i = chunk * plan.nz + a
                copies.append(
                    pltpu.make_async_copy(
                        r.w_hbm.at[pl.ds(a * plan.slice + chunk * plan.width, plan.width)],
                        r.w.at[pl.ds(i * plan.width, plan.width)],
                        r.w_sem.at[i],
                    )
                )
        return copies


def forward_half(s, w_copies, agg_ready, pg_ready):
    plan, r, send = s.plan, s.r, s.send
    nz, ny, nx, fs, width = plan.nz, plan.ny, plan.nx, plan.slice, plan.width
    half, third = plan.half, plan.third
    z, y, x, k = s.z, s.y, s.x, s.k

    mates = s.to_x + [s.twin] + s.to_far
    mate_cols = [a * CORES + k for a in s.xs] + [x * CORES + 1 - k] + [a * CORES + 1 - k for a in s.xs]
    col = x * CORES + k
    mine = at((y * nz + z) * NODE, NODE)

    for device in s.to_z:
        send(r.codes, r.line_codes.at[z], r.codes_sem.at[z], device)
    for chunk in range(CHUNKS):
        rows = pl.ds(chunk * width, width)
        for a, device in zip(s.zs, s.to_z):
            send(r.x_t.at[at(a * fs + chunk * width, width)], r.gathered.at[rows, mine], r.slice_sem.at[chunk, z], device)
        for device in s.to_y:
            send(r.x_t.at[at(z * fs + chunk * width, width)], r.gathered.at[rows, mine], r.line_sem.at[chunk, z, y], device)
    for device, c in zip(mates, mate_cols):
        send(r.count.at[c], r.degrees.at[col], r.degree_sem.at[col], device)
    r.gathered[:, mine] = r.x_t[at(z * fs, fs), :]
    r.degrees[col] = r.count[col]

    groups = (plan.rows + 3) // 4
    strip = 32

    def build(a, source):
        for c in range(plan.cols):
            columns = at((((c % CORES) * nx + c // CORES) * nz + a) * NODE, NODE)
            part = source[:, c * NODE : (c + 1) * NODE]
            low = jnp.where(part >= 0, part % NODE, -1)
            high = jnp.where(part >= 0, part // NODE, -1)
            adds = [
                sum(jnp.where(high == 4 * g + i, 1 << (8 * i), 0) for i in range(4) if 4 * g + i < plan.rows)
                for g in range(groups)
            ]
            for start in range(0, NODE, strip):
                lanes = lax.broadcasted_iota(I32, (strip, NODE), 0) + start
                packed = [jnp.zeros((strip, NODE), I32) for _ in range(groups)]
                for slot in range(plan.slots):
                    hit = low[slot : slot + 1, :] == lanes
                    packed = [p + jnp.where(hit, v[slot : slot + 1, :], 0) for p, v in zip(packed, adds)]
                for row in range(plan.rows):
                    start_row = ((row % ny) * nz + row // ny) * NODE + start
                    number = (packed[row // 4] >> (8 * (row % 4))) & 255
                    r.adj[start_row : start_row + strip, columns] = number.astype(F32).astype(BF16)

    def build_from(a):
        s.arrived(r.line_codes.at[a], r.codes_sem.at[a])
        build(a, r.line_codes.at[a])

    def block_of(a, b):
        return at((b * nz + a) * NODE, NODE)

    def pass_on(chunk):
        rows = pl.ds(chunk * width, width)
        for a in s.zs:
            piece = r.gathered.at[rows, block_of(a, y)]
            s.arrived(piece, r.slice_sem.at[chunk, a])
            for device in s.to_y:
                send(piece, piece, r.line_sem.at[chunk, a, y], device)

    tile = 256

    def product(chunk, columns_from, store):
        rows = pl.ds(chunk * width, width)

        def step(i):
            columns = r.adj[:, at(columns_from + i * tile, tile)]
            store(at(i * tile, tile), jnp.dot(r.gathered[rows, :], columns, preferred_element_type=F32))

        loop(half // tile, step)

    def first(chunk):
        rows = pl.ds(chunk * width, width)
        for a in range(nz):
            for b in s.ys:
                s.arrived(r.gathered.at[rows, block_of(a, b)], r.line_sem.at[chunk, a, b])

        def to_half(cols, value):
            r.half_send[chunk, :, cols] = value.astype(BF16)

        product(chunk, (1 - k) * half, to_half)
        send(r.half_send.at[chunk], r.half_recv.at[chunk], r.half_sem.at[chunk], s.twin)

        def to_own(cols, value):
            r.own[chunk, :, cols] = value

        product(chunk, k * half, to_own)

    def second(chunk):
        s.arrived(r.half_recv.at[chunk], r.half_sem.at[chunk])
        for a, device in zip(s.xs, s.to_x):
            cols = at(a * third, third)
            r.x_send[chunk, :, cols] = (r.own[chunk, :, cols] + r.half_recv[chunk, :, cols].astype(F32)).astype(BF16)
            send(r.x_send.at[chunk, :, cols], r.x_recv.at[chunk, x], r.x_sem.at[chunk, x], device)

    def last(chunk):
        cols = at(x * third, third)
        value = r.own[chunk, :, cols] + r.half_recv[chunk, :, cols].astype(F32)
        for a in s.xs:
            s.arrived(r.x_recv.at[chunk, a], r.x_sem.at[chunk, a])
            value = value + r.x_recv[chunk, a].astype(F32)
        r.total[chunk] = value.astype(BF16)
        rows = at(z * fs + chunk * width, width)
        for a, device in zip(s.zs, s.to_z):
            send(r.total.at[chunk, :, at(a * NODE, NODE)], r.summed.at[rows], r.back_sem.at[chunk, z], device)
        r.summed[rows, :] = r.total[chunk, :, at(z * NODE, NODE)]

    build(z, r.codes)
    build_from(s.zs[0])
    build_from(s.zs[1])
    pass_on(0)
    build_from(s.zs[2])
    pass_on(1)
    pass_on(2)
    first(0)
    pass_on(3)
    second(0)
    first(1)
    first(2)
    second(1)
    last(0)
    first(3)
    second(2)
    second(3)
    last(1)

    for device, c in zip(mates, mate_cols):
        s.arrived(r.degrees.at[c], r.degree_sem.at[c])
    degree = r.degrees[0]
    for c in range(1, plan.cols):
        degree = degree + r.degrees[c]
    scale = 1.0 / (degree[0:1, :] + 1.0)
    scale_col = jnp.broadcast_to(scale, (NODE, NODE)).T[:, 0:1]

    def combine(chunk):
        for a in s.zs:
            s.arrived(r.summed.at[at(a * fs + chunk * width, width)], r.back_sem.at[chunk, a])
        for a in range(nz):
            rows = pl.ds(a * fs + chunk * width, width)
            value = scale * (r.summed[rows, :].astype(F32) + 2.0 * r.x_t[rows, :].astype(F32))
            r.agg[rows, :] = value.astype(BF16)
            r.agg_rows[:, (chunk * nz + a) * width : (chunk * nz + a + 1) * width] = value.T.astype(BF16)

    def part_of(chunk, cols):
        rows = pl.ds(chunk * fs, fs)
        return jnp.dot(r.agg_rows[:, rows], r.w[rows, cols], preferred_element_type=F32)

    def add_chunk(chunk):
        for i in range(chunk * nz, (chunk + 1) * nz):
            w_copies[i].wait()

        def step(i):
            cols = at(i * 512, 512)
            if chunk == 0:
                r.preact[:, cols] = part_of(chunk, cols)
            else:
                r.preact[:, cols] += part_of(chunk, cols)

        loop(plan.feat // 512, step)

    combine(0)
    last(2)
    add_chunk(0)
    combine(1)
    last(3)
    add_chunk(1)
    combine(2)
    add_chunk(2)
    combine(3)
    agg_ready()
    for i in range(3 * nz, 4 * nz):
        w_copies[i].wait()
    r.cot_copy.wait()

    def layer(cols):
        pre = r.preact[:, cols] + part_of(3, cols) + r.bias[:, cols]
        square = pre * pre
        slope = 0.7978845608028654
        t = jnp.tanh(slope * pre * (1.0 + 0.044715 * square))
        r.act[:, cols] = (0.5 * pre * (1.0 + t)).astype(BF16)
        grad = 0.5 * (1.0 + t) + 0.5 * pre * (1.0 - t * t) * (slope * (1.0 + 3.0 * 0.044715 * square))
        low = (r.cot[:, cols].astype(F32) * grad).astype(BF16)
        r.pg[:, cols] = low
        wide = low.astype(F32)
        r.scaled[:, cols] = (scale_col * wide).astype(BF16)
        r.bias_sum[:, cols] = jnp.sum(wide, axis=0, keepdims=True)

    for part in range(WIDE):
        loop(ny, lambda b: layer(at(b * plan.fp + part * plan.fw, plan.fw)))
        pg_ready(part)


class BackwardHalf:
    def __init__(self, s, w_copies):
        self.s, self.w_copies = s, w_copies
        plan = s.plan
        self.pair = s.z + 1 - 2 * lax.rem(s.z, 2)
        self.other = plan.nz - 1 - s.z
        self.middle = lax.rem(s.z, 3) > 0
        self.end = lax.rem(s.z, 3) == 0
        self.tile = min(256, plan.fh)
        self.copies = []

    def nodes(self, b, a):
        return at((b * self.s.plan.nx + a) * NODE, NODE)

    def line_rows(self, c, a):
        return at((c * self.s.plan.nx + a) * self.s.plan.group, self.s.plan.group)

    def wide_cols(self, b, part):
        return at(b * self.s.plan.fp + part * self.s.plan.fw, self.s.plan.fw)

    def agg_ready(self):
        s, r, fa = self.s, self.s.r, self.s.plan.fa
        mine = self.nodes(s.y, s.x)
        for a, device in zip(s.xs, s.to_x):
            s.send(r.agg.at[at(a * fa, fa)], r.agg_all.at[:, mine], r.agg_x_sem.at[s.x], device)
        for device in s.to_y:
            s.send(r.agg.at[at(s.x * fa, fa)], r.agg_all.at[:, mine], r.agg_y_sem.at[s.y, s.x], device)
        r.agg_all[:, mine] = r.agg[at(s.x * fa, fa), :]

    def pg_ready(self, part):
        s, r, fw = self.s, self.s.r, self.s.plan.fw
        mine, cols = self.nodes(s.y, s.x), pl.ds(part * fw, fw)
        for b, device in zip(s.ys, s.to_y):
            s.send(r.pg.at[:, self.wide_cols(b, part)], r.pg_all.at[mine, cols], r.pg_y_sem.at[part, s.y], device)
        for device in s.to_x:
            s.send(
                r.pg.at[:, self.wide_cols(s.y, part)], r.pg_all.at[mine, cols], r.pg_x_sem.at[part, s.y, s.x], device
            )
        r.pg_all[mine, cols] = r.pg[:, self.wide_cols(s.y, part)]

    def pass_agg(self):
        s, r = self.s, self.s.r
        for a in s.xs:
            ref = r.agg_all.at[:, self.nodes(s.y, a)]
            s.arrived(ref, r.agg_x_sem.at[a])
            for device in s.to_y:
                s.send(ref, ref, r.agg_y_sem.at[s.y, a], device)

    def pass_pg(self, part):
        s, r, fw = self.s, self.s.r, self.s.plan.fw
        for b in s.ys:
            ref = r.pg_all.at[self.nodes(b, s.x), pl.ds(part * fw, fw)]
            s.arrived(ref, r.pg_y_sem.at[part, b])
            for device in s.to_x:
                s.send(ref, ref, r.pg_x_sem.at[part, b, s.x], device)

    def await_agg(self):
        s, r = self.s, self.s.r
        for b in s.ys:
            for a in range(s.plan.nx):
                s.arrived(r.agg_all.at[:, self.nodes(b, a)], r.agg_y_sem.at[b, a])

    def tile_part(self, part):
        s, r, plan = self.s, self.s.r, self.s.plan
        fw, fh, tile = plan.fw, plan.fh, self.tile
        cols = pl.ds(part * fw, fw)
        for a in s.xs:
            for b in range(plan.ny):
                s.arrived(r.pg_all.at[self.nodes(b, a), cols], r.pg_x_sem.at[part, b, a])

        def product(rows_from, store):
            def step(i):
                rows = r.agg_all[at(rows_from + i * tile, tile), :]
                store(at(i * tile, tile), jnp.dot(rows, r.pg_all[:, cols], preferred_element_type=F32))

            loop(fh // tile, step)

        def to_half(rows, value):
            r.tile_send[part, rows, :] = value.astype(BF16)

        product((1 - s.k) * fh, to_half)
        s.send(r.tile_send.at[part], r.tile_recv.at[part], r.tile_sem.at[part], s.twin)

        def to_own(rows, value):
            r.tile[part, rows, :] = value

        product(s.k * fh, to_own)

    def own_part(self, part, a):
        r, fz = self.s.r, self.s.plan.fz
        rows = at(a * fz, fz)
        return r.tile[part, rows, :] + r.tile_recv[part, rows, :].astype(F32)

    def sum_start(self, part):
        s, r = self.s, self.s.r
        s.arrived(r.tile_recv.at[part], r.tile_sem.at[part])
        pair, other = self.pair, self.other
        targets = [other, s.plan.nz - 1 - pair, pair]

        @pl.when(self.end)
        def _():
            for i, a in enumerate(targets):
                r.sum_send[part, i] = self.own_part(part, a).astype(BF16)

        for i in range(3):
            s.send(
                r.sum_send.at[part, i], r.sum_recv.at[part, i], r.sum_sem.at[part, i],
                s.plan.device(pair, s.y, s.x, s.k), self.end,
            )

    def sum_step(self, part, i, into, a, to):
        s, r = self.s, self.s.r

        @pl.when(self.middle)
        def _():
            s.arrived(r.sum_recv.at[part, i], r.sum_sem.at[part, i])
            r.sum_send[part, into - 3] = (self.own_part(part, a) + r.sum_recv[part, i].astype(F32)).astype(BF16)

        s.send(
            r.sum_send.at[part, into - 3], r.sum_recv.at[part, into], r.sum_sem.at[part, into],
            s.plan.device(to, s.y, s.x, s.k), self.middle,
        )

    def sum_across(self, part):
        far = self.s.plan.nz - 1 - self.pair
        self.sum_step(part, 0, 3, far, self.other)
        self.sum_step(part, 1, 4, self.other, self.other)

    def sum_out(self, part):
        self.sum_step(part, 3, 5, self.pair, self.pair)

    def sum_end(self, part):
        s, r = self.s, self.s.r
        mine = self.own_part(part, s.z)

        @pl.when(self.middle)
        def _():
            s.arrived(r.sum_recv.at[part, 2], r.sum_sem.at[part, 2])
            s.arrived(r.sum_recv.at[part, 4], r.sum_sem.at[part, 4])
            r.final[part] = (mine + r.sum_recv[part, 2].astype(F32) + r.sum_recv[part, 4].astype(F32)).astype(BF16)

        @pl.when(self.end)
        def _():
            s.arrived(r.sum_recv.at[part, 5], r.sum_sem.at[part, 5])
            r.final[part] = (mine + r.sum_recv[part, 5].astype(F32)).astype(BF16)

        here = (s.z, s.y, s.x, s.k)
        self.spread(r.final.at[part], part, here, s.to_x + s.to_y + [s.twin])
        pair, other = s.plan.device(self.pair, s.y, s.x, s.k), s.plan.device(self.other, s.y, s.x, s.k)
        self.spread(r.final.at[part], part, here, [pair])
        self.spread(r.final.at[part], part, here, [other], self.middle)
        copy = pltpu.make_async_copy(r.final.at[part], self.piece(part, *here), r.local_sem.at[part])
        copy.start()
        self.copies.append(copy)

    def piece(self, part, a_z, a_y, a_x, a_k):
        plan = self.s.plan
        return self.s.r.low.at[at(a_x * plan.fa + a_k * plan.fh + a_z * plan.fz, plan.fz), self.wide_cols(a_y, part)]

    def spread(self, source, part, origin, devices, when=None):
        for device in devices:
            self.s.send(source, self.piece(part, *origin), self.s.r.gather_sem.at[(part,) + origin], device, when)

    def take(self, part, *origin):
        self.s.arrived(self.piece(part, *origin), self.s.r.gather_sem.at[(part,) + origin])

    def line_order(self):
        return [self.s.z, self.pair, 2 - self.s.z // 2, 3 - 3 * (self.s.z // 2)]

    def gather_line(self, part, i):
        s = self.s
        origin = (self.line_order()[i], s.y, s.x, s.k)
        self.take(part, *origin)
        onward = s.plan.device(self.other if i == 1 else self.pair, s.y, s.x, s.k)
        self.spread(self.piece(part, *origin), part, origin, [onward], self.middle)
        self.spread(self.piece(part, *origin), part, origin, s.to_x + s.to_y + [s.twin])

    def gather_plane(self, part, i):
        s = self.s
        a_z = self.line_order()[i]
        even = lax.rem(a_z, 2) == 0
        odd = lax.rem(a_z, 2) == 1
        for a_x in s.xs:
            origin = (a_z, s.y, a_x, s.k)
            self.take(part, *origin)
            self.spread(self.piece(part, *origin), part, origin, s.to_y, even)
            self.spread(self.piece(part, *origin), part, origin, [s.twin])
        for a_y in s.ys:
            origin = (a_z, a_y, s.x, s.k)
            self.take(part, *origin)
            self.spread(self.piece(part, *origin), part, origin, s.to_x, odd)
            self.spread(self.piece(part, *origin), part, origin, [s.twin])

    def gather_corner(self, part, i):
        s = self.s
        for a_x in s.xs:
            for a_y in s.ys:
                origin = (self.line_order()[i], a_y, a_x, s.k)
                self.take(part, *origin)
                self.spread(self.piece(part, *origin), part, origin, [s.twin])

    def gather_twin(self, part):
        s, plan = self.s, self.s.plan
        for a_z in range(plan.nz):
            for a_y in range(plan.ny):
                for a_x in range(plan.nx):
                    self.take(part, a_z, a_y, a_x, 1 - s.k)

    def grads_start(self):
        s, r, plan = self.s, self.s.r, self.s.plan
        fs, wb = plan.slice, plan.wb
        mine = at(((s.k * plan.nx + s.x) * plan.nz + s.z) * NODE, NODE)
        for part in range(BACK):
            for a, device in zip(s.zs, s.to_z):
                s.send(
                    r.scaled.at[:, at(a * fs + part * wb, wb)], r.grads.at[mine, pl.ds(part * wb, wb)],
                    r.grads_z_sem.at[part, s.z], device,
                )
        r.grads[mine, :] = r.scaled[:, at(s.z * fs, fs)]

    def grads_x(self, part):
        s, r, plan = self.s, self.s.r, self.s.plan
        cols = pl.ds(part * plan.wb, plan.wb)
        for a in s.zs:
            s.arrived(
                r.grads.at[at(((s.k * plan.nx + s.x) * plan.nz + a) * NODE, NODE), cols], r.grads_z_sem.at[part, a]
            )
        ref = r.grads.at[self.line_rows(s.k, s.x), cols]
        for device in s.to_x:
            s.send(ref, ref, r.grads_x_sem.at[part, s.x], device)
        s.send(ref, ref, r.grads_k_sem.at[part, s.x], s.twin)

    def grads_twin(self, part):
        s, r, plan = self.s, self.s.r, self.s.plan
        for a in s.xs:
            ref = r.grads.at[self.line_rows(s.k, a), pl.ds(part * plan.wb, plan.wb)]
            s.arrived(ref, r.grads_x_sem.at[part, a])
            s.send(ref, ref, r.grads_k_sem.at[part, a], s.twin)

    def target(self, part):
        s, r, plan = self.s, self.s.r, self.s.plan
        cols = pl.ds(part * plan.wb, plan.wb)
        for a in range(plan.nx):
            s.arrived(r.grads.at[self.line_rows(1 - s.k, a), cols], r.grads_k_sem.at[part, a])

        def product(b, store):
            def step(i):
                rows = r.adj[at(b * plan.group + i * 256, 256), :]
                store(at(i * 256, 256), jnp.dot(rows, r.grads[:, cols], preferred_element_type=F32))

            loop(plan.group // 256, step)

        for i, (b, device) in enumerate(zip(s.ys, s.to_y)):

            def to_y(rows, value):
                r.y_send[part, i, rows, :] = value.astype(BF16)

            product(b, to_y)
            there = plan.ny - 2 - i
            s.send(r.y_send.at[part, i], r.y_recv.at[part, there], r.y_sem.at[part, there], device)

        def to_target(rows, value):
            r.target[part, rows, :] = value

        product(s.y, to_target)

    def back(self, part):
        s, r, plan = self.s, self.s.r, self.s.plan
        value = r.target[part]
        for i in range(plan.ny - 1):
            s.arrived(r.y_recv.at[part, i], r.y_sem.at[part, i])
            value = value + r.y_recv[part, i].astype(F32)
        r.back[part] = value.astype(BF16)
        cols = at(s.z * plan.slice + part * plan.wb, plan.wb)
        for a, device in zip(s.zs, s.to_z):
            s.send(r.back.at[part, at(a * NODE, NODE)], r.returned.at[:, cols], r.returned_sem.at[part, s.z], device)
        r.returned[:, cols] = r.back[part, at(s.z * NODE, NODE), :]

    def through(self):
        s, r, plan = self.s, self.s.r, self.s.plan
        for part in range(BACK):
            for a in s.zs:
                cols = at(a * plan.slice + part * plan.wb, plan.wb)
                s.arrived(r.returned.at[:, cols], r.returned_sem.at[part, a])
        r.returned[...] = (r.returned[...].astype(F32) + 2.0 * r.scaled[...].astype(F32)).astype(BF16)
        for chunk in range(CHUNKS):
            rows = pl.ds(chunk * plan.slice, plan.slice)
            value = lax.dot_general(
                r.returned[...], r.w[rows, :], (((1,), (1,)), ((), ())), preferred_element_type=F32
            )
            for a in range(plan.nz):
                cols = pl.ds(a * plan.slice + chunk * plan.width, plan.width)
                r.fg[:, cols] = value[:, a * plan.width : (a + 1) * plan.width]

    def bias_start(self):
        s, r = self.s, self.s.r
        s.send(r.bias_sum, r.bias_k.at[s.k], r.bias_k_sem.at[s.k], s.twin)
        r.bias_k[s.k] = r.bias_sum[...]

    def bias_stage(self, stage):
        s, r, plan = self.s, self.s.r, self.s.plan
        ref, sem, peers, count = (
            (r.bias_k, r.bias_k_sem, [1 - s.k], CORES),
            (r.bias_x, r.bias_x_sem, s.xs, plan.nx),
            (r.bias_y, r.bias_y_sem, s.ys, plan.ny),
            (r.bias_z, r.bias_z_sem, s.zs, plan.nz),
        )[stage]
        for a in peers:
            s.arrived(ref.at[a], sem.at[a])
        value = ref[0]
        for a in range(1, count):
            value = value + ref[a]
        if stage == 3:
            r.bias_grad[...] = value
            return
        ref, sem, index, devices = (
            (r.bias_x, r.bias_x_sem, s.x, s.to_x),
            (r.bias_y, r.bias_y_sem, s.y, s.to_y),
            (r.bias_z, r.bias_z_sem, s.z, s.to_z),
        )[stage]
        ref[index] = value
        for device in devices:
            s.send(ref.at[index], ref.at[index], sem.at[index], device)

    def run(self):
        self.bias_start()
        self.pass_agg()
        self.pass_pg(0)
        self.grads_start()
        self.bias_stage(0)
        self.pass_pg(1)
        self.await_agg()
        self.tile_part(0)
        self.grads_x(0)
        self.sum_start(0)
        self.tile_part(1)
        self.grads_x(1)
        self.sum_start(1)
        self.sum_across(0)
        self.grads_twin(0)
        self.bias_stage(1)
        self.target(0)
        self.sum_out(0)
        self.sum_end(0)
        self.sum_across(1)
        self.grads_twin(1)
        self.target(1)
        self.gather_line(0, 1)
        self.sum_out(1)
        self.sum_end(1)
        self.back(0)
        self.bias_stage(2)
        self.gather_plane(0, 0)
        self.gather_line(0, 2)
        self.gather_plane(0, 1)
        self.gather_line(0, 3)
        self.back(1)
        self.gather_plane(0, 2)
        self.gather_line(1, 1)
        self.gather_plane(0, 3)
        self.gather_plane(1, 0)
        self.gather_line(1, 2)
        self.gather_plane(1, 1)
        self.gather_line(1, 3)
        self.gather_plane(1, 2)
        self.gather_plane(1, 3)
        self.bias_stage(3)
        self.through()
        for part in range(WIDE):
            for i in range(self.s.plan.nz):
                self.gather_corner(part, i)
        for part in range(WIDE):
            self.gather_twin(part)
        for copy in self.copies:
            copy.wait()


def prepare(s):
    plan, r = s.plan, s.r
    for start in range(0, plan.feat, NODE):
        r.x_t[start : start + NODE, :] = r.x[:, start : start + NODE].T
    for c in range(plan.cols):
        part = r.codes[:, c * NODE : (c + 1) * NODE]
        ones = jnp.sum(jnp.where(part >= 0, 1.0, 0.0), axis=0, keepdims=True)
        r.count[c] = jnp.broadcast_to(ones, (8, NODE))


def whole_kernel(plan, names, *refs):
    s = Step(plan, Refs(names, refs))
    w_copies = s.weight_copies()
    s.r.cot_copy = pltpu.make_async_copy(s.r.cot_hbm, s.r.cot, s.r.cot_sem)
    for copy in w_copies + [s.r.cot_copy]:
        copy.start()
    prepare(s)
    greet(s.to_z + s.to_y + s.to_x + [s.twin] + s.to_far)
    backward = BackwardHalf(s, [])
    forward_half(s, w_copies, backward.agg_ready, backward.pg_ready)
    backward.run()
    s.send.finish()


def forward_kernel(plan, names, *refs):
    s = Step(plan, Refs(names, refs))
    w_copies = s.weight_copies()
    s.r.cot_copy = pltpu.make_async_copy(s.r.cot_hbm, s.r.cot, s.r.cot_sem)
    for copy in w_copies + [s.r.cot_copy]:
        copy.start()
    prepare(s)
    greet(s.to_z + s.to_y + s.to_x + [s.twin] + s.to_far)
    forward_half(s, w_copies, lambda: None, lambda part: None)
    s.send.finish()


def backward_kernel(plan, names, *refs):
    s = Step(plan, Refs(names, refs))
    w_copies = s.weight_copies()
    for copy in w_copies:
        copy.start()
    greet(s.to_z + s.to_y + s.to_x + [s.twin])
    backward = BackwardHalf(s, w_copies)
    backward.agg_ready()
    for part in range(WIDE):
        backward.pg_ready(part)
    for copy in w_copies:
        copy.wait()
    backward.run()
    s.send.finish()


def cast_kernel(low, act_in, fg_in, bias_in, out, act_out, fg_out, bias_out, wide, sems):
    copies = [
        pltpu.make_async_copy(src, dst, sems.at[i])
        for i, (src, dst) in enumerate(((act_in, act_out), (fg_in, fg_out), (bias_in, bias_out)))
    ]
    for copy in copies:
        copy.start()
    count, rows, _ = wide.shape
    for i in range(count):
        wide[i] = low[i * rows : (i + 1) * rows, :].astype(F32)
        copy = pltpu.make_async_copy(wide.at[i], out.at[pl.ds(i * rows, rows)], sems.at[3 + i])
        copy.start()
        copies.append(copy)
    for copy in copies:
        copy.wait()


def shaped(*items):
    return jax.ShapeDtypeStruct(*items)


def forward_scratch(plan):
    c, nz = CHUNKS, plan.nz
    v = pltpu.VMEM
    return dict(
        x_t=v((plan.feat, NODE), BF16),
        cot=v((NODE, plan.feat), BF16),
        gathered=v((plan.slice, plan.columns), BF16),
        line_codes=v((nz, plan.slots, plan.block), I32),
        count=v((plan.cols, 8, NODE), F32),
        degrees=v((plan.cols, 8, NODE), F32),
        half_send=v((c, plan.width, plan.half), BF16),
        half_recv=v((c, plan.width, plan.half), BF16),
        x_send=v((c, plan.width, plan.half), BF16),
        x_recv=v((c, plan.nx, plan.width, plan.third), BF16),
        own=v((c, plan.width, plan.half), F32),
        total=v((c, plan.width, plan.third), BF16),
        summed=v((plan.feat, NODE), BF16),
        agg_rows=v((NODE, plan.feat), BF16),
        preact=v((NODE, plan.feat), F32),
        cot_sem=DMA(()),
        codes_sem=DMA((nz,)),
        degree_sem=DMA((plan.cols,)),
        slice_sem=DMA((c, nz)),
        line_sem=DMA((c, nz, plan.ny)),
        half_sem=DMA((c,)),
        x_sem=DMA((c, plan.nx)),
        back_sem=DMA((c, nz)),
    )


def forward_sends(plan):
    dz, dy, dx = plan.nz - 1, plan.ny - 1, plan.nx - 1
    return dz + CHUNKS * (dz + dy) + plan.cols - 1 + CHUNKS * dz * dy + CHUNKS * (1 + dx + dz)


def backward_scratch(plan):
    nz, ny, nx, w = plan.nz, plan.ny, plan.nx, WIDE
    v = pltpu.VMEM
    return dict(
        agg_all=v((plan.fa, plan.depth), BF16),
        pg_all=v((plan.depth, plan.fp), BF16),
        grads=v((plan.line, plan.slice), BF16),
        tile_send=v((w, plan.fh, plan.fw), BF16),
        tile_recv=v((w, plan.fh, plan.fw), BF16),
        tile=v((w, plan.fh, plan.fw), F32),
        sum_send=v((w, 3, plan.fz, plan.fw), BF16),
        sum_recv=v((w, 6, plan.fz, plan.fw), BF16),
        final=v((w, plan.fz, plan.fw), BF16),
        y_send=v((BACK, ny - 1, plan.group, plan.wb), BF16),
        y_recv=v((BACK, ny - 1, plan.group, plan.wb), BF16),
        target=v((BACK, plan.group, plan.wb), F32),
        back=v((BACK, plan.group, plan.wb), BF16),
        returned=v((NODE, plan.feat), BF16),
        bias_k=v((CORES, 1, plan.feat), F32),
        bias_x=v((nx, 1, plan.feat), F32),
        bias_y=v((ny, 1, plan.feat), F32),
        bias_z=v((nz, 1, plan.feat), F32),
        local_sem=DMA((w,)),
        agg_x_sem=DMA((nx,)),
        agg_y_sem=DMA((ny, nx)),
        pg_y_sem=DMA((w, ny)),
        pg_x_sem=DMA((w, ny, nx)),
        grads_z_sem=DMA((BACK, nz)),
        grads_x_sem=DMA((BACK, nx)),
        grads_k_sem=DMA((BACK, nx)),
        tile_sem=DMA((w,)),
        sum_sem=DMA((w, 6)),
        gather_sem=DMA((w, nz, ny, nx, CORES)),
        y_sem=DMA((BACK, ny - 1)),
        returned_sem=DMA((BACK, nz)),
        bias_k_sem=DMA((CORES,)),
        bias_x_sem=DMA((nx,)),
        bias_y_sem=DMA((ny,)),
        bias_z_sem=DMA((nz,)),
    )


def backward_sends(plan):
    dz, dy, dx = plan.nz - 1, plan.ny - 1, plan.nx - 1
    factors = dx + dy + WIDE * (dx + dy) + dx * dy + WIDE * dx * dy
    tiles = WIDE * (1 + 3 + 3)
    gathers = WIDE * (dx + dy + 3 + 3 * (dx + dy + 2) + 4 * (2 * dx * dy + dx + dy) + 4 * dx * dy)
    grads = BACK * (dz + 2 * dx + 1 + dy + dz)
    return factors + tiles + gathers + grads + 1 + dx + dy + dz


def call(body, plan, name, identity, inputs, outputs, scratch, n_sends, vmem=127 << 19):
    scratch = dict(scratch, w=pltpu.VMEM((plan.feat, plan.feat), BF16), w_sem=DMA((CHUNKS * plan.nz,)), sems=DMA((n_sends,)))
    names = list(inputs) + list(outputs) + list(scratch)
    return pl.pallas_call(
        functools.partial(body, plan, names),
        name=name,
        out_shape=[pltpu.VMEM(shape, kind) if plan.merged else shaped(shape, kind) for shape, kind, _ in outputs.values()],
        in_specs=[pl.BlockSpec(memory_space=space) for _, space in inputs.values()],
        out_specs=[pl.BlockSpec(memory_space=space) for _, _, space in outputs.values()],
        scratch_shapes=list(scratch.values()),
        compiler_params=pltpu.CompilerParams(
            collective_id=identity, has_side_effects=True, vmem_limit_bytes=vmem
        ),
    )(*[array for array, _ in inputs.values()])


def on_device(plan, features, neighbours, edge_mask, weight, bias, cotangent):
    codes = jnp.where(edge_mask > 0, neighbours, -1).T
    feat, v, far = plan.feat, pltpu.VMEM, pl.ANY
    arguments = dict(x=(features, v), codes=(codes, v), w_hbm=(weight, far), bias=(bias.reshape(1, -1), v), cot_hbm=(cotangent, far))
    between = dict(
        pg=((NODE, feat), BF16),
        scaled=((NODE, feat), BF16),
        agg=((feat, NODE), BF16),
        adj=((plan.columns, plan.line), BF16),
        bias_sum=((1, feat), F32),
    )
    act = dict(act=((NODE, feat), BF16, v))
    results = dict(fg=((NODE, feat), F32, v), low=((feat, feat), BF16, far), bias_grad=((1, feat), F32, v))
    if plan.merged:
        scratch = dict(forward_scratch(plan), **backward_scratch(plan))
        scratch.update({name: v(*item) for name, item in between.items()})
        activations, feature_grad, low, bias_grad = call(
            whole_kernel, plan, "layer", 0, arguments, dict(act, **results), scratch,
            forward_sends(plan) + backward_sends(plan), 46 << 20,
        )
    else:
        activations, *kept = call(
            forward_kernel, plan, "forward", 0, arguments,
            dict(act, **{name: item + (v,) for name, item in between.items()}),
            forward_scratch(plan), forward_sends(plan),
        )
        feature_grad, low, bias_grad = call(
            backward_kernel, plan, "backward", 1,
            dict({name: (array, v) for name, array in zip(between, kept)}, w_hbm=(weight, far)),
            results, backward_scratch(plan), backward_sends(plan),
        )
    parts = 8
    vmem, hbm = pl.BlockSpec(memory_space=v), pl.BlockSpec(memory_space=far)
    weight_grad, activations, feature_grad, bias_grad = pl.pallas_call(
        cast_kernel,
        name="cast",
        out_shape=[shaped(low.shape, F32)] + [shaped(a.shape, a.dtype) for a in (activations, feature_grad, bias_grad)],
        in_specs=[vmem] * 4,
        out_specs=[hbm] * 4,
        scratch_shapes=[v((parts, feat // parts, feat), F32), DMA((3 + parts,))],
        compiler_params=pltpu.CompilerParams(vmem_limit_bytes=30 << 20),
    )(low, activations, feature_grad, bias_grad)
    return activations, feature_grad, weight_grad, bias_grad.reshape(-1)


def solution(mesh):
    placed = (
        P(("row", "col"), None),
        P("row", "col"),
        P("row", "col"),
        P(),
        P(),
        P(("row", "col"), None),
    )

    def run(*args):
        plan = Plan(mesh, args[0].shape[1], args[1].shape[1] // mesh.shape["col"])
        return jax.shard_map(
            functools.partial(on_device, plan),
            mesh=mesh,
            in_specs=placed,
            out_specs=(P(("row", "col"), None), P(("row", "col"), None), P(), P()),
            check_vma=False,
        )(*args)

    return run
```

```python
import functools

import jax
import jax.numpy as jnp
from jax import lax
from jax.experimental import pallas as pl
from jax.experimental.pallas import tpu as pltpu
from jax.sharding import PartitionSpec as P

MESH = pl.DeviceIdType.MESH
BF16, F32, I32 = jnp.bfloat16, jnp.float32, jnp.int32
DMA = pltpu.SemaphoreType.DMA
NODE = 128
SPLIT = 4
CORES = 2
CHUNKS = 4
WIDE = 4
BACK = 2


class Plan:
    def __init__(self, mesh, feat, slots):
        rows, cols = mesh.shape["row"], mesh.shape["col"]
        self.rows, self.cols, self.feat, self.slots = rows, cols, feat, slots
        self.nz, self.ny, self.nx = SPLIT, rows // SPLIT, cols // CORES
        self.slice = feat // self.nz
        self.width = self.slice // CHUNKS
        self.columns = rows * NODE
        self.block = cols * NODE
        self.line = self.nz * self.block
        self.half = self.line // CORES
        self.third = self.half // self.nx
        self.fa, self.fp = feat // self.nx, feat // self.ny
        self.wide = min(WIDE, self.fp // NODE)
        self.fh, self.fw = self.fa // CORES, self.fp // self.wide
        self.fz = self.fh // self.nz
        self.group = self.nz * NODE
        self.wb = self.slice // BACK
        self.depth = self.ny * self.nx * NODE
        self.merged = self.columns * self.line <= 1 << 22

    def place(self):
        row, col = lax.axis_index("row"), lax.axis_index("col")
        return row // self.ny, lax.rem(row, self.ny), col // CORES, lax.rem(col, CORES)

    def device(self, z, y, x, k):
        return (z * self.ny + y, x * CORES + k)


class Refs:
    def __init__(self, names, refs):
        self.__dict__.update(zip(names, refs, strict=True))


def guarded(when, act):
    if when is None:
        act()
    else:
        pl.when(when)(act)


class Sends:
    def __init__(self, sems):
        self.sems, self.started = sems, []

    def __call__(self, src, dst, recv, device, when=None):
        copy = pltpu.make_async_remote_copy(
            src_ref=src,
            dst_ref=dst,
            send_sem=self.sems.at[len(self.started)],
            recv_sem=recv,
            device_id=device,
            device_id_type=MESH,
        )
        guarded(when, copy.start)
        self.started.append((copy, when))

    def finish(self):
        for copy, when in self.started:
            guarded(when, copy.wait_send)


def others(index, count):
    return [lax.rem(index + step, count) for step in range(1, count)]


def at(start, size):
    return pl.ds(pl.multiple_of(start, size), size)


def loop(count, step):
    if count <= 4:
        for i in range(count):
            step(i)
    else:

        def body(i, carry):
            step(i)
            return carry

        lax.fori_loop(0, count, body, 0)


def greet(devices):
    barrier = pltpu.get_barrier_semaphore()
    for device in devices:
        pl.semaphore_signal(barrier, inc=1, device_id=device, device_id_type=MESH)
    return lambda: pl.semaphore_wait(barrier, len(devices))


class Step:
    def __init__(self, plan, refs):
        self.plan, self.r = plan, refs
        self.z, self.y, self.x, self.k = z, y, x, k = plan.place()
        self.zs, self.ys, self.xs = others(z, plan.nz), others(y, plan.ny), others(x, plan.nx)
        self.here, self.twin = plan.device(z, y, x, k), plan.device(z, y, x, 1 - k)
        self.to_z = [plan.device(a, y, x, k) for a in self.zs]
        self.to_y = [plan.device(z, b, x, k) for b in self.ys]
        self.to_x = [plan.device(z, y, a, k) for a in self.xs]
        self.to_far = [plan.device(z, y, a, 1 - k) for a in self.xs]
        self.send = Sends(refs.sems)

    def arrived(self, ref, sem):
        pltpu.make_async_remote_copy(
            src_ref=ref, dst_ref=ref, send_sem=sem, recv_sem=sem, device_id=self.here, device_id_type=MESH
        ).wait_recv()

    def weight_copies(self):
        plan, r = self.plan, self.r
        copies = []
        for chunk in range(CHUNKS):
            for a in range(plan.nz):
                i = chunk * plan.nz + a
                copies.append(
                    pltpu.make_async_copy(
                        r.w_hbm.at[pl.ds(a * plan.slice + chunk * plan.width, plan.width)],
                        r.w.at[pl.ds(i * plan.width, plan.width)],
                        r.w_sem.at[i],
                    )
                )
        return copies


def forward_half(s, w_copies, agg_ready, pass_agg, pg_ready):
    plan, r, send = s.plan, s.r, s.send
    nz, ny, nx, fs, width = plan.nz, plan.ny, plan.nx, plan.slice, plan.width
    half, third = plan.half, plan.third
    z, y, x, k = s.z, s.y, s.x, s.k

    mates = s.to_x + [s.twin] + s.to_far
    mate_cols = [a * CORES + k for a in s.xs] + [x * CORES + 1 - k] + [a * CORES + 1 - k for a in s.xs]
    col = x * CORES + k
    mine = at((y * nz + z) * NODE, NODE)

    for device in s.to_z:
        send(r.codes, r.line_codes.at[z], r.codes_sem.at[z], device)
    for chunk in range(CHUNKS):
        rows = pl.ds(chunk * width, width)
        for a, device in zip(s.zs, s.to_z):
            send(r.x_t.at[at(a * fs + chunk * width, width)], r.gathered.at[rows, mine], r.slice_sem.at[chunk, z], device)
        for device in s.to_y:
            send(r.x_t.at[at(z * fs + chunk * width, width)], r.gathered.at[rows, mine], r.line_sem.at[chunk, z, y], device)
    for device, c in zip(mates, mate_cols):
        send(r.count.at[c], r.degrees.at[col], r.degree_sem.at[col], device)
    r.gathered[:, mine] = r.x_t[at(z * fs, fs), :]
    r.degrees[col] = r.count[col]

    groups = (plan.rows + 3) // 4
    strip = 32

    def build(a, source):
        for c in range(plan.cols):
            columns = at((((c % CORES) * nx + c // CORES) * nz + a) * NODE, NODE)
            part = source[:, c * NODE : (c + 1) * NODE]
            low = jnp.where(part >= 0, part % NODE, -1)
            high = jnp.where(part >= 0, part // NODE, -1)
            adds = [
                sum(jnp.where(high == 4 * g + i, 1 << (8 * i), 0) for i in range(4) if 4 * g + i < plan.rows)
                for g in range(groups)
            ]
            for start in range(0, NODE, strip):
                lanes = lax.broadcasted_iota(I32, (strip, NODE), 0) + start
                packed = [jnp.zeros((strip, NODE), I32) for _ in range(groups)]
                for slot in range(plan.slots):
                    hit = low[slot : slot + 1, :] == lanes
                    packed = [p + jnp.where(hit, v[slot : slot + 1, :], 0) for p, v in zip(packed, adds)]
                for row in range(plan.rows):
                    start_row = ((row % ny) * nz + row // ny) * NODE + start
                    number = (packed[row // 4] >> (8 * (row % 4))) & 255
                    r.adj[start_row : start_row + strip, columns] = number.astype(F32).astype(BF16)

    def build_from(a):
        s.arrived(r.line_codes.at[a], r.codes_sem.at[a])
        build(a, r.line_codes.at[a])

    def block_of(a, b):
        return at((b * nz + a) * NODE, NODE)

    def pass_on(chunk):
        rows = pl.ds(chunk * width, width)
        for a in s.zs:
            piece = r.gathered.at[rows, block_of(a, y)]
            s.arrived(piece, r.slice_sem.at[chunk, a])
            for device in s.to_y:
                send(piece, piece, r.line_sem.at[chunk, a, y], device)

    tile = 256

    def product(chunk, columns_from, store):
        rows = pl.ds(chunk * width, width)

        def step(i):
            columns = r.adj[:, at(columns_from + i * tile, tile)]
            store(at(i * tile, tile), jnp.dot(r.gathered[rows, :], columns, preferred_element_type=F32))

        loop(half // tile, step)

    def first(chunk):
        rows = pl.ds(chunk * width, width)
        for a in range(nz):
            for b in s.ys:
                s.arrived(r.gathered.at[rows, block_of(a, b)], r.line_sem.at[chunk, a, b])

        def to_half(cols, value):
            r.half_send[chunk, :, cols] = value.astype(BF16)

        product(chunk, (1 - k) * half, to_half)
        send(r.half_send.at[chunk], r.half_recv.at[chunk], r.half_sem.at[chunk], s.twin)

        def to_own(cols, value):
            r.own[chunk, :, cols] = value

        product(chunk, k * half, to_own)

    def second(chunk):
        s.arrived(r.half_recv.at[chunk], r.half_sem.at[chunk])
        for a, device in zip(s.xs, s.to_x):
            cols = at(a * third, third)
            r.x_send[chunk, :, cols] = (r.own[chunk, :, cols] + r.half_recv[chunk, :, cols].astype(F32)).astype(BF16)
            send(r.x_send.at[chunk, :, cols], r.x_recv.at[chunk, x], r.third_sem.at[chunk, x], device)

    def last(chunk):
        cols = at(x * third, third)
        value = r.own[chunk, :, cols] + r.half_recv[chunk, :, cols].astype(F32)
        for a in s.xs:
            s.arrived(r.x_recv.at[chunk, a], r.third_sem.at[chunk, a])
            value = value + r.x_recv[chunk, a].astype(F32)
        r.total[chunk] = value.astype(BF16)
        rows = at(z * fs + chunk * width, width)
        for a, device in zip(s.zs, s.to_z):
            send(r.total.at[chunk, :, at(a * NODE, NODE)], r.summed.at[rows], r.back_sem.at[chunk, z], device)
        r.summed[rows, :] = r.total[chunk, :, at(z * NODE, NODE)]

    build(z, r.codes)
    build_from(s.zs[0])
    build_from(s.zs[1])
    pass_on(0)
    build_from(s.zs[2])
    pass_on(1)
    pass_on(2)
    first(0)
    pass_on(3)
    second(0)
    first(1)
    first(2)
    second(1)
    last(0)
    first(3)
    second(2)
    second(3)
    last(1)

    for device, c in zip(mates, mate_cols):
        s.arrived(r.degrees.at[c], r.degree_sem.at[c])
    degree = r.degrees[0]
    for c in range(1, plan.cols):
        degree = degree + r.degrees[c]
    scale = 1.0 / (degree[0:1, :] + 1.0)
    scale_col = jnp.broadcast_to(scale, (NODE, NODE)).T[:, 0:1]

    def combine(chunk):
        for a in s.zs:
            s.arrived(r.summed.at[at(a * fs + chunk * width, width)], r.back_sem.at[chunk, a])
        for a in range(nz):
            rows = pl.ds(a * fs + chunk * width, width)
            value = scale * (r.summed[rows, :].astype(F32) + 2.0 * r.x_t[rows, :].astype(F32))
            r.agg[rows, :] = value.astype(BF16)
            r.agg_rows[:, (chunk * nz + a) * width : (chunk * nz + a + 1) * width] = value.T.astype(BF16)
        agg_ready(chunk)

    def part_of(chunk, cols):
        rows = pl.ds(chunk * fs, fs)
        return jnp.dot(r.agg_rows[:, rows], r.w[rows, cols], preferred_element_type=F32)

    def add_chunk(chunk):
        for i in range(chunk * nz, (chunk + 1) * nz):
            w_copies[i].wait()

        def step(i):
            cols = at(i * 512, 512)
            if chunk == 0:
                r.preact[:, cols] = part_of(chunk, cols)
            else:
                r.preact[:, cols] += part_of(chunk, cols)

        loop(plan.feat // 512, step)

    combine(0)
    last(2)
    add_chunk(0)
    combine(1)
    last(3)
    add_chunk(1)
    pass_agg(0)
    combine(2)
    add_chunk(2)
    pass_agg(1)
    combine(3)
    pass_agg(2)
    for i in range(3 * nz, 4 * nz):
        w_copies[i].wait()
    r.cot_copy.wait()

    def layer(cols):
        pre = r.preact[:, cols] + part_of(3, cols) + r.bias[:, cols]
        square = pre * pre
        slope = 0.7978845608028654
        t = jnp.tanh(slope * pre * (1.0 + 0.044715 * square))
        r.act[:, cols] = (0.5 * pre * (1.0 + t)).astype(BF16)
        grad = 0.5 * (1.0 + t) + 0.5 * pre * (1.0 - t * t) * (slope * (1.0 + 3.0 * 0.044715 * square))
        low = (r.cot[:, cols].astype(F32) * grad).astype(BF16)
        r.pg[:, cols] = low
        wide = low.astype(F32)
        r.scaled[:, cols] = (scale_col * wide).astype(BF16)
        r.bias_sum[:, cols] = jnp.sum(wide, axis=0, keepdims=True)

    for part in range(plan.wide):
        loop(ny, lambda b: layer(at(b * plan.fp + part * plan.fw, plan.fw)))
        pg_ready(part)


class BackwardHalf:
    def __init__(self, s):
        self.s = s
        plan = s.plan
        self.pair = s.z + 1 - 2 * lax.rem(s.z, 2)
        self.other = plan.nz - 1 - s.z
        self.middle = lax.rem(s.z, 3) > 0
        self.end = lax.rem(s.z, 3) == 0
        self.tile = min(256, plan.fh)
        self.copies = []

    def nodes(self, b, a):
        return at((b * self.s.plan.nx + a) * NODE, NODE)

    def line_rows(self, c, a):
        return at((c * self.s.plan.nx + a) * self.s.plan.group, self.s.plan.group)

    def wide_cols(self, b, part):
        return at(b * self.s.plan.fp + part * self.s.plan.fw, self.s.plan.fw)

    def agg_blocks(self, chunk, part):
        plan = self.s.plan
        for i in range(plan.nz // plan.nx):
            start = i * plan.slice + chunk * plan.width
            yield at(part * plan.fa + start, plan.width), pl.ds(start, plan.width)

    def agg_ready(self, chunk):
        s, r = self.s, self.s.r
        mine = self.nodes(s.y, s.x)
        for a, device in zip(s.xs, s.to_x):
            for i, (source, rows) in enumerate(self.agg_blocks(chunk, a)):
                s.send(r.agg.at[source], r.agg_all.at[rows, mine], r.agg_x_sem.at[chunk, i, s.x], device)
        for i, (source, rows) in enumerate(self.agg_blocks(chunk, s.x)):
            for device in s.to_y:
                s.send(r.agg.at[source], r.agg_all.at[rows, mine], r.agg_y_sem.at[chunk, i, s.y, s.x], device)
            r.agg_all[rows, mine] = r.agg[source, :]

    def pg_x(self, part):
        s, r, fw = self.s, self.s.r, self.s.plan.fw
        mine, cols = self.nodes(s.y, s.x), pl.ds(part * fw, fw)
        for device in s.to_x:
            s.send(
                r.pg.at[:, self.wide_cols(s.y, part)], r.pg_all.at[mine, cols], r.pg_x_sem.at[part, s.y, s.x], device
            )
        r.pg_all[mine, cols] = r.pg[:, self.wide_cols(s.y, part)]

    def pg_y(self, part):
        s, r, fw = self.s, self.s.r, self.s.plan.fw
        mine, cols = self.nodes(s.y, s.x), pl.ds(part * fw, fw)
        for b, device in zip(s.ys, s.to_y):
            s.send(r.pg.at[:, self.wide_cols(b, part)], r.pg_all.at[mine, cols], r.pg_y_sem.at[part, s.y], device)

    def pg_ready(self, part):
        self.pg_y(part)
        self.pg_x(part)

    def pass_agg(self, chunk):
        s, r = self.s, self.s.r
        for i, (_, rows) in enumerate(self.agg_blocks(chunk, s.x)):
            for a in s.xs:
                ref = r.agg_all.at[rows, self.nodes(s.y, a)]
                s.arrived(ref, r.agg_x_sem.at[chunk, i, a])
                for device in s.to_y:
                    s.send(ref, ref, r.agg_y_sem.at[chunk, i, s.y, a], device)

    def pass_pg(self, part):
        s, r, fw = self.s, self.s.r, self.s.plan.fw
        for b in s.ys:
            ref = r.pg_all.at[self.nodes(b, s.x), pl.ds(part * fw, fw)]
            s.arrived(ref, r.pg_y_sem.at[part, b])
            for device in s.to_x:
                s.send(ref, ref, r.pg_x_sem.at[part, b, s.x], device)

    def await_agg(self):
        s, r = self.s, self.s.r
        for chunk in range(CHUNKS):
            for i, (_, rows) in enumerate(self.agg_blocks(chunk, s.x)):
                for b in s.ys:
                    for a in range(s.plan.nx):
                        s.arrived(r.agg_all.at[rows, self.nodes(b, a)], r.agg_y_sem.at[chunk, i, b, a])

    def tile_part(self, part):
        s, r, plan = self.s, self.s.r, self.s.plan
        fw, fh, tile = plan.fw, plan.fh, self.tile
        cols = pl.ds(part * fw, fw)
        for a in s.xs:
            for b in range(plan.ny):
                s.arrived(r.pg_all.at[self.nodes(b, a), cols], r.pg_x_sem.at[part, b, a])

        def product(rows_from, store):
            def step(i):
                rows = r.agg_all[at(rows_from + i * tile, tile), :]
                store(at(i * tile, tile), jnp.dot(rows, r.pg_all[:, cols], preferred_element_type=F32))

            loop(fh // tile, step)

        def to_half(rows, value):
            r.tile_send[part, rows, :] = value.astype(BF16)

        product((1 - s.k) * fh, to_half)
        s.send(r.tile_send.at[part], r.tile_recv.at[part], r.tile_sem.at[part], s.twin)

        def to_own(rows, value):
            r.tile[part, rows, :] = value

        product(s.k * fh, to_own)

    def own_part(self, part, a):
        r, fz = self.s.r, self.s.plan.fz
        rows = at(a * fz, fz)
        return r.tile[part, rows, :] + r.tile_recv[part, rows, :].astype(F32)

    def sum_start(self, part):
        s, r = self.s, self.s.r
        s.arrived(r.tile_recv.at[part], r.tile_sem.at[part])
        pair, other = self.pair, self.other
        targets = [other, s.plan.nz - 1 - pair, pair]

        @pl.when(self.end)
        def _():
            for i, a in enumerate(targets):
                r.sum_send[part, i] = self.own_part(part, a).astype(BF16)

        for i in range(3):
            s.send(
                r.sum_send.at[part, i], r.sum_recv.at[part, i], r.sum_sem.at[part, i],
                s.plan.device(pair, s.y, s.x, s.k), self.end,
            )

    def sum_step(self, part, i, into, a, to):
        s, r = self.s, self.s.r

        @pl.when(self.middle)
        def _():
            s.arrived(r.sum_recv.at[part, i], r.sum_sem.at[part, i])
            r.sum_send[part, into - 3] = (self.own_part(part, a) + r.sum_recv[part, i].astype(F32)).astype(BF16)

        s.send(
            r.sum_send.at[part, into - 3], r.sum_recv.at[part, into], r.sum_sem.at[part, into],
            s.plan.device(to, s.y, s.x, s.k), self.middle,
        )

    def sum_across(self, part):
        far = self.s.plan.nz - 1 - self.pair
        self.sum_step(part, 0, 3, far, self.other)
        self.sum_step(part, 1, 4, self.other, self.other)

    def sum_out(self, part):
        self.sum_step(part, 3, 5, self.pair, self.pair)

    def sum_end(self, part):
        s, r = self.s, self.s.r
        mine = self.own_part(part, s.z)

        @pl.when(self.middle)
        def _():
            s.arrived(r.sum_recv.at[part, 2], r.sum_sem.at[part, 2])
            s.arrived(r.sum_recv.at[part, 4], r.sum_sem.at[part, 4])
            r.final[part] = (mine + r.sum_recv[part, 2].astype(F32) + r.sum_recv[part, 4].astype(F32)).astype(BF16)

        @pl.when(self.end)
        def _():
            s.arrived(r.sum_recv.at[part, 5], r.sum_sem.at[part, 5])
            r.final[part] = (mine + r.sum_recv[part, 5].astype(F32)).astype(BF16)

        here = (s.z, s.y, s.x, s.k)
        self.spread(r.final.at[part], part, here, s.to_x + s.to_y + [s.twin])
        pair, other = s.plan.device(self.pair, s.y, s.x, s.k), s.plan.device(self.other, s.y, s.x, s.k)
        self.spread(r.final.at[part], part, here, [pair])
        self.spread(r.final.at[part], part, here, [other], self.middle)
        copy = pltpu.make_async_copy(r.final.at[part], self.piece(part, *here), r.local_sem.at[part])
        copy.start()
        self.copies.append(copy)

    def piece(self, part, a_z, a_y, a_x, a_k):
        plan = self.s.plan
        return self.s.r.low.at[at(a_x * plan.fa + a_k * plan.fh + a_z * plan.fz, plan.fz), self.wide_cols(a_y, part)]

    def spread(self, source, part, origin, devices, when=None):
        for device in devices:
            self.s.send(source, self.piece(part, *origin), self.s.r.gather_sem.at[(part,) + origin], device, when)

    def take(self, part, *origin):
        self.s.arrived(self.piece(part, *origin), self.s.r.gather_sem.at[(part,) + origin])

    def line_order(self):
        return [self.s.z, self.pair, 2 - self.s.z // 2, 3 - 3 * (self.s.z // 2)]

    def gather_line(self, part, i):
        s = self.s
        origin = (self.line_order()[i], s.y, s.x, s.k)
        self.take(part, *origin)
        onward = s.plan.device(self.other if i == 1 else self.pair, s.y, s.x, s.k)
        self.spread(self.piece(part, *origin), part, origin, [onward], self.middle)
        self.spread(self.piece(part, *origin), part, origin, s.to_x + s.to_y + [s.twin])

    def gather_plane(self, part, i):
        s = self.s
        a_z = self.line_order()[i]
        even = lax.rem(a_z, 2) == 0
        odd = lax.rem(a_z, 2) == 1
        for a_x in s.xs:
            origin = (a_z, s.y, a_x, s.k)
            self.take(part, *origin)
            self.spread(self.piece(part, *origin), part, origin, s.to_y, even)
            self.spread(self.piece(part, *origin), part, origin, [s.twin])
        for a_y in s.ys:
            origin = (a_z, a_y, s.x, s.k)
            self.take(part, *origin)
            self.spread(self.piece(part, *origin), part, origin, s.to_x, odd)
            self.spread(self.piece(part, *origin), part, origin, [s.twin])

    def gather_corner(self, part, i):
        s = self.s
        for a_x in s.xs:
            for a_y in s.ys:
                origin = (self.line_order()[i], a_y, a_x, s.k)
                self.take(part, *origin)
                self.spread(self.piece(part, *origin), part, origin, [s.twin])

    def gather_twin(self, part):
        s, plan = self.s, self.s.plan
        for a_z in range(plan.nz):
            for a_y in range(plan.ny):
                for a_x in range(plan.nx):
                    self.take(part, a_z, a_y, a_x, 1 - s.k)

    def grads_start(self):
        s, r, plan = self.s, self.s.r, self.s.plan
        fs, wb = plan.slice, plan.wb
        mine = at(((s.k * plan.nx + s.x) * plan.nz + s.z) * NODE, NODE)
        for part in range(BACK):
            for a, device in zip(s.zs, s.to_z):
                s.send(
                    r.scaled.at[:, at(a * fs + part * wb, wb)], r.grads.at[mine, pl.ds(part * wb, wb)],
                    r.grads_z_sem.at[part, s.z], device,
                )
        r.grads[mine, :] = r.scaled[:, at(s.z * fs, fs)]

    def grads_x(self, part):
        s, r, plan = self.s, self.s.r, self.s.plan
        cols = pl.ds(part * plan.wb, plan.wb)
        for a in s.zs:
            s.arrived(
                r.grads.at[at(((s.k * plan.nx + s.x) * plan.nz + a) * NODE, NODE), cols], r.grads_z_sem.at[part, a]
            )
        ref = r.grads.at[self.line_rows(s.k, s.x), cols]
        for device in s.to_x:
            s.send(ref, ref, r.grads_x_sem.at[part, s.x], device)
        s.send(ref, ref, r.grads_k_sem.at[part, s.x], s.twin)

    def grads_twin(self, part):
        s, r, plan = self.s, self.s.r, self.s.plan
        for a in s.xs:
            ref = r.grads.at[self.line_rows(s.k, a), pl.ds(part * plan.wb, plan.wb)]
            s.arrived(ref, r.grads_x_sem.at[part, a])
            s.send(ref, ref, r.grads_k_sem.at[part, a], s.twin)

    def target(self, part):
        s, r, plan = self.s, self.s.r, self.s.plan
        cols = pl.ds(part * plan.wb, plan.wb)
        for a in range(plan.nx):
            s.arrived(r.grads.at[self.line_rows(1 - s.k, a), cols], r.grads_k_sem.at[part, a])

        def product(b, store):
            def step(i):
                rows = r.adj[at(b * plan.group + i * 256, 256), :]
                store(at(i * 256, 256), jnp.dot(rows, r.grads[:, cols], preferred_element_type=F32))

            loop(plan.group // 256, step)

        for i, (b, device) in enumerate(zip(s.ys, s.to_y)):

            def to_y(rows, value):
                r.y_send[part, i, rows, :] = value.astype(BF16)

            product(b, to_y)
            there = plan.ny - 2 - i
            s.send(r.y_send.at[part, i], r.y_recv.at[part, there], r.y_sem.at[part, there], device)

        def to_target(rows, value):
            r.target[part, rows, :] = value

        product(s.y, to_target)

    def back(self, part):
        s, r, plan = self.s, self.s.r, self.s.plan
        value = r.target[part]
        for i in range(plan.ny - 1):
            s.arrived(r.y_recv.at[part, i], r.y_sem.at[part, i])
            value = value + r.y_recv[part, i].astype(F32)
        r.back[part] = value.astype(BF16)
        cols = at(s.z * plan.slice + part * plan.wb, plan.wb)
        for a, device in zip(s.zs, s.to_z):
            s.send(r.back.at[part, at(a * NODE, NODE)], r.returned.at[:, cols], r.returned_sem.at[part, s.z], device)
        r.returned[:, cols] = r.back[part, at(s.z * NODE, NODE), :]

    def through(self):
        s, r, plan = self.s, self.s.r, self.s.plan
        for part in range(BACK):
            for a in s.zs:
                cols = at(a * plan.slice + part * plan.wb, plan.wb)
                s.arrived(r.returned.at[:, cols], r.returned_sem.at[part, a])
        r.returned[...] = (r.returned[...].astype(F32) + 2.0 * r.scaled[...].astype(F32)).astype(BF16)
        for chunk in range(CHUNKS):
            rows = pl.ds(chunk * plan.slice, plan.slice)
            value = lax.dot_general(
                r.returned[...], r.w[rows, :], (((1,), (1,)), ((), ())), preferred_element_type=F32
            )
            for a in range(plan.nz):
                cols = pl.ds(a * plan.slice + chunk * plan.width, plan.width)
                r.fg[:, cols] = value[:, a * plan.width : (a + 1) * plan.width]

    def bias_start(self):
        s, r = self.s, self.s.r
        s.send(r.bias_sum, r.bias_k.at[s.k], r.bias_k_sem.at[s.k], s.twin)
        r.bias_k[s.k] = r.bias_sum[...]

    def bias_stage(self, stage):
        s, r, plan = self.s, self.s.r, self.s.plan
        ref, sem, peers, count = (
            (r.bias_k, r.bias_k_sem, [1 - s.k], CORES),
            (r.bias_x, r.bias_x_sem, s.xs, plan.nx),
            (r.bias_y, r.bias_y_sem, s.ys, plan.ny),
            (r.bias_z, r.bias_z_sem, s.zs, plan.nz),
        )[stage]
        for a in peers:
            s.arrived(ref.at[a], sem.at[a])
        value = ref[0]
        for a in range(1, count):
            value = value + ref[a]
        if stage == 3:
            r.bias_grad[...] = value
            return
        ref, sem, index, devices = (
            (r.bias_x, r.bias_x_sem, s.x, s.to_x),
            (r.bias_y, r.bias_y_sem, s.y, s.to_y),
            (r.bias_z, r.bias_z_sem, s.z, s.to_z),
        )[stage]
        ref[index] = value
        for device in devices:
            s.send(ref.at[index], ref.at[index], sem.at[index], device)

    def run(self):
        wide, nz = self.s.plan.wide, self.s.plan.nz
        self.bias_start()
        self.grads_start()
        self.pass_agg(3)
        for part in range(wide):
            self.pass_pg(part)
        self.await_agg()
        stages = [
            lambda p: (self.tile_part(p), self.sum_start(p)),
            self.sum_across,
            self.sum_out,
            self.sum_end,
            lambda p: (self.gather_line(p, 1), self.gather_plane(p, 0)),
            lambda p: (self.gather_line(p, 2), self.gather_plane(p, 1)),
            lambda p: (self.gather_line(p, 3), self.gather_plane(p, 2)),
            lambda p: self.gather_plane(p, 3),
            lambda p: [self.gather_corner(p, i) for i in range(nz)],
        ]
        between = {0: (lambda: self.bias_stage(0), lambda: self.grads_x(0),), 1: (lambda: self.grads_x(1), lambda: self.bias_stage(1),), 2: (lambda: self.grads_twin(0), lambda: self.target(0),), 3: (lambda: self.grads_twin(1), lambda: self.target(1),), 5: (lambda: self.bias_stage(2),), 6: (lambda: self.back(0),), 7: (lambda: self.back(1),), 10: (lambda: self.bias_stage(3),), 11: (lambda: self.through(),)}
        for tick in range(max(len(stages) + wide - 1, 1 + max(between))):
            for part in reversed(range(wide)):
                if 0 <= tick - part < len(stages):
                    stages[tick - part](part)
            for act in between.get(tick, ()):
                act()
        for part in range(wide):
            self.gather_twin(part)
        for copy in self.copies:
            copy.wait()


def fetch(s, names):
    copies = [pltpu.make_async_copy(getattr(s.r, name + "_far"), getattr(s.r, name), getattr(s.r, name + "_sem")) for name in names]
    for copy in copies:
        copy.start()
    return copies


def prepare(s):
    plan, r = s.plan, s.r
    for c in range(plan.cols):
        cols = pl.ds(c * NODE, NODE)
        part = jnp.where(r.mask[:, cols] > 0, r.lists[:, cols], -1)
        r.codes[:, cols] = part
        ones = jnp.sum(jnp.where(part >= 0, 1.0, 0.0), axis=0, keepdims=True)
        r.count[c] = jnp.broadcast_to(ones, (8, NODE))
    for start in range(0, plan.feat, NODE):
        r.x_t[start : start + NODE, :] = r.x[:, start : start + NODE].T


def opening(s):
    met = greet(s.to_z + s.to_y + s.to_x + [s.twin] + s.to_far)
    lists, mask, x, bias, s.r.cot_copy = fetch(s, ("lists", "mask", "x", "bias", "cot"))
    w_copies = s.weight_copies()
    for copy in w_copies:
        copy.start()
    for copy in (lists, mask, x, bias):
        copy.wait()
    prepare(s)
    met()
    return w_copies


def whole_kernel(plan, names, *refs):
    s = Step(plan, Refs(names, refs))
    w_copies = opening(s)
    backward = BackwardHalf(s)
    forward_half(s, w_copies, backward.agg_ready, backward.pass_agg, backward.pg_ready)
    backward.run()
    s.send.finish()


def forward_kernel(plan, names, *refs):
    s = Step(plan, Refs(names, refs))
    w_copies = opening(s)
    skip = lambda part: None
    forward_half(s, w_copies, skip, skip, skip)
    s.send.finish()


def backward_kernel(plan, names, *refs):
    s = Step(plan, Refs(names, refs))
    w_copies = s.weight_copies()
    for copy in w_copies:
        copy.start()
    greet(s.to_z + s.to_y + s.to_x + [s.twin])()
    backward = BackwardHalf(s)
    for chunk in range(CHUNKS):
        backward.agg_ready(chunk)
    for part in range(plan.wide):
        backward.pg_ready(part)
    for copy in w_copies:
        copy.wait()
    for chunk in range(CHUNKS - 1):
        backward.pass_agg(chunk)
    backward.run()
    s.send.finish()


def cast_kernel(low, act_in, fg_in, bias_in, out, act_out, fg_out, bias_out, wide, sems):
    copies = [
        pltpu.make_async_copy(src, dst, sems.at[i])
        for i, (src, dst) in enumerate(((act_in, act_out), (fg_in, fg_out), (bias_in, bias_out)))
    ]
    for copy in copies:
        copy.start()
    count, rows, _ = wide.shape
    for i in range(count):
        wide[i] = low[i * rows : (i + 1) * rows, :].astype(F32)
        copy = pltpu.make_async_copy(wide.at[i], out.at[pl.ds(i * rows, rows)], sems.at[3 + i])
        copy.start()
        copies.append(copy)
    for copy in copies:
        copy.wait()


def shaped(*items):
    return jax.ShapeDtypeStruct(*items)


def forward_scratch(plan):
    c, nz = CHUNKS, plan.nz
    v = pltpu.VMEM
    return dict(
        x=v((NODE, plan.feat), BF16),
        x_sem=DMA(()),
        lists=v((plan.slots, plan.block), I32),
        lists_sem=DMA(()),
        mask=v((plan.slots, plan.block), I32),
        mask_sem=DMA(()),
        bias=v((1, plan.feat), F32),
        bias_sem=DMA(()),
        cot=v((NODE, plan.feat), BF16),
        codes=v((plan.slots, plan.block), I32),
        x_t=v((plan.feat, NODE), BF16),
        gathered=v((plan.slice, plan.columns), BF16),
        line_codes=v((nz, plan.slots, plan.block), I32),
        count=v((plan.cols, 8, NODE), F32),
        degrees=v((plan.cols, 8, NODE), F32),
        half_send=v((c, plan.width, plan.half), BF16),
        half_recv=v((c, plan.width, plan.half), BF16),
        x_send=v((c, plan.width, plan.half), BF16),
        x_recv=v((c, plan.nx, plan.width, plan.third), BF16),
        own=v((c, plan.width, plan.half), F32),
        total=v((c, plan.width, plan.third), BF16),
        summed=v((plan.feat, NODE), BF16),
        agg_rows=v((NODE, plan.feat), BF16),
        preact=v((NODE, plan.feat), F32),
        cot_sem=DMA(()),
        codes_sem=DMA((nz,)),
        degree_sem=DMA((plan.cols,)),
        slice_sem=DMA((c, nz)),
        line_sem=DMA((c, nz, plan.ny)),
        half_sem=DMA((c,)),
        third_sem=DMA((c, plan.nx)),
        back_sem=DMA((c, nz)),
    )


def forward_sends(plan):
    dz, dy, dx = plan.nz - 1, plan.ny - 1, plan.nx - 1
    return dz + CHUNKS * (dz + dy) + plan.cols - 1 + CHUNKS * dz * dy + CHUNKS * (1 + dx + dz)


def backward_scratch(plan):
    nz, ny, nx, w = plan.nz, plan.ny, plan.nx, plan.wide
    v = pltpu.VMEM
    return dict(
        agg_all=v((plan.fa, plan.depth), BF16),
        pg_all=v((plan.depth, plan.fp), BF16),
        grads=v((plan.line, plan.slice), BF16),
        tile_send=v((w, plan.fh, plan.fw), BF16),
        tile_recv=v((w, plan.fh, plan.fw), BF16),
        tile=v((w, plan.fh, plan.fw), F32),
        sum_send=v((w, 3, plan.fz, plan.fw), BF16),
        sum_recv=v((w, 6, plan.fz, plan.fw), BF16),
        final=v((w, plan.fz, plan.fw), BF16),
        y_send=v((BACK, ny - 1, plan.group, plan.wb), BF16),
        y_recv=v((BACK, ny - 1, plan.group, plan.wb), BF16),
        target=v((BACK, plan.group, plan.wb), F32),
        back=v((BACK, plan.group, plan.wb), BF16),
        returned=v((NODE, plan.feat), BF16),
        bias_k=v((CORES, 1, plan.feat), F32),
        bias_x=v((nx, 1, plan.feat), F32),
        bias_y=v((ny, 1, plan.feat), F32),
        bias_z=v((nz, 1, plan.feat), F32),
        local_sem=DMA((w,)),
        agg_x_sem=DMA((CHUNKS, nz // nx, nx)),
        agg_y_sem=DMA((CHUNKS, nz // nx, ny, nx)),
        pg_y_sem=DMA((w, ny)),
        pg_x_sem=DMA((w, ny, nx)),
        grads_z_sem=DMA((BACK, nz)),
        grads_x_sem=DMA((BACK, nx)),
        grads_k_sem=DMA((BACK, nx)),
        tile_sem=DMA((w,)),
        sum_sem=DMA((w, 6)),
        gather_sem=DMA((w, nz, ny, nx, CORES)),
        y_sem=DMA((BACK, ny - 1)),
        returned_sem=DMA((BACK, nz)),
        bias_k_sem=DMA((CORES,)),
        bias_x_sem=DMA((nx,)),
        bias_y_sem=DMA((ny,)),
        bias_z_sem=DMA((nz,)),
    )


def backward_sends(plan):
    dz, dy, dx, wide = plan.nz - 1, plan.ny - 1, plan.nx - 1, plan.wide
    factors = (CHUNKS * plan.nz // plan.nx + wide) * (dx + dy + dx * dy)
    tiles = wide * (1 + 3 + 3)
    gathers = wide * (dx + dy + 3 + 3 * (dx + dy + 2) + 4 * (2 * dx * dy + dx + dy) + 4 * dx * dy)
    grads = BACK * (dz + 2 * dx + 1 + dy + dz)
    return factors + tiles + gathers + grads + 1 + dx + dy + dz


def call(body, plan, name, identity, inputs, outputs, scratch, n_sends, vmem=127 << 19):
    scratch = dict(scratch, w=pltpu.VMEM((plan.feat, plan.feat), BF16), w_sem=DMA((CHUNKS * plan.nz,)), sems=DMA((n_sends,)))
    names = list(inputs) + list(outputs) + list(scratch)
    return pl.pallas_call(
        functools.partial(body, plan, names),
        name=name,
        out_shape=[pltpu.VMEM(shape, kind) if plan.merged else shaped(shape, kind) for shape, kind, _ in outputs.values()],
        in_specs=[pl.BlockSpec(memory_space=space) for _, space in inputs.values()],
        out_specs=[pl.BlockSpec(memory_space=space) for _, _, space in outputs.values()],
        scratch_shapes=list(scratch.values()),
        compiler_params=pltpu.CompilerParams(
            collective_id=identity, has_side_effects=True, vmem_limit_bytes=vmem
        ),
    )(*[array for array, _ in inputs.values()])


def on_device(plan, features, neighbours, edge_mask, weight, bias, cotangent):
    feat, v, far = plan.feat, pltpu.VMEM, pl.ANY
    arguments = dict(
        x_far=(features, far),
        lists_far=(neighbours.T, far),
        mask_far=(edge_mask.T, far),
        w_hbm=(weight, far),
        bias_far=(bias.reshape(1, -1), far),
        cot_far=(cotangent, far),
    )
    between = dict(
        pg=((NODE, feat), BF16),
        scaled=((NODE, feat), BF16),
        agg=((feat, NODE), BF16),
        adj=((plan.columns, plan.line), BF16),
        bias_sum=((1, feat), F32),
    )
    act = dict(act=((NODE, feat), BF16, v))
    results = dict(fg=((NODE, feat), F32, v), low=((feat, feat), BF16, far), bias_grad=((1, feat), F32, v))
    if plan.merged:
        scratch = dict(forward_scratch(plan), **backward_scratch(plan))
        scratch.update({name: v(*item) for name, item in between.items()})
        activations, feature_grad, low, bias_grad = call(
            whole_kernel, plan, "layer", 0, arguments, dict(act, **results), scratch,
            forward_sends(plan) + backward_sends(plan), 46 << 20,
        )
    else:
        activations, *kept = call(
            forward_kernel, plan, "forward", 0, arguments,
            dict(act, **{name: item + (v,) for name, item in between.items()}),
            forward_scratch(plan), forward_sends(plan),
        )
        feature_grad, low, bias_grad = call(
            backward_kernel, plan, "backward", 1,
            dict({name: (array, v) for name, array in zip(between, kept)}, w_hbm=(weight, far)),
            results, backward_scratch(plan), backward_sends(plan),
        )
    parts = 8
    vmem, hbm = pl.BlockSpec(memory_space=v), pl.BlockSpec(memory_space=far)
    weight_grad, activations, feature_grad, bias_grad = pl.pallas_call(
        cast_kernel,
        name="cast",
        out_shape=[shaped(low.shape, F32)] + [shaped(a.shape, a.dtype) for a in (activations, feature_grad, bias_grad)],
        in_specs=[vmem] * 4,
        out_specs=[hbm] * 4,
        scratch_shapes=[v((parts, feat // parts, feat), F32), DMA((3 + parts,))],
        compiler_params=pltpu.CompilerParams(vmem_limit_bytes=30 << 20),
    )(low, activations, feature_grad, bias_grad)
    return activations, feature_grad, weight_grad, bias_grad.reshape(-1)


def solution(mesh):
    placed = (
        P(("row", "col"), None),
        P("row", "col"),
        P("row", "col"),
        P(),
        P(),
        P(("row", "col"), None),
    )

    def run(*args):
        plan = Plan(mesh, args[0].shape[1], args[1].shape[1] // mesh.shape["col"])
        return jax.shard_map(
            functools.partial(on_device, plan),
            mesh=mesh,
            in_specs=placed,
            out_specs=(P(("row", "col"), None), P(("row", "col"), None), P(), P()),
            check_vma=False,
        )(*args)

    return run
```

```python
import functools

import jax
import jax.numpy as jnp
from jax import lax
from jax.experimental import pallas as pl
from jax.experimental.pallas import tpu as pltpu
from jax.sharding import PartitionSpec as P

MESH = pl.DeviceIdType.MESH
BF16, F32, I32 = jnp.bfloat16, jnp.float32, jnp.int32
DMA = pltpu.SemaphoreType.DMA
NODE = 128
SPLIT = 4
CORES = 2
CHUNKS = 4
FINE = (4, 4, 4, 4)
WIDE = 4
BACK = 4
RING = 96


class Plan:
    def __init__(self, mesh, feat, slots):
        rows, cols = mesh.shape["row"], mesh.shape["col"]
        self.rows, self.cols, self.feat, self.slots = rows, cols, feat, slots
        self.nz, self.ny, self.nx = SPLIT, rows // SPLIT, cols // CORES
        self.slice = feat // self.nz
        self.width = self.slice // CHUNKS
        sizes = [self.slice // share for share in FINE]
        self.fine = [(sum(sizes[:i]), size) for i, size in enumerate(sizes)]
        self.columns = rows * NODE
        self.block = cols * NODE
        self.line = self.nz * self.block
        self.half = self.line // CORES
        self.third = self.half // self.nx
        self.fa, self.fp = feat // self.nx, feat // self.ny
        self.wide = min(WIDE, self.fp // NODE)
        self.fh, self.fw = self.fa // CORES, self.fp // self.wide
        self.fz = self.fh // self.nz
        self.group = self.nz * NODE
        self.wb = self.slice // BACK
        self.depth = self.ny * self.nx * NODE
        self.merged = self.columns * self.line <= 1 << 22

    def place(self):
        row, col = lax.axis_index("row"), lax.axis_index("col")
        return row // self.ny, lax.rem(row, self.ny), col // CORES, lax.rem(col, CORES)

    def device(self, z, y, x, k):
        return (z * self.ny + y, x * CORES + k)


class Refs:
    def __init__(self, names, refs):
        self.__dict__.update(zip(names, refs, strict=True))


def guarded(when, act):
    if when is None:
        act()
    else:
        pl.when(when)(act)


class Sends:
    def __init__(self, sems):
        self.sems, self.started, self.settled = sems, [], 0

    def __call__(self, src, dst, recv, device, when=None):
        self.settle(RING - 1)
        copy = pltpu.make_async_remote_copy(
            src_ref=src,
            dst_ref=dst,
            send_sem=self.sems.at[len(self.started) % RING],
            recv_sem=recv,
            device_id=device,
            device_id_type=MESH,
        )
        guarded(when, copy.start)
        self.started.append((copy, when))

    def settle(self, keep):
        while len(self.started) - self.settled > keep:
            copy, when = self.started[self.settled]
            guarded(when, copy.wait_send)
            self.settled += 1


def others(index, count):
    return [lax.rem(index + step, count) for step in range(1, count)]


def seen(i, count):
    return count - 2 - i


def at(start, size):
    return pl.ds(pl.multiple_of(start, size), size)


def span(start, size):
    return pl.ds(pl.multiple_of(start, 16), size)


def loop(count, step):
    if count <= 4:
        for i in range(count):
            step(i)
    else:

        def body(i, carry):
            step(i)
            return carry

        lax.fori_loop(0, count, body, 0)


def greet(devices):
    barrier = pltpu.get_barrier_semaphore()
    for device in devices:
        pl.semaphore_signal(barrier, inc=1, device_id=device, device_id_type=MESH)
    return lambda: pl.semaphore_wait(barrier, len(devices))


class Step:
    def __init__(self, plan, refs):
        self.plan, self.r = plan, refs
        self.z, self.y, self.x, self.k = z, y, x, k = plan.place()
        self.zs, self.ys, self.xs = others(z, plan.nz), others(y, plan.ny), others(x, plan.nx)
        self.here, self.twin = plan.device(z, y, x, k), plan.device(z, y, x, 1 - k)
        self.to_z = [plan.device(a, y, x, k) for a in self.zs]
        self.to_y = [plan.device(z, b, x, k) for b in self.ys]
        self.to_x = [plan.device(z, y, a, k) for a in self.xs]
        self.to_far = [plan.device(z, y, a, 1 - k) for a in self.xs]
        self.send = Sends(refs.sems)

    def arrived(self, ref, sem):
        pltpu.make_async_remote_copy(
            src_ref=ref, dst_ref=ref, send_sem=sem, recv_sem=sem, device_id=self.here, device_id_type=MESH
        ).wait_recv()

    def weight_copies(self):
        plan, r = self.plan, self.r
        copies = []
        for chunk in range(CHUNKS):
            for a in range(plan.nz):
                i = chunk * plan.nz + a
                copies.append(
                    pltpu.make_async_copy(
                        r.w_hbm.at[pl.ds(a * plan.slice + chunk * plan.width, plan.width)],
                        r.w.at[pl.ds(i * plan.width, plan.width)],
                        r.w_sem.at[chunk],
                    )
                )
        return copies


def of_part(task):
    def run(half, part, *where):
        if part < half.s.plan.wide:
            task(half, part, *where)

    return run


class ForwardHalf:
    def __init__(self, s):
        self.s = s
        plan, r, x, k = s.plan, s.r, s.x, s.k
        self.mates = s.to_x + [s.twin] + s.to_far
        self.mate_cols = [a * CORES + k for a in s.xs] + [x * CORES + 1 - k] + [a * CORES + 1 - k for a in s.xs]
        self.start()

    def block_of(self, a, b):
        return at((b * self.s.plan.nz + a) * NODE, NODE)

    def start(self):
        s = self.s
        plan, r, send, z, y, x, k = s.plan, s.r, s.send, s.z, s.y, s.x, s.k
        fs = plan.slice
        col, mine = x * CORES + k, self.block_of(z, y)
        for device in s.to_z:
            send(r.codes, r.line_codes.at[z], r.codes_sem.at[z], device)
        for chunk, (start, size) in enumerate(plan.fine):
            rows = pl.ds(start, size)
            for a, device in zip(s.zs, s.to_z):
                source = r.x_t.at[span(a * fs + start, size)]
                send(source, r.gathered.at[rows, mine], r.slice_sem.at[chunk, z], device)
            for i, device in enumerate(s.to_y):
                source = r.x_t.at[span(z * fs + start, size)]
                send(source, r.gathered.at[rows, mine], r.line_sem.at[chunk, seen(i, plan.ny)], device)
        for device, c in zip(self.mates, self.mate_cols):
            send(r.count.at[c], r.degrees.at[col], r.degree_sem, device)
        r.gathered[:, mine] = r.x_t[at(z * fs, fs), :]
        r.degrees[col] = r.count[col]

    def build(self, i):
        s = self.s
        plan, r, nz, ny = s.plan, s.r, s.plan.nz, s.plan.ny
        a = ([s.z] + s.zs)[i]
        source = r.codes if i == 0 else r.line_codes.at[a]
        if i > 0:
            s.arrived(source, r.codes_sem.at[a])
        groups, strip = (plan.rows + 3) // 4, 32
        for c in range(plan.cols):
            columns = at((((c % CORES) * plan.nx + c // CORES) * nz + a) * NODE, NODE)
            part = source[:, c * NODE : (c + 1) * NODE]
            low = jnp.where(part >= 0, part % NODE, -1)
            high = jnp.where(part >= 0, part // NODE, -1)
            adds = [
                sum(jnp.where(high == 4 * g + j, 1 << (8 * j), 0) for j in range(4) if 4 * g + j < plan.rows)
                for g in range(groups)
            ]
            for start in range(0, NODE, strip):
                lanes = lax.broadcasted_iota(I32, (strip, NODE), 0) + start
                packed = [jnp.zeros((strip, NODE), I32) for _ in range(groups)]
                for slot in range(plan.slots):
                    hit = low[slot : slot + 1, :] == lanes
                    packed = [p + jnp.where(hit, v[slot : slot + 1, :], 0) for p, v in zip(packed, adds)]
                for row in range(plan.rows):
                    start_row = ((row % ny) * nz + row // ny) * NODE + start
                    number = (packed[row // 4] >> (8 * (row % 4))) & 255
                    r.adj[start_row : start_row + strip, columns] = number.astype(F32).astype(BF16)

    def pass_on(self, chunk, i):
        s, r, a = self.s, self.s.r, self.s.zs[i]
        piece = r.gathered.at[pl.ds(*s.plan.fine[chunk]), self.block_of(a, s.y)]
        s.arrived(piece, r.slice_sem.at[chunk, a])
        for j, device in enumerate(s.to_y):
            s.send(piece, piece, r.line_sem.at[chunk, seen(j, s.plan.ny)], device)

    def product(self, chunk, columns_from, store):
        r, plan, tile = self.s.r, self.s.plan, 256
        rows = pl.ds(*plan.fine[chunk])

        def step(i):
            columns = r.adj[:, at(columns_from + i * tile, tile)]
            store(at(i * tile, tile), jnp.dot(r.gathered[rows, :], columns, preferred_element_type=F32))

        loop(plan.half // tile, step)

    def first(self, chunk):
        s, r, plan = self.s, self.s.r, self.s.plan
        rows = pl.ds(*plan.fine[chunk])
        for i in range(plan.ny - 1):
            s.arrived(r.gathered.at[rows, pl.ds(0, plan.group)], r.line_sem.at[chunk, i])

        def to_half(cols, value):
            r.half_send[rows, cols] = value.astype(BF16)

        self.product(chunk, (1 - s.k) * plan.half, to_half)
        s.send(r.half_send.at[rows], r.half_recv.at[rows], r.half_sem.at[chunk], s.twin)

    def own(self, chunk):
        r, rows = self.s.r, pl.ds(*self.s.plan.fine[chunk])

        def to_own(cols, value):
            r.own[rows, cols] = value

        self.product(chunk, self.s.k * self.s.plan.half, to_own)

    def second(self, chunk):
        s, r, third = self.s, self.s.r, self.s.plan.third
        rows = pl.ds(*s.plan.fine[chunk])
        s.arrived(r.half_recv.at[rows], r.half_sem.at[chunk])
        for i, (a, device) in enumerate(zip(s.xs, s.to_x)):
            cols, there = at(a * third, third), seen(i, s.plan.nx)
            r.x_send[rows, cols] = (r.own[rows, cols] + r.half_recv[rows, cols].astype(F32)).astype(BF16)
            s.send(r.x_send.at[rows, cols], r.x_recv.at[there, rows], r.third_sem.at[chunk, there], device)

    def last(self, chunk):
        s, r, plan = self.s, self.s.r, self.s.plan
        start, size = plan.fine[chunk]
        rows, cols = pl.ds(start, size), at(s.x * plan.third, plan.third)
        value = r.own[rows, cols] + r.half_recv[rows, cols].astype(F32)
        for i in range(plan.nx - 1):
            s.arrived(r.x_recv.at[i, rows], r.third_sem.at[chunk, i])
            value = value + r.x_recv[i, rows].astype(F32)
        r.total[rows] = value.astype(BF16)
        there = span(s.z * plan.slice + start, size)
        for a, device in zip(s.zs, s.to_z):
            s.send(r.total.at[rows, at(a * NODE, NODE)], r.summed.at[there], r.back_sem.at[chunk], device)
        r.summed[there, :] = r.total[rows, at(s.z * NODE, NODE)]

    def scale(self):
        s, r = self.s, self.s.r
        s.arrived(r.degrees.at[pl.ds(0, s.plan.cols - 1)], r.degree_sem)
        degree = r.degrees[0]
        for c in range(1, s.plan.cols):
            degree = degree + r.degrees[c]
        self.row = 1.0 / (degree[0:1, :] + 1.0)
        self.column = jnp.broadcast_to(self.row, (NODE, NODE)).T[:, 0:1]

    def combine(self, chunk):
        s, r, plan = self.s, self.s.r, self.s.plan
        nz, fs, width = plan.nz, plan.slice, plan.width
        start, size = plan.fine[chunk]
        s.arrived(r.summed.at[pl.ds(0, (nz - 1) * size)], r.back_sem.at[chunk])
        for a in range(nz):
            rows = pl.ds(a * fs + start, size)
            value = self.row * (r.summed[rows, :].astype(F32) + 2.0 * r.x_t[rows, :].astype(F32))
            r.agg[rows, :] = value.astype(BF16)
        end = start + size
        for begin in range(end // width * width - (width if end % width == 0 else 0), end - width + 1, width):
            for a in range(nz):
                place = begin * nz + a * width
                r.agg_rows[:, place : place + width] = r.agg[a * fs + begin : a * fs + begin + width, :].T

    def await_weight(self, chunk):
        r = self.s.r
        rows = r.w.at[pl.ds(chunk * self.s.plan.slice, self.s.plan.slice)]
        pltpu.make_async_copy(rows, rows, r.w_sem.at[chunk]).wait()

    def part_of(self, chunk, cols):
        r = self.s.r
        rows = pl.ds(chunk * self.s.plan.slice, self.s.plan.slice)
        return jnp.dot(r.agg_rows[:, rows], r.w[rows, cols], preferred_element_type=F32)

    def add(self, chunk):
        r = self.s.r
        self.await_weight(chunk)

        def step(i):
            cols = at(i * 512, 512)
            if chunk == 0:
                r.preact[:, cols] = self.part_of(chunk, cols)
            else:
                r.preact[:, cols] += self.part_of(chunk, cols)

        loop(self.s.plan.feat // 512, step)

    @of_part
    def layer(self, part):
        plan = self.s.plan
        if part == 0:
            self.await_weight(CHUNKS - 1)
            self.s.r.cot_copy.wait()
        loop(plan.ny, lambda b: self.layer_columns(at(b * plan.fp + part * plan.fw, plan.fw)))

    def layer_columns(self, cols):
        r = self.s.r
        pre = r.preact[:, cols] + self.part_of(CHUNKS - 1, cols) + r.bias[:, cols]
        square = pre * pre
        slope = 0.7978845608028654
        t = jnp.tanh(slope * pre * (1.0 + 0.044715 * square))
        r.act[:, cols] = (0.5 * pre * (1.0 + t)).astype(BF16)
        grad = 0.5 * (1.0 + t) + 0.5 * pre * (1.0 - t * t) * (slope * (1.0 + 3.0 * 0.044715 * square))
        low = (r.cot[:, cols].astype(F32) * grad).astype(BF16)
        r.pg[:, cols] = low
        wide = low.astype(F32)
        r.scaled[:, cols] = (self.column * wide).astype(BF16)
        r.bias_sum[:, cols] = jnp.sum(wide, axis=0, keepdims=True)


class BackwardHalf:
    def __init__(self, s):
        self.s = s
        plan = s.plan
        self.pair = s.z + 1 - 2 * lax.rem(s.z, 2)
        self.other = plan.nz - 1 - s.z
        self.middle = lax.rem(s.z, 3) > 0
        self.end = lax.rem(s.z, 3) == 0
        self.tile = min(256, plan.fh)
        self.copies = {}

    def nodes(self, b, a):
        return at((b * self.s.plan.nx + a) * NODE, NODE)

    def line_rows(self, c, a):
        return at((c * self.s.plan.nx + a) * self.s.plan.group, self.s.plan.group)

    def wide_cols(self, b, part):
        return at(b * self.s.plan.fp + part * self.s.plan.fw, self.s.plan.fw)

    def agg_blocks(self, chunk, part):
        plan = self.s.plan
        begin, size = plan.fine[chunk]
        for i in range(plan.nz // plan.nx):
            start = i * plan.slice + begin
            yield span(part * plan.fa + start, size), pl.ds(start, size)

    def agg_send(self, chunk):
        s, r = self.s, self.s.r
        mine = self.nodes(s.y, s.x)
        for j, (a, device) in enumerate(zip(s.xs, s.to_x)):
            for source, rows in self.agg_blocks(chunk, a):
                s.send(r.agg.at[source], r.agg_all.at[rows, mine], r.agg_x_sem.at[chunk, seen(j, s.plan.nx)], device)
        for source, rows in self.agg_blocks(chunk, s.x):
            for j, device in enumerate(s.to_y):
                s.send(r.agg.at[source], r.agg_all.at[rows, mine], r.agg_y_sem.at[seen(j, s.plan.ny)], device)
            r.agg_all[rows, mine] = r.agg[source, :]

    @of_part
    def pg_x(self, part):
        s, r, fw = self.s, self.s.r, self.s.plan.fw
        mine, cols = self.nodes(s.y, s.x), pl.ds(part * fw, fw)
        for j, device in enumerate(s.to_x):
            source = r.pg.at[:, self.wide_cols(s.y, part)]
            s.send(source, r.pg_all.at[mine, cols], r.pg_x_sem.at[part, seen(j, s.plan.nx)], device)
        r.pg_all[mine, cols] = r.pg[:, self.wide_cols(s.y, part)]

    @of_part
    def pg_y(self, part):
        s, r, fw = self.s, self.s.r, self.s.plan.fw
        mine, cols = self.nodes(s.y, s.x), pl.ds(part * fw, fw)
        for j, (b, device) in enumerate(zip(s.ys, s.to_y)):
            source = r.pg.at[:, self.wide_cols(b, part)]
            s.send(source, r.pg_all.at[mine, cols], r.pg_y_sem.at[part, seen(j, s.plan.ny)], device)

    def pass_agg(self, chunk):
        s, r, plan = self.s, self.s.r, self.s.plan
        size = plan.fine[chunk][1] * (plan.nz // plan.nx)
        for i, a in enumerate(s.xs):
            s.arrived(r.agg_all.at[pl.ds(0, size), self.nodes(s.y, a)], r.agg_x_sem.at[chunk, i])
            for _, rows in self.agg_blocks(chunk, s.x):
                ref = r.agg_all.at[rows, self.nodes(s.y, a)]
                for j, device in enumerate(s.to_y):
                    s.send(ref, ref, r.agg_y_sem.at[seen(j, plan.ny)], device)

    @of_part
    def pass_pg(self, part):
        s, r, plan = self.s, self.s.r, self.s.plan
        for i, b in enumerate(s.ys):
            ref = r.pg_all.at[self.nodes(b, s.x), pl.ds(part * plan.fw, plan.fw)]
            s.arrived(ref, r.pg_y_sem.at[part, i])
            for j, device in enumerate(s.to_x):
                s.send(ref, ref, r.pg_x_sem.at[part, seen(j, plan.nx)], device)

    def await_agg(self):
        s, r = self.s, self.s.r
        for i in range(s.plan.ny - 1):
            s.arrived(r.agg_all.at[:, pl.ds(0, s.plan.nx * NODE)], r.agg_y_sem.at[i])

    def tile_product(self, part, rows_from, store):
        r, plan, tile = self.s.r, self.s.plan, self.tile
        cols = pl.ds(part * plan.fw, plan.fw)

        def step(i):
            rows = r.agg_all[at(rows_from + i * tile, tile), :]
            store(at(i * tile, tile), jnp.dot(rows, r.pg_all[:, cols], preferred_element_type=F32))

        loop(plan.fh // tile, step)

    @of_part
    def tile_part(self, part):
        s, r, plan = self.s, self.s.r, self.s.plan
        for i in range(plan.nx - 1):
            s.arrived(r.pg_all.at[pl.ds(0, plan.ny * NODE), pl.ds(part * plan.fw, plan.fw)], r.pg_x_sem.at[part, i])

        def to_half(rows, value):
            r.tile_send[part, rows, :] = value.astype(BF16)

        self.tile_product(part, (1 - s.k) * plan.fh, to_half)
        s.send(r.tile_send.at[part], r.tile_recv.at[part], r.tile_sem.at[part], s.twin)

    @of_part
    def tile_own(self, part):
        r = self.s.r

        def to_own(rows, value):
            r.tile[part, rows, :] = value

        self.tile_product(part, self.s.k * self.s.plan.fh, to_own)

    def own_part(self, part, a):
        r, fz = self.s.r, self.s.plan.fz
        rows = at(a * fz, fz)
        return r.tile[part, rows, :] + r.tile_recv[part, rows, :].astype(F32)

    @of_part
    def sum_start(self, part):
        s, r = self.s, self.s.r
        s.arrived(r.tile_recv.at[part], r.tile_sem.at[part])
        pair, other = self.pair, self.other
        targets = [other, s.plan.nz - 1 - pair, pair]

        @pl.when(self.end)
        def _():
            for i, a in enumerate(targets):
                r.sum_send[part, i] = self.own_part(part, a).astype(BF16)

        for i in range(3):
            s.send(
                r.sum_send.at[part, i], r.sum_recv.at[part, i], r.sum_sem.at[part, i],
                s.plan.device(pair, s.y, s.x, s.k), self.end,
            )

    def sum_step(self, part, i, into, slot, a, to):
        s, r = self.s, self.s.r

        @pl.when(self.middle)
        def _():
            s.arrived(r.sum_recv.at[part, i], r.sum_sem.at[part, i])
            r.sum_send[part, slot] = (self.own_part(part, a) + r.sum_recv[part, i].astype(F32)).astype(BF16)

        s.send(
            r.sum_send.at[part, slot], r.sum_recv.at[part, into], r.sum_sem.at[part, into],
            s.plan.device(to, s.y, s.x, s.k), self.middle,
        )

    @of_part
    def sum_far(self, part):
        self.sum_step(part, 0, 3, 0, self.s.plan.nz - 1 - self.pair, self.other)

    @of_part
    def sum_other(self, part):
        self.sum_step(part, 1, 4, 1, self.other, self.other)

    @of_part
    def sum_out(self, part):
        self.sum_step(part, 3, 0, 2, self.pair, self.pair)

    @of_part
    def sum_end(self, part):
        s, r = self.s, self.s.r
        mine = self.own_part(part, s.z)

        @pl.when(self.middle)
        def _():
            s.arrived(r.sum_recv.at[part, 2], r.sum_sem.at[part, 2])
            s.arrived(r.sum_recv.at[part, 4], r.sum_sem.at[part, 4])
            r.final[part] = (mine + r.sum_recv[part, 2].astype(F32) + r.sum_recv[part, 4].astype(F32)).astype(BF16)

        @pl.when(self.end)
        def _():
            s.arrived(r.sum_recv.at[part, 0], r.sum_sem.at[part, 0])
            r.final[part] = (mine + r.sum_recv[part, 0].astype(F32)).astype(BF16)

        copy = pltpu.make_async_copy(r.final.at[part], self.piece(part, s.z, s.y, s.x), r.local_sem.at[part])
        copy.start()
        self.copies[part] = copy
        self.spread(r.final.at[part], part, s.z)
        self.along(r.final.at[part], part, s.z, self.pair, None)
        self.along(r.final.at[part], part, s.z, self.other, self.middle)

    def block(self, part, a_y, a_x):
        plan = self.s.plan
        return self.s.r.low.at[at(a_x * plan.fa + self.s.k * plan.fh, plan.fh), self.wide_cols(a_y, part)]

    def piece(self, part, a_z, a_y, a_x):
        plan = self.s.plan
        rows = at(a_x * plan.fa + self.s.k * plan.fh + a_z * plan.fz, plan.fz)
        return self.s.r.low.at[rows, self.wide_cols(a_y, part)]

    def along(self, source, part, a_z, to, when):
        s = self.s
        device = s.plan.device(to, s.y, s.x, s.k)
        s.send(source, self.piece(part, a_z, s.y, s.x), s.r.gather_z_sem.at[part, a_z], device, when)

    def spread(self, source, part, a_z):
        s, r = self.s, self.s.r
        target = self.piece(part, a_z, s.y, s.x)
        for i, device in enumerate(s.to_x):
            s.send(source, target, r.gather_x_sem.at[part, a_z, seen(i, s.plan.nx)], device)
        for i, device in enumerate(s.to_y):
            s.send(source, target, r.gather_y_sem.at[part, a_z, seen(i, s.plan.ny)], device)

    def line_order(self):
        return [self.s.z, self.pair, 2 - self.s.z // 2, 3 - 3 * (self.s.z // 2)]

    @of_part
    def gather_line(self, part, i):
        s = self.s
        a_z = self.line_order()[i]
        piece = self.piece(part, a_z, s.y, s.x)
        s.arrived(piece, s.r.gather_z_sem.at[part, a_z])
        self.along(piece, part, a_z, self.other if i == 1 else self.pair, self.middle)
        self.spread(piece, part, a_z)

    @of_part
    def gather_x(self, part, i):
        s, r, plan = self.s, self.s.r, self.s.plan
        a_z = self.line_order()[i]
        for j, a_x in enumerate(s.xs):
            piece = self.piece(part, a_z, s.y, a_x)
            s.arrived(piece, r.gather_x_sem.at[part, a_z, j])
            for m, device in enumerate(s.to_y):
                s.send(piece, piece, r.corner_sem.at[part, seen(m, plan.ny), j], device, lax.rem(a_z, 2) == 0)

    @of_part
    def gather_y(self, part, i):
        s, r, plan = self.s, self.s.r, self.s.plan
        a_z = self.line_order()[i]
        for j, a_y in enumerate(s.ys):
            piece = self.piece(part, a_z, a_y, s.x)
            s.arrived(piece, r.gather_y_sem.at[part, a_z, j])
            for m, device in enumerate(s.to_x):
                s.send(piece, piece, r.corner_sem.at[part, j, seen(m, plan.nx)], device, lax.rem(a_z, 2) == 1)

    def to_twin(self, part, a_y, a_x):
        s = self.s
        block = self.block(part, a_y, a_x)
        s.send(block, block, s.r.twin_sem, s.twin)

    @of_part
    def twin_own(self, part):
        self.copies[part].wait()
        self.to_twin(part, self.s.y, self.s.x)

    @of_part
    def twin_x(self, part):
        for a_x in self.s.xs:
            self.to_twin(part, self.s.y, a_x)

    @of_part
    def twin_y(self, part):
        for a_y in self.s.ys:
            self.to_twin(part, a_y, self.s.x)

    @of_part
    def twin_corner(self, part):
        s = self.s
        for j, a_y in enumerate(s.ys):
            for i, a_x in enumerate(s.xs):
                s.arrived(self.block(part, a_y, a_x), s.r.corner_sem.at[part, j, i])
                self.to_twin(part, a_y, a_x)

    def gather_twin(self):
        s, feat = self.s, self.s.plan.feat
        s.send.settle(16)
        s.arrived(s.r.low.at[pl.ds(0, feat // CORES)], s.r.twin_sem)

    def grads_start(self, part):
        s, r, plan = self.s, self.s.r, self.s.plan
        fs, wb = plan.slice, plan.wb
        mine, cols = at(((s.k * plan.nx + s.x) * plan.nz + s.z) * NODE, NODE), pl.ds(part * wb, wb)
        for a, device in zip(s.zs, s.to_z):
            s.send(r.scaled.at[:, at(a * fs + part * wb, wb)], r.grads.at[mine, cols], r.grads_z_sem.at[part], device)
        r.grads[mine, cols] = r.scaled[:, at(s.z * fs + part * wb, wb)]

    def grads_x(self, part):
        s, r, plan = self.s, self.s.r, self.s.plan
        cols = pl.ds(part * plan.wb, plan.wb)
        s.arrived(r.grads.at[pl.ds(0, (plan.nz - 1) * NODE), cols], r.grads_z_sem.at[part])
        ref = r.grads.at[self.line_rows(s.k, s.x), cols]
        for i, device in enumerate(s.to_x):
            s.send(ref, ref, r.grads_x_sem.at[part, seen(i, plan.nx)], device)
        s.send(ref, ref, r.grads_k_sem.at[part], s.twin)

    def grads_twin(self, part):
        s, r, plan = self.s, self.s.r, self.s.plan
        for i, a in enumerate(s.xs):
            ref = r.grads.at[self.line_rows(s.k, a), pl.ds(part * plan.wb, plan.wb)]
            s.arrived(ref, r.grads_x_sem.at[part, i])
            s.send(ref, ref, r.grads_k_sem.at[part], s.twin)

    def target_product(self, part, b, store):
        r, plan = self.s.r, self.s.plan
        cols = pl.ds(part * plan.wb, plan.wb)

        def step(i):
            rows = r.adj[at(b * plan.group + i * 256, 256), :]
            store(at(i * 256, 256), jnp.dot(rows, r.grads[:, cols], preferred_element_type=F32))

        loop(plan.group // 256, step)

    def target(self, part):
        s, r, plan = self.s, self.s.r, self.s.plan
        s.arrived(r.grads.at[pl.ds(0, plan.line // CORES), pl.ds(part * plan.wb, plan.wb)], r.grads_k_sem.at[part])
        for i, (b, device) in enumerate(zip(s.ys, s.to_y)):

            def to_y(rows, value):
                r.y_send[part, i, rows, :] = value.astype(BF16)

            self.target_product(part, b, to_y)
            there = seen(i, plan.ny)
            s.send(r.y_send.at[part, i], r.y_recv.at[part, there], r.y_sem.at[part, there], device)

    def target_own(self, part):
        r = self.s.r

        def to_target(rows, value):
            r.target[part, rows, :] = value

        self.target_product(part, self.s.y, to_target)

    def back(self, part):
        s, r, plan = self.s, self.s.r, self.s.plan
        value = r.target[part]
        for i in range(plan.ny - 1):
            s.arrived(r.y_recv.at[part, i], r.y_sem.at[part, i])
            value = value + r.y_recv[part, i].astype(F32)
        r.back[part] = value.astype(BF16)
        cols = at(s.z * plan.slice + part * plan.wb, plan.wb)
        for a, device in zip(s.zs, s.to_z):
            s.send(r.back.at[part, at(a * NODE, NODE)], r.returned.at[:, cols], r.returned_sem.at[part], device)
        r.returned[:, cols] = r.back[part, at(s.z * NODE, NODE), :]

    def through(self):
        s, r, plan = self.s, self.s.r, self.s.plan
        for part in range(BACK):
            s.arrived(r.returned.at[:, pl.ds(0, (plan.nz - 1) * plan.wb)], r.returned_sem.at[part])
        r.returned[...] = (r.returned[...].astype(F32) + 2.0 * r.scaled[...].astype(F32)).astype(BF16)
        for chunk in range(CHUNKS):
            rows = pl.ds(chunk * plan.slice, plan.slice)
            value = lax.dot_general(
                r.returned[...], r.w[rows, :], (((1,), (1,)), ((), ())), preferred_element_type=F32
            )
            for a in range(plan.nz):
                cols = pl.ds(a * plan.slice + chunk * plan.width, plan.width)
                r.fg[:, cols] = value[:, a * plan.width : (a + 1) * plan.width]

    def bias_start(self):
        s, r = self.s, self.s.r
        s.send(r.bias_sum, r.bias_k.at[s.k], r.total_sem.at[0], s.twin)
        r.bias_k[s.k] = r.bias_sum[...]

    def bias_stage(self, stage):
        s, r, plan = self.s, self.s.r, self.s.plan
        ref, count = ((r.bias_k, CORES), (r.bias_x, plan.nx), (r.bias_y, plan.ny), (r.bias_z, plan.nz))[stage]
        s.arrived(ref.at[pl.ds(0, count - 1)], r.total_sem.at[stage])
        value = ref[0]
        for a in range(1, count):
            value = value + ref[a]
        if stage == 3:
            r.bias_grad[...] = value
            return
        ref, index, devices = ((r.bias_x, s.x, s.to_x), (r.bias_y, s.y, s.to_y), (r.bias_z, s.z, s.to_z))[stage]
        ref[index] = value
        for device in devices:
            s.send(ref.at[index], ref.at[index], r.total_sem.at[stage + 1], device)


class Skip:
    def __getattr__(self, name):
        return lambda *where: None


def schedule(f, b):
    f.build(0)
    f.build(3)
    f.pass_on(0, 2)
    f.pass_on(0, 1)
    f.pass_on(0, 0)
    f.build(2)
    f.pass_on(1, 2)
    f.build(1)
    f.pass_on(1, 0)
    f.pass_on(1, 1)
    f.first(0)
    f.scale()
    f.pass_on(2, 2)
    f.own(0)
    f.pass_on(2, 0)
    f.pass_on(2, 1)
    f.second(0)
    f.first(1)
    f.pass_on(3, 0)
    f.own(1)
    f.pass_on(3, 1)
    f.second(1)
    f.pass_on(3, 2)
    f.first(2)
    f.last(0)
    f.own(2)
    f.second(2)
    f.first(3)
    f.last(1)
    f.own(3)
    f.second(3)
    f.last(2)
    f.combine(0)
    b.agg_send(0)
    f.add(0)
    f.combine(1)
    b.agg_send(1)
    f.last(3)
    f.add(1)
    b.pass_agg(0)
    f.combine(2)
    b.agg_send(2)
    f.add(2)
    f.combine(3)
    b.agg_send(3)
    f.layer(0)
    b.pg_y(0)
    b.pg_x(0)
    f.layer(1)
    b.pg_y(1)
    f.layer(2)
    b.pg_x(2)
    f.layer(3)
    b.bias_start()
    b.pass_agg(2)
    b.grads_start(0)
    b.pass_agg(3)
    b.pass_agg(1)
    b.pg_y(2)
    b.pg_x(1)
    b.grads_start(2)
    b.grads_start(3)
    b.pass_pg(0)
    b.grads_start(1)
    b.pass_pg(1)
    b.grads_x(0)
    b.await_agg()
    b.tile_part(1)
    b.tile_own(1)
    b.grads_x(2)
    b.pg_y(3)
    b.sum_start(1)
    b.grads_twin(0)
    b.pass_pg(2)
    b.tile_part(0)
    b.tile_own(0)
    b.grads_x(3)
    b.pass_pg(3)
    b.sum_start(0)
    b.target(0)
    b.sum_far(1)
    b.pg_x(3)
    b.grads_x(1)
    b.grads_twin(2)
    b.tile_part(2)
    b.sum_other(1)
    b.tile_own(2)
    b.target(2)
    b.sum_out(1)
    b.sum_start(2)
    b.grads_twin(3)
    b.sum_far(0)
    b.target(3)
    b.bias_stage(0)
    b.sum_other(0)
    b.target_own(0)
    b.sum_out(0)
    b.sum_far(2)
    b.sum_end(1)
    b.tile_part(3)
    b.tile_own(3)
    b.grads_twin(1)
    b.sum_other(2)
    b.bias_stage(1)
    b.sum_end(0)
    b.sum_start(3)
    b.sum_out(2)
    b.target(1)
    b.gather_line(1, 1)
    b.gather_line(1, 2)
    b.sum_end(2)
    b.target_own(2)
    b.gather_x(0, 0)
    b.gather_line(0, 2)
    b.sum_far(3)
    b.sum_other(3)
    b.gather_line(1, 3)
    b.gather_line(0, 1)
    b.gather_line(2, 2)
    b.sum_out(3)
    b.gather_y(1, 2)
    b.gather_line(2, 1)
    b.sum_end(3)
    b.gather_x(1, 3)
    b.gather_line(0, 3)
    b.gather_y(1, 0)
    b.gather_line(2, 3)
    b.gather_y(0, 0)
    b.back(0)
    b.gather_line(3, 2)
    b.gather_x(1, 0)
    b.gather_line(3, 1)
    b.gather_x(1, 2)
    b.gather_y(1, 1)
    b.target_own(1)
    b.gather_x(1, 1)
    b.gather_x(0, 3)
    b.gather_y(1, 3)
    b.bias_stage(2)
    b.back(2)
    b.back(1)
    b.gather_y(2, 1)
    b.gather_y(0, 1)
    b.gather_y(0, 2)
    b.target_own(3)
    b.gather_line(3, 3)
    b.gather_y(3, 0)
    b.gather_x(0, 1)
    b.twin_own(2)
    b.gather_x(2, 2)
    b.twin_own(1)
    b.twin_own(3)
    b.gather_x(2, 0)
    b.gather_y(0, 3)
    b.gather_x(0, 2)
    b.gather_x(2, 3)
    b.back(3)
    b.gather_x(2, 1)
    b.gather_y(2, 0)
    b.twin_x(0)
    b.gather_x(3, 2)
    b.gather_x(3, 0)
    b.twin_x(1)
    b.gather_y(2, 3)
    b.gather_y(2, 2)
    b.twin_y(0)
    b.gather_y(3, 2)
    b.gather_y(3, 3)
    b.twin_corner(1)
    b.gather_x(3, 3)
    b.twin_y(1)
    b.twin_y(2)
    b.twin_x(2)
    b.gather_y(3, 1)
    b.twin_y(3)
    b.gather_x(3, 1)
    b.through()
    b.twin_x(3)
    b.twin_corner(0)
    b.twin_corner(2)
    b.twin_own(0)
    b.twin_corner(3)
    b.bias_stage(3)
    b.gather_twin()


def fetch(s, names):
    copies = [pltpu.make_async_copy(getattr(s.r, name + "_far"), getattr(s.r, name), getattr(s.r, name + "_sem")) for name in names]
    for copy in copies:
        copy.start()
    return copies


def prepare(s):
    plan, r = s.plan, s.r
    for c in range(plan.cols):
        cols = pl.ds(c * NODE, NODE)
        part = jnp.where(r.mask[:, cols] > 0, r.lists[:, cols], -1)
        r.codes[:, cols] = part
        ones = jnp.sum(jnp.where(part >= 0, 1.0, 0.0), axis=0, keepdims=True)
        r.count[c] = jnp.broadcast_to(ones, (8, NODE))
    for start in range(0, plan.feat, NODE):
        r.x_t[start : start + NODE, :] = r.x[:, start : start + NODE].T


def opening(s):
    met = greet(s.to_z + s.to_y + s.to_x + [s.twin] + s.to_far)
    lists, mask, x, bias, s.r.cot_copy = fetch(s, ("lists", "mask", "x", "bias", "cot"))
    for copy in s.weight_copies():
        copy.start()
    for copy in (lists, mask, x, bias):
        copy.wait()
    prepare(s)
    met()


def whole_kernel(plan, names, *refs):
    s = Step(plan, Refs(names, refs))
    opening(s)
    schedule(ForwardHalf(s), BackwardHalf(s))
    s.send.settle(0)


def forward_kernel(plan, names, *refs):
    s = Step(plan, Refs(names, refs))
    opening(s)
    schedule(ForwardHalf(s), Skip())
    s.send.settle(0)


def backward_kernel(plan, names, *refs):
    s = Step(plan, Refs(names, refs))
    for copy in s.weight_copies():
        copy.start()
    greet(s.to_z + s.to_y + s.to_x + [s.twin])()
    half = BackwardHalf(s)
    for chunk in range(CHUNKS):
        rows = s.r.w.at[pl.ds(chunk * plan.slice, plan.slice)]
        pltpu.make_async_copy(rows, rows, s.r.w_sem.at[chunk]).wait()
    schedule(Skip(), half)
    s.send.settle(0)


def cast_kernel(low, act_in, fg_in, bias_in, out, act_out, fg_out, bias_out, wide, sems):
    copies = [
        pltpu.make_async_copy(src, dst, sems.at[i])
        for i, (src, dst) in enumerate(((act_in, act_out), (fg_in, fg_out), (bias_in, bias_out)))
    ]
    for copy in copies:
        copy.start()
    count, rows, _ = wide.shape
    for i in range(count):
        wide[i] = low[i * rows : (i + 1) * rows, :].astype(F32)
        copy = pltpu.make_async_copy(wide.at[i], out.at[pl.ds(i * rows, rows)], sems.at[3 + i])
        copy.start()
        copies.append(copy)
    for copy in copies:
        copy.wait()


def shaped(*items):
    return jax.ShapeDtypeStruct(*items)


def forward_scratch(plan):
    c, nz, fs = len(FINE), plan.nz, plan.slice
    v = pltpu.VMEM
    return dict(
        x=v((NODE, plan.feat), BF16),
        x_sem=DMA(()),
        lists=v((plan.slots, plan.block), I32),
        lists_sem=DMA(()),
        mask=v((plan.slots, plan.block), I32),
        mask_sem=DMA(()),
        bias=v((1, plan.feat), F32),
        bias_sem=DMA(()),
        cot=v((NODE, plan.feat), BF16),
        codes=v((plan.slots, plan.block), I32),
        x_t=v((plan.feat, NODE), BF16),
        gathered=v((plan.slice, plan.columns), BF16),
        line_codes=v((nz, plan.slots, plan.block), I32),
        count=v((plan.cols, 8, NODE), F32),
        degrees=v((plan.cols, 8, NODE), F32),
        half_send=v((fs, plan.half), BF16),
        half_recv=v((fs, plan.half), BF16),
        x_send=v((fs, plan.half), BF16),
        x_recv=v((plan.nx - 1, fs, plan.third), BF16),
        own=v((fs, plan.half), F32),
        total=v((fs, plan.third), BF16),
        summed=v((plan.feat, NODE), BF16),
        agg_rows=v((NODE, plan.feat), BF16),
        preact=v((NODE, plan.feat), F32),
        cot_sem=DMA(()),
        codes_sem=DMA((nz,)),
        degree_sem=DMA(()),
        slice_sem=DMA((c, nz)),
        line_sem=DMA((c, plan.ny - 1)),
        half_sem=DMA((c,)),
        third_sem=DMA((c, plan.nx - 1)),
        back_sem=DMA((c,)),
    )


def backward_scratch(plan):
    nz, ny, nx, w = plan.nz, plan.ny, plan.nx, plan.wide
    v = pltpu.VMEM
    return dict(
        agg_all=v((plan.fa, plan.depth), BF16),
        pg_all=v((plan.depth, plan.fp), BF16),
        grads=v((plan.line, plan.slice), BF16),
        tile_send=v((w, plan.fh, plan.fw), BF16),
        tile_recv=v((w, plan.fh, plan.fw), BF16),
        tile=v((w, plan.fh, plan.fw), F32),
        sum_send=v((w, 3, plan.fz, plan.fw), BF16),
        sum_recv=v((w, 5, plan.fz, plan.fw), BF16),
        final=v((w, plan.fz, plan.fw), BF16),
        y_send=v((BACK, ny - 1, plan.group, plan.wb), BF16),
        y_recv=v((BACK, ny - 1, plan.group, plan.wb), BF16),
        target=v((BACK, plan.group, plan.wb), F32),
        back=v((BACK, plan.group, plan.wb), BF16),
        returned=v((NODE, plan.feat), BF16),
        bias_k=v((CORES, 1, plan.feat), F32),
        bias_x=v((nx, 1, plan.feat), F32),
        bias_y=v((ny, 1, plan.feat), F32),
        bias_z=v((nz, 1, plan.feat), F32),
        local_sem=DMA((w,)),
        agg_x_sem=DMA((len(FINE), nx - 1)),
        agg_y_sem=DMA((ny - 1,)),
        pg_y_sem=DMA((w, ny - 1)),
        pg_x_sem=DMA((w, nx - 1)),
        grads_z_sem=DMA((BACK,)),
        grads_x_sem=DMA((BACK, nx - 1)),
        grads_k_sem=DMA((BACK,)),
        tile_sem=DMA((w,)),
        sum_sem=DMA((w, 5)),
        gather_z_sem=DMA((w, nz)),
        gather_x_sem=DMA((w, nz, nx - 1)),
        gather_y_sem=DMA((w, nz, ny - 1)),
        corner_sem=DMA((w, ny - 1, nx - 1)),
        twin_sem=DMA(()),
        y_sem=DMA((BACK, ny - 1)),
        returned_sem=DMA((BACK,)),
        total_sem=DMA((4,)),
    )


def call(body, plan, name, identity, inputs, outputs, scratch, vmem=127 << 19):
    scratch = dict(scratch, w=pltpu.VMEM((plan.feat, plan.feat), BF16), w_sem=DMA((CHUNKS,)), sems=DMA((RING,)))
    names = list(inputs) + list(outputs) + list(scratch)
    return pl.pallas_call(
        functools.partial(body, plan, names),
        name=name,
        out_shape=[pltpu.VMEM(shape, kind) if plan.merged else shaped(shape, kind) for shape, kind, _ in outputs.values()],
        in_specs=[pl.BlockSpec(memory_space=space) for _, space in inputs.values()],
        out_specs=[pl.BlockSpec(memory_space=space) for _, _, space in outputs.values()],
        scratch_shapes=list(scratch.values()),
        compiler_params=pltpu.CompilerParams(
            collective_id=identity, has_side_effects=True, vmem_limit_bytes=vmem
        ),
    )(*[array for array, _ in inputs.values()])


def on_device(plan, features, neighbours, edge_mask, weight, bias, cotangent):
    feat, v, far = plan.feat, pltpu.VMEM, pl.ANY
    arguments = dict(
        x_far=(features, far),
        lists_far=(neighbours.T, far),
        mask_far=(edge_mask.T, far),
        w_hbm=(weight, far),
        bias_far=(bias.reshape(1, -1), far),
        cot_far=(cotangent, far),
    )
    between = dict(
        pg=((NODE, feat), BF16),
        scaled=((NODE, feat), BF16),
        agg=((feat, NODE), BF16),
        adj=((plan.columns, plan.line), BF16),
        bias_sum=((1, feat), F32),
    )
    act = dict(act=((NODE, feat), BF16, v))
    results = dict(fg=((NODE, feat), F32, v), low=((feat, feat), BF16, far), bias_grad=((1, feat), F32, v))
    if plan.merged:
        scratch = dict(forward_scratch(plan), **backward_scratch(plan))
        scratch.update({name: v(*item) for name, item in between.items()})
        activations, feature_grad, low, bias_grad = call(
            whole_kernel, plan, "layer", 0, arguments, dict(act, **results), scratch,
            46 << 20,
        )
    else:
        activations, *kept = call(
            forward_kernel, plan, "forward", 0, arguments,
            dict(act, **{name: item + (v,) for name, item in between.items()}),
            forward_scratch(plan),
        )
        feature_grad, low, bias_grad = call(
            backward_kernel, plan, "backward", 1,
            dict({name: (array, v) for name, array in zip(between, kept)}, w_hbm=(weight, far)),
            results, backward_scratch(plan),
        )
    parts = 8
    vmem, hbm = pl.BlockSpec(memory_space=v), pl.BlockSpec(memory_space=far)
    weight_grad, activations, feature_grad, bias_grad = pl.pallas_call(
        cast_kernel,
        name="cast",
        out_shape=[shaped(low.shape, F32)] + [shaped(a.shape, a.dtype) for a in (activations, feature_grad, bias_grad)],
        in_specs=[vmem] * 4,
        out_specs=[hbm] * 4,
        scratch_shapes=[v((parts, feat // parts, feat), F32), DMA((3 + parts,))],
        compiler_params=pltpu.CompilerParams(vmem_limit_bytes=30 << 20),
    )(low, activations, feature_grad, bias_grad)
    return activations, feature_grad, weight_grad, bias_grad.reshape(-1)


def solution(mesh):
    placed = (
        P(("row", "col"), None),
        P("row", "col"),
        P("row", "col"),
        P(),
        P(),
        P(("row", "col"), None),
    )

    def run(*args):
        plan = Plan(mesh, args[0].shape[1], args[1].shape[1] // mesh.shape["col"])
        return jax.shard_map(
            functools.partial(on_device, plan),
            mesh=mesh,
            in_specs=placed,
            out_specs=(P(("row", "col"), None), P(("row", "col"), None), P(), P()),
            check_vma=False,
        )(*args)

    return run
```

```python
import functools

import jax
import jax.numpy as jnp
from jax import lax
from jax.experimental import pallas as pl
from jax.experimental.pallas import tpu as pltpu
from jax.sharding import PartitionSpec as P

MESH = pl.DeviceIdType.MESH
BF16, F32, I32 = jnp.bfloat16, jnp.float32, jnp.int32
DMA = pltpu.SemaphoreType.DMA
NODE = 128
SPLIT = 4
CORES = 2
CHUNKS = 4
FINE = (4, 4, 4, 4)
WIDE = 4
BACK = 4
RING = 32


class Plan:
    def __init__(self, mesh, feat, slots):
        rows, cols = mesh.shape["row"], mesh.shape["col"]
        self.rows, self.cols, self.feat, self.slots = rows, cols, feat, slots
        self.nz, self.ny, self.nx = SPLIT, rows // SPLIT, cols // CORES
        self.slice = feat // self.nz
        self.width = self.slice // CHUNKS
        sizes = [self.slice // share for share in FINE]
        self.fine = [(sum(sizes[:i]), size) for i, size in enumerate(sizes)]
        self.columns = rows * NODE
        self.block = cols * NODE
        self.line = self.nz * self.block
        self.half = self.line // CORES
        self.third = self.half // self.nx
        self.fa, self.fp = feat // self.nx, feat // self.ny
        self.wide = min(WIDE, self.fp // NODE)
        self.fh, self.fw = self.fa // CORES, self.fp // self.wide
        self.fz = self.fh // self.nz
        self.group = self.nz * NODE
        self.wb = self.slice // BACK
        self.depth = self.ny * self.nx * NODE
        self.merged = self.columns * self.line <= 1 << 22

    def place(self):
        row, col = lax.axis_index("row"), lax.axis_index("col")
        return row // self.ny, lax.rem(row, self.ny), col // CORES, lax.rem(col, CORES)

    def device(self, z, y, x, k):
        return (z * self.ny + y, x * CORES + k)


class Refs:
    def __init__(self, names, refs):
        self.__dict__.update(zip(names, refs, strict=True))


def guarded(when, act):
    if when is None:
        act()
    else:
        pl.when(when)(act)


class Sends:
    def __init__(self, sems):
        self.sems, self.started, self.settled = sems, [], 0

    def __call__(self, src, dst, recv, device, when=None):
        self.settle(RING - 1)
        copy = pltpu.make_async_remote_copy(
            src_ref=src,
            dst_ref=dst,
            send_sem=self.sems.at[len(self.started) % RING],
            recv_sem=recv,
            device_id=device,
            device_id_type=MESH,
        )
        guarded(when, copy.start)
        self.started.append((copy, when))

    def settle(self, keep):
        while len(self.started) - self.settled > keep:
            copy, when = self.started[self.settled]
            guarded(when, copy.wait_send)
            self.settled += 1


def others(index, count):
    return [lax.rem(index + step, count) for step in range(1, count)]


def seen(i, count):
    return count - 2 - i


def at(start, size):
    return pl.ds(pl.multiple_of(start, size), size)


def span(start, size):
    return pl.ds(pl.multiple_of(start, 16), size)


def loop(count, step):
    if count <= 4:
        for i in range(count):
            step(i)
    else:

        def body(i, carry):
            step(i)
            return carry

        lax.fori_loop(0, count, body, 0)


def greet(devices):
    barrier = pltpu.get_barrier_semaphore()
    for device in devices:
        pl.semaphore_signal(barrier, inc=1, device_id=device, device_id_type=MESH)
    return lambda: pl.semaphore_wait(barrier, len(devices))


class Step:
    def __init__(self, plan, refs):
        self.plan, self.r = plan, refs
        self.z, self.y, self.x, self.k = z, y, x, k = plan.place()
        self.zs, self.ys, self.xs = others(z, plan.nz), others(y, plan.ny), others(x, plan.nx)
        self.here, self.twin = plan.device(z, y, x, k), plan.device(z, y, x, 1 - k)
        self.to_z = [plan.device(a, y, x, k) for a in self.zs]
        self.to_y = [plan.device(z, b, x, k) for b in self.ys]
        self.to_x = [plan.device(z, y, a, k) for a in self.xs]
        self.to_far = [plan.device(z, y, a, 1 - k) for a in self.xs]
        self.send = Sends(refs.sems)

    def arrived(self, ref, sem):
        pltpu.make_async_remote_copy(
            src_ref=ref, dst_ref=ref, send_sem=sem, recv_sem=sem, device_id=self.here, device_id_type=MESH
        ).wait_recv()

    def weight_copies(self):
        plan, r = self.plan, self.r
        copies = []
        for chunk in range(CHUNKS):
            for a in range(plan.nz):
                i = chunk * plan.nz + a
                copies.append(
                    pltpu.make_async_copy(
                        r.w_hbm.at[pl.ds(a * plan.slice + chunk * plan.width, plan.width)],
                        r.w.at[pl.ds(i * plan.width, plan.width)],
                        r.w_sem.at[chunk],
                    )
                )
        return copies


def of_part(task):
    def run(half, part, *where):
        if part < half.s.plan.wide:
            task(half, part, *where)

    return run


class ForwardHalf:
    def __init__(self, s):
        self.s = s
        plan, r, x, k = s.plan, s.r, s.x, s.k
        self.mates = s.to_x + [s.twin] + s.to_far
        self.mate_cols = [a * CORES + k for a in s.xs] + [x * CORES + 1 - k] + [a * CORES + 1 - k for a in s.xs]

    def block_of(self, a, b):
        return at((b * self.s.plan.nz + a) * NODE, NODE)

    def send_codes(self):
        s, r = self.s, self.s.r
        for device in s.to_z:
            s.send(r.codes, r.line_codes.at[s.z], r.codes_sem.at[s.z], device)

    def send_counts(self):
        s, r = self.s, self.s.r
        col = s.x * CORES + s.k
        for device, c in zip(self.mates, self.mate_cols):
            s.send(r.count.at[c], r.degrees.at[col], r.degree_sem, device)
        r.degrees[col] = r.count[col]

    def send_slices(self, chunk):
        s, r, plan = self.s, self.s.r, self.s.plan
        start, size = plan.fine[chunk]
        rows, mine = pl.ds(start, size), self.block_of(s.z, s.y)
        for a, device in zip(s.zs, s.to_z):
            source = r.x_t.at[span(a * plan.slice + start, size)]
            s.send(source, r.gathered.at[rows, mine], r.slice_sem.at[chunk, s.z], device)
        own = span(s.z * plan.slice + start, size)
        for i, device in enumerate(s.to_y):
            s.send(r.x_t.at[own], r.gathered.at[rows, mine], r.line_sem.at[chunk, seen(i, plan.ny)], device)
        r.gathered[rows, mine] = r.x_t[own, :]

    def build(self, i):
        s = self.s
        plan, r, nz, ny = s.plan, s.r, s.plan.nz, s.plan.ny
        a = ([s.z] + s.zs)[i]
        source = r.codes if i == 0 else r.line_codes.at[a]
        if i > 0:
            s.arrived(source, r.codes_sem.at[a])
        groups, strip = (plan.rows + 3) // 4, 32
        for c in range(plan.cols):
            columns = at((((c % CORES) * plan.nx + c // CORES) * nz + a) * NODE, NODE)
            part = source[:, c * NODE : (c + 1) * NODE]
            low = jnp.where(part >= 0, part % NODE, -1)
            high = jnp.where(part >= 0, part // NODE, -1)
            adds = [
                sum(jnp.where(high == 4 * g + j, 1 << (8 * j), 0) for j in range(4) if 4 * g + j < plan.rows)
                for g in range(groups)
            ]
            for start in range(0, NODE, strip):
                lanes = lax.broadcasted_iota(I32, (strip, NODE), 0) + start
                packed = [jnp.zeros((strip, NODE), I32) for _ in range(groups)]
                for slot in range(plan.slots):
                    hit = low[slot : slot + 1, :] == lanes
                    packed = [p + jnp.where(hit, v[slot : slot + 1, :], 0) for p, v in zip(packed, adds)]
                for row in range(plan.rows):
                    start_row = ((row % ny) * nz + row // ny) * NODE + start
                    number = (packed[row // 4] >> (8 * (row % 4))) & 255
                    r.adj[start_row : start_row + strip, columns] = number.astype(F32).astype(BF16)

    def pass_on(self, chunk, i):
        s, r, a = self.s, self.s.r, self.s.zs[i]
        piece = r.gathered.at[pl.ds(*s.plan.fine[chunk]), self.block_of(a, s.y)]
        s.arrived(piece, r.slice_sem.at[chunk, a])
        for j, device in enumerate(s.to_y):
            s.send(piece, piece, r.line_sem.at[chunk, seen(j, s.plan.ny)], device)

    def product(self, chunk, columns_from, store):
        r, plan, tile = self.s.r, self.s.plan, 256
        rows = pl.ds(*plan.fine[chunk])

        def step(i):
            columns = r.adj[:, at(columns_from + i * tile, tile)]
            store(at(i * tile, tile), jnp.dot(r.gathered[rows, :], columns, preferred_element_type=F32))

        loop(plan.half // tile, step)

    def first(self, chunk):
        s, r, plan = self.s, self.s.r, self.s.plan
        rows = pl.ds(*plan.fine[chunk])
        for i in range(plan.ny - 1):
            s.arrived(r.gathered.at[rows, pl.ds(0, plan.group)], r.line_sem.at[chunk, i])

        def to_half(cols, value):
            r.half_send[rows, cols] = value.astype(BF16)

        self.product(chunk, (1 - s.k) * plan.half, to_half)
        s.send(r.half_send.at[rows], r.half_recv.at[rows], r.half_sem.at[chunk], s.twin)

    def own(self, chunk):
        r, rows = self.s.r, pl.ds(*self.s.plan.fine[chunk])

        def to_own(cols, value):
            r.own[rows, cols] = value

        self.product(chunk, self.s.k * self.s.plan.half, to_own)

    def second(self, chunk):
        s, r, third = self.s, self.s.r, self.s.plan.third
        rows = pl.ds(*s.plan.fine[chunk])
        s.arrived(r.half_recv.at[rows], r.half_sem.at[chunk])
        for i, (a, device) in enumerate(zip(s.xs, s.to_x)):
            cols, there = at(a * third, third), seen(i, s.plan.nx)
            r.x_send[rows, cols] = (r.own[rows, cols] + r.half_recv[rows, cols].astype(F32)).astype(BF16)
            s.send(r.x_send.at[rows, cols], r.x_recv.at[there, rows], r.third_sem.at[chunk, there], device)

    def last(self, chunk):
        s, r, plan = self.s, self.s.r, self.s.plan
        start, size = plan.fine[chunk]
        rows, cols = pl.ds(start, size), at(s.x * plan.third, plan.third)
        value = r.own[rows, cols] + r.half_recv[rows, cols].astype(F32)
        for i in range(plan.nx - 1):
            s.arrived(r.x_recv.at[i, rows], r.third_sem.at[chunk, i])
            value = value + r.x_recv[i, rows].astype(F32)
        r.total[rows] = value.astype(BF16)
        there = span(s.z * plan.slice + start, size)
        for a, device in zip(s.zs, s.to_z):
            s.send(r.total.at[rows, at(a * NODE, NODE)], r.summed.at[there], r.back_sem.at[chunk], device)
        r.summed[there, :] = r.total[rows, at(s.z * NODE, NODE)]

    def scale(self):
        s, r = self.s, self.s.r
        s.arrived(r.degrees.at[pl.ds(0, s.plan.cols - 1)], r.degree_sem)
        degree = r.degrees[0]
        for c in range(1, s.plan.cols):
            degree = degree + r.degrees[c]
        self.row = 1.0 / (degree[0:1, :] + 1.0)
        self.column = jnp.broadcast_to(self.row, (NODE, NODE)).T[:, 0:1]

    def combine(self, chunk):
        s, r, plan = self.s, self.s.r, self.s.plan
        nz, fs, width = plan.nz, plan.slice, plan.width
        start, size = plan.fine[chunk]
        s.arrived(r.summed.at[pl.ds(0, (nz - 1) * size)], r.back_sem.at[chunk])
        for a in range(nz):
            rows = pl.ds(a * fs + start, size)
            value = self.row * (r.summed[rows, :].astype(F32) + 2.0 * r.x_t[rows, :].astype(F32))
            r.agg[rows, :] = value.astype(BF16)
        end = start + size
        for begin in range(end // width * width - (width if end % width == 0 else 0), end - width + 1, width):
            for a in range(nz):
                place = begin * nz + a * width
                r.agg_rows[:, place : place + width] = r.agg[a * fs + begin : a * fs + begin + width, :].T

    def await_weight(self, chunk):
        r = self.s.r
        rows = r.w.at[pl.ds(chunk * self.s.plan.slice, self.s.plan.slice)]
        pltpu.make_async_copy(rows, rows, r.w_sem.at[chunk]).wait()

    def part_of(self, chunk, cols):
        r = self.s.r
        rows = pl.ds(chunk * self.s.plan.slice, self.s.plan.slice)
        return jnp.dot(r.agg_rows[:, rows], r.w[rows, cols], preferred_element_type=F32)

    def add(self, chunk):
        r = self.s.r
        self.await_weight(chunk)

        def step(i):
            cols = at(i * 512, 512)
            if chunk == 0:
                r.preact[:, cols] = self.part_of(chunk, cols)
            else:
                r.preact[:, cols] += self.part_of(chunk, cols)

        loop(self.s.plan.feat // 512, step)

    @of_part
    def layer(self, part):
        plan = self.s.plan
        if part == 0:
            self.await_weight(CHUNKS - 1)
            self.s.r.cot_copy.wait()
        loop(plan.ny, lambda b: self.layer_columns(at(b * plan.fp + part * plan.fw, plan.fw)))

    def layer_columns(self, cols):
        r = self.s.r
        pre = r.preact[:, cols] + self.part_of(CHUNKS - 1, cols) + r.bias[:, cols]
        square = pre * pre
        slope = 0.7978845608028654
        t = jnp.tanh(slope * pre * (1.0 + 0.044715 * square))
        r.act[:, cols] = (0.5 * pre * (1.0 + t)).astype(BF16)
        grad = 0.5 * (1.0 + t) + 0.5 * pre * (1.0 - t * t) * (slope * (1.0 + 3.0 * 0.044715 * square))
        low = (r.cot[:, cols].astype(F32) * grad).astype(BF16)
        r.pg[:, cols] = low
        wide = low.astype(F32)
        r.scaled[:, cols] = (self.column * wide).astype(BF16)
        r.bias_sum[:, cols] = jnp.sum(wide, axis=0, keepdims=True)


class BackwardHalf:
    def __init__(self, s):
        self.s = s
        plan = s.plan
        self.pair = s.z + 1 - 2 * lax.rem(s.z, 2)
        self.other = plan.nz - 1 - s.z
        self.middle = lax.rem(s.z, 3) > 0
        self.end = lax.rem(s.z, 3) == 0
        self.tile = min(256, plan.fh)
        self.copies = {}

    def nodes(self, b, a):
        return at((b * self.s.plan.nx + a) * NODE, NODE)

    def line_rows(self, c, a):
        return at((c * self.s.plan.nx + a) * self.s.plan.group, self.s.plan.group)

    def wide_cols(self, b, part):
        return at(b * self.s.plan.fp + part * self.s.plan.fw, self.s.plan.fw)

    def agg_blocks(self, chunk, part):
        plan = self.s.plan
        begin, size = plan.fine[chunk]
        for i in range(plan.nz // plan.nx):
            start = i * plan.slice + begin
            yield span(part * plan.fa + start, size), pl.ds(start, size)

    def agg_send(self, chunk):
        s, r = self.s, self.s.r
        mine = self.nodes(s.y, s.x)
        for j, (a, device) in enumerate(zip(s.xs, s.to_x)):
            for source, rows in self.agg_blocks(chunk, a):
                s.send(r.agg.at[source], r.agg_all.at[rows, mine], r.agg_x_sem.at[chunk, seen(j, s.plan.nx)], device)
        for source, rows in self.agg_blocks(chunk, s.x):
            for j, device in enumerate(s.to_y):
                s.send(r.agg.at[source], r.agg_all.at[rows, mine], r.agg_y_sem.at[seen(j, s.plan.ny)], device)
            r.agg_all[rows, mine] = r.agg[source, :]

    @of_part
    def pg_x(self, part):
        s, r, fw = self.s, self.s.r, self.s.plan.fw
        mine, cols = self.nodes(s.y, s.x), pl.ds(part * fw, fw)
        for j, device in enumerate(s.to_x):
            source = r.pg.at[:, self.wide_cols(s.y, part)]
            s.send(source, r.pg_all.at[mine, cols], r.pg_x_sem.at[part, seen(j, s.plan.nx)], device)
        r.pg_all[mine, cols] = r.pg[:, self.wide_cols(s.y, part)]

    @of_part
    def pg_y(self, part):
        s, r, fw = self.s, self.s.r, self.s.plan.fw
        mine, cols = self.nodes(s.y, s.x), pl.ds(part * fw, fw)
        for j, (b, device) in enumerate(zip(s.ys, s.to_y)):
            source = r.pg.at[:, self.wide_cols(b, part)]
            s.send(source, r.pg_all.at[mine, cols], r.pg_y_sem.at[part, seen(j, s.plan.ny)], device)

    def pass_agg(self, chunk):
        s, r, plan = self.s, self.s.r, self.s.plan
        size = plan.fine[chunk][1] * (plan.nz // plan.nx)
        for i, a in enumerate(s.xs):
            s.arrived(r.agg_all.at[pl.ds(0, size), self.nodes(s.y, a)], r.agg_x_sem.at[chunk, i])
            for _, rows in self.agg_blocks(chunk, s.x):
                ref = r.agg_all.at[rows, self.nodes(s.y, a)]
                for j, device in enumerate(s.to_y):
                    s.send(ref, ref, r.agg_y_sem.at[seen(j, plan.ny)], device)

    @of_part
    def pass_pg(self, part):
        s, r, plan = self.s, self.s.r, self.s.plan
        for i, b in enumerate(s.ys):
            ref = r.pg_all.at[self.nodes(b, s.x), pl.ds(part * plan.fw, plan.fw)]
            s.arrived(ref, r.pg_y_sem.at[part, i])
            for j, device in enumerate(s.to_x):
                s.send(ref, ref, r.pg_x_sem.at[part, seen(j, plan.nx)], device)

    def await_agg(self):
        s, r = self.s, self.s.r
        for i in range(s.plan.ny - 1):
            s.arrived(r.agg_all.at[:, pl.ds(0, s.plan.nx * NODE)], r.agg_y_sem.at[i])

    def tile_product(self, part, rows_from, store):
        r, plan, tile = self.s.r, self.s.plan, self.tile
        cols = pl.ds(part * plan.fw, plan.fw)

        def step(i):
            rows = r.agg_all[at(rows_from + i * tile, tile), :]
            store(at(i * tile, tile), jnp.dot(rows, r.pg_all[:, cols], preferred_element_type=F32))

        loop(plan.fh // tile, step)

    @of_part
    def tile_part(self, part):
        s, r, plan = self.s, self.s.r, self.s.plan
        for i in range(plan.nx - 1):
            s.arrived(r.pg_all.at[pl.ds(0, plan.ny * NODE), pl.ds(part * plan.fw, plan.fw)], r.pg_x_sem.at[part, i])

        def to_half(rows, value):
            r.tile_send[part, rows, :] = value.astype(BF16)

        self.tile_product(part, (1 - s.k) * plan.fh, to_half)
        s.send(r.tile_send.at[part], r.tile_recv.at[part], r.tile_sem.at[part], s.twin)

    @of_part
    def tile_own(self, part):
        r = self.s.r

        def to_own(rows, value):
            r.tile[part, rows, :] = value

        self.tile_product(part, self.s.k * self.s.plan.fh, to_own)

    def own_part(self, part, a):
        r, fz = self.s.r, self.s.plan.fz
        rows = at(a * fz, fz)
        return r.tile[part, rows, :] + r.tile_recv[part, rows, :].astype(F32)

    @of_part
    def sum_start(self, part):
        s, r = self.s, self.s.r
        s.arrived(r.tile_recv.at[part], r.tile_sem.at[part])
        pair, other = self.pair, self.other
        targets = [other, s.plan.nz - 1 - pair, pair]

        @pl.when(self.end)
        def _():
            for i, a in enumerate(targets):
                r.sum_send[part, i] = self.own_part(part, a).astype(BF16)

        for i in range(3):
            s.send(
                r.sum_send.at[part, i], r.sum_recv.at[part, i], r.sum_sem.at[part, i],
                s.plan.device(pair, s.y, s.x, s.k), self.end,
            )

    def sum_step(self, part, i, into, slot, a, to):
        s, r = self.s, self.s.r

        @pl.when(self.middle)
        def _():
            s.arrived(r.sum_recv.at[part, i], r.sum_sem.at[part, i])
            r.sum_send[part, slot] = (self.own_part(part, a) + r.sum_recv[part, i].astype(F32)).astype(BF16)

        s.send(
            r.sum_send.at[part, slot], r.sum_recv.at[part, into], r.sum_sem.at[part, into],
            s.plan.device(to, s.y, s.x, s.k), self.middle,
        )

    @of_part
    def sum_far(self, part):
        self.sum_step(part, 0, 3, 0, self.s.plan.nz - 1 - self.pair, self.other)

    @of_part
    def sum_other(self, part):
        self.sum_step(part, 1, 4, 1, self.other, self.other)

    @of_part
    def sum_out(self, part):
        self.sum_step(part, 3, 0, 2, self.pair, self.pair)

    @of_part
    def sum_end(self, part):
        s, r = self.s, self.s.r
        mine = self.own_part(part, s.z)

        @pl.when(self.middle)
        def _():
            s.arrived(r.sum_recv.at[part, 2], r.sum_sem.at[part, 2])
            s.arrived(r.sum_recv.at[part, 4], r.sum_sem.at[part, 4])
            r.final[part] = (mine + r.sum_recv[part, 2].astype(F32) + r.sum_recv[part, 4].astype(F32)).astype(BF16)

        @pl.when(self.end)
        def _():
            s.arrived(r.sum_recv.at[part, 0], r.sum_sem.at[part, 0])
            r.final[part] = (mine + r.sum_recv[part, 0].astype(F32)).astype(BF16)

        copy = pltpu.make_async_copy(r.final.at[part], self.piece(part, s.z, s.y, s.x), r.local_sem.at[part])
        copy.start()
        self.copies[part] = copy
        self.spread(r.final.at[part], part, s.z)
        self.along(r.final.at[part], part, s.z, self.pair, None)
        self.along(r.final.at[part], part, s.z, self.other, self.middle)

    def block(self, part, a_y, a_x):
        plan = self.s.plan
        return self.s.r.low.at[at(a_x * plan.fa + self.s.k * plan.fh, plan.fh), self.wide_cols(a_y, part)]

    def piece(self, part, a_z, a_y, a_x):
        plan = self.s.plan
        rows = at(a_x * plan.fa + self.s.k * plan.fh + a_z * plan.fz, plan.fz)
        return self.s.r.low.at[rows, self.wide_cols(a_y, part)]

    def along(self, source, part, a_z, to, when):
        s = self.s
        device = s.plan.device(to, s.y, s.x, s.k)
        s.send(source, self.piece(part, a_z, s.y, s.x), s.r.gather_z_sem.at[part, a_z], device, when)

    def spread(self, source, part, a_z):
        s, r = self.s, self.s.r
        target = self.piece(part, a_z, s.y, s.x)
        for i, device in enumerate(s.to_x):
            s.send(source, target, r.gather_x_sem.at[part, a_z, seen(i, s.plan.nx)], device)
        for i, device in enumerate(s.to_y):
            s.send(source, target, r.gather_y_sem.at[part, a_z, seen(i, s.plan.ny)], device)

    def line_order(self):
        return [self.s.z, self.pair, 2 - self.s.z // 2, 3 - 3 * (self.s.z // 2)]

    @of_part
    def gather_line(self, part, i):
        s = self.s
        a_z = self.line_order()[i]
        piece = self.piece(part, a_z, s.y, s.x)
        s.arrived(piece, s.r.gather_z_sem.at[part, a_z])
        self.along(piece, part, a_z, self.other if i == 1 else self.pair, self.middle)
        self.spread(piece, part, a_z)

    @of_part
    def gather_x(self, part, i):
        s, r, plan = self.s, self.s.r, self.s.plan
        a_z = self.line_order()[i]
        for j, a_x in enumerate(s.xs):
            piece = self.piece(part, a_z, s.y, a_x)
            s.arrived(piece, r.gather_x_sem.at[part, a_z, j])
            for m, device in enumerate(s.to_y):
                s.send(piece, piece, r.corner_sem.at[part, seen(m, plan.ny), j], device, lax.rem(a_z, 2) == 0)

    @of_part
    def gather_y(self, part, i):
        s, r, plan = self.s, self.s.r, self.s.plan
        a_z = self.line_order()[i]
        for j, a_y in enumerate(s.ys):
            piece = self.piece(part, a_z, a_y, s.x)
            s.arrived(piece, r.gather_y_sem.at[part, a_z, j])
            for m, device in enumerate(s.to_x):
                s.send(piece, piece, r.corner_sem.at[part, j, seen(m, plan.nx)], device, lax.rem(a_z, 2) == 1)

    def to_twin(self, part, a_y, a_x):
        s = self.s
        block = self.block(part, a_y, a_x)
        s.send(block, block, s.r.twin_sem, s.twin)

    @of_part
    def twin_own(self, part):
        self.copies[part].wait()
        self.to_twin(part, self.s.y, self.s.x)

    @of_part
    def twin_x(self, part):
        for a_x in self.s.xs:
            self.to_twin(part, self.s.y, a_x)

    @of_part
    def twin_y(self, part):
        for a_y in self.s.ys:
            self.to_twin(part, a_y, self.s.x)

    @of_part
    def twin_corner(self, part):
        s = self.s
        for j, a_y in enumerate(s.ys):
            for i, a_x in enumerate(s.xs):
                s.arrived(self.block(part, a_y, a_x), s.r.corner_sem.at[part, j, i])
                self.to_twin(part, a_y, a_x)

    def gather_twin(self):
        s, feat = self.s, self.s.plan.feat
        s.send.settle(16)
        s.arrived(s.r.low.at[pl.ds(0, feat // CORES)], s.r.twin_sem)

    def grads_start(self, part):
        s, r, plan = self.s, self.s.r, self.s.plan
        fs, wb = plan.slice, plan.wb
        mine, cols = at(((s.k * plan.nx + s.x) * plan.nz + s.z) * NODE, NODE), pl.ds(part * wb, wb)
        for a, device in zip(s.zs, s.to_z):
            s.send(r.scaled.at[:, at(a * fs + part * wb, wb)], r.grads.at[mine, cols], r.grads_z_sem.at[part], device)
        r.grads[mine, cols] = r.scaled[:, at(s.z * fs + part * wb, wb)]

    def grads_x(self, part):
        s, r, plan = self.s, self.s.r, self.s.plan
        cols = pl.ds(part * plan.wb, plan.wb)
        s.arrived(r.grads.at[pl.ds(0, (plan.nz - 1) * NODE), cols], r.grads_z_sem.at[part])
        ref = r.grads.at[self.line_rows(s.k, s.x), cols]
        for i, device in enumerate(s.to_x):
            s.send(ref, ref, r.grads_x_sem.at[part, seen(i, plan.nx)], device)
        s.send(ref, ref, r.grads_k_sem.at[part], s.twin)

    def grads_twin(self, part):
        s, r, plan = self.s, self.s.r, self.s.plan
        for i, a in enumerate(s.xs):
            ref = r.grads.at[self.line_rows(s.k, a), pl.ds(part * plan.wb, plan.wb)]
            s.arrived(ref, r.grads_x_sem.at[part, i])
            s.send(ref, ref, r.grads_k_sem.at[part], s.twin)

    def target_product(self, part, b, store):
        r, plan = self.s.r, self.s.plan
        cols = pl.ds(part * plan.wb, plan.wb)

        def step(i):
            rows = r.adj[at(b * plan.group + i * 256, 256), :]
            store(at(i * 256, 256), jnp.dot(rows, r.grads[:, cols], preferred_element_type=F32))

        loop(plan.group // 256, step)

    def target(self, part):
        s, r, plan = self.s, self.s.r, self.s.plan
        s.arrived(r.grads.at[pl.ds(0, plan.line // CORES), pl.ds(part * plan.wb, plan.wb)], r.grads_k_sem.at[part])
        for i, (b, device) in enumerate(zip(s.ys, s.to_y)):

            def to_y(rows, value):
                r.y_send[part, i, rows, :] = value.astype(BF16)

            self.target_product(part, b, to_y)
            there = seen(i, plan.ny)
            s.send(r.y_send.at[part, i], r.y_recv.at[part, there], r.y_sem.at[part, there], device)

    def target_own(self, part):
        r = self.s.r

        def to_target(rows, value):
            r.target[part, rows, :] = value

        self.target_product(part, self.s.y, to_target)

    def back(self, part):
        s, r, plan = self.s, self.s.r, self.s.plan
        value = r.target[part]
        for i in range(plan.ny - 1):
            s.arrived(r.y_recv.at[part, i], r.y_sem.at[part, i])
            value = value + r.y_recv[part, i].astype(F32)
        r.back[part] = value.astype(BF16)
        cols = at(s.z * plan.slice + part * plan.wb, plan.wb)
        for a, device in zip(s.zs, s.to_z):
            s.send(r.back.at[part, at(a * NODE, NODE)], r.returned.at[:, cols], r.returned_sem.at[part], device)
        r.returned[:, cols] = r.back[part, at(s.z * NODE, NODE), :]

    def through(self):
        s, r, plan = self.s, self.s.r, self.s.plan
        for part in range(BACK):
            s.arrived(r.returned.at[:, pl.ds(0, (plan.nz - 1) * plan.wb)], r.returned_sem.at[part])
        r.returned[...] = (r.returned[...].astype(F32) + 2.0 * r.scaled[...].astype(F32)).astype(BF16)
        for chunk in range(CHUNKS):
            rows = pl.ds(chunk * plan.slice, plan.slice)
            value = lax.dot_general(
                r.returned[...], r.w[rows, :], (((1,), (1,)), ((), ())), preferred_element_type=F32
            )
            for a in range(plan.nz):
                cols = pl.ds(a * plan.slice + chunk * plan.width, plan.width)
                r.fg[:, cols] = value[:, a * plan.width : (a + 1) * plan.width]

    def bias_start(self):
        s, r = self.s, self.s.r
        s.send(r.bias_sum, r.bias_k.at[s.k], r.total_sem.at[0], s.twin)
        r.bias_k[s.k] = r.bias_sum[...]

    def bias_stage(self, stage):
        s, r, plan = self.s, self.s.r, self.s.plan
        ref, count = ((r.bias_k, CORES), (r.bias_x, plan.nx), (r.bias_y, plan.ny), (r.bias_z, plan.nz))[stage]
        s.arrived(ref.at[pl.ds(0, count - 1)], r.total_sem.at[stage])
        value = ref[0]
        for a in range(1, count):
            value = value + ref[a]
        if stage == 3:
            r.bias_grad[...] = value
            return
        ref, index, devices = ((r.bias_x, s.x, s.to_x), (r.bias_y, s.y, s.to_y), (r.bias_z, s.z, s.to_z))[stage]
        ref[index] = value
        for device in devices:
            s.send(ref.at[index], ref.at[index], r.total_sem.at[stage + 1], device)


class Skip:
    def __getattr__(self, name):
        return lambda *where: None


def schedule(f, b):
    f.send_slices(0)
    f.send_counts()
    f.scale()
    f.send_codes()
    f.build(0)
    f.pass_on(0, 0)
    f.send_slices(1)
    f.send_slices(2)
    f.pass_on(0, 2)
    f.pass_on(0, 1)
    f.build(3)
    f.build(1)
    f.pass_on(1, 2)
    f.build(2)
    f.pass_on(1, 1)
    f.pass_on(1, 0)
    f.send_slices(3)
    f.first(0)
    f.pass_on(2, 2)
    f.own(0)
    f.pass_on(2, 1)
    f.pass_on(2, 0)
    f.second(0)
    f.first(1)
    f.pass_on(3, 1)
    f.own(1)
    f.pass_on(3, 0)
    f.second(1)
    f.pass_on(3, 2)
    f.first(2)
    f.last(0)
    f.own(2)
    f.second(2)
    f.first(3)
    f.last(1)
    f.own(3)
    f.second(3)
    f.combine(0)
    f.last(2)
    b.agg_send(0)
    f.add(0)
    f.combine(1)
    b.agg_send(1)
    f.last(3)
    f.add(1)
    b.pass_agg(0)
    f.combine(2)
    b.pass_agg(1)
    b.agg_send(2)
    f.add(2)
    f.combine(3)
    b.agg_send(3)
    f.layer(0)
    b.pg_y(0)
    f.layer(1)
    b.pg_x(0)
    f.layer(2)
    f.layer(3)
    b.grads_start(3)
    b.pg_x(2)
    b.pg_y(1)
    b.grads_start(0)
    b.pass_agg(2)
    b.grads_start(2)
    b.pg_x(1)
    b.pass_agg(3)
    b.pg_y(2)
    b.pg_y(3)
    b.pass_pg(0)
    b.pass_pg(1)
    b.grads_x(3)
    b.grads_start(1)
    b.await_agg()
    b.tile_part(0)
    b.tile_own(0)
    b.grads_x(0)
    b.bias_start()
    b.sum_start(0)
    b.tile_part(1)
    b.tile_own(1)
    b.pass_pg(2)
    b.grads_twin(3)
    b.bias_stage(0)
    b.sum_start(1)
    b.target(3)
    b.grads_x(1)
    b.sum_far(0)
    b.pass_pg(3)
    b.pg_x(3)
    b.grads_twin(0)
    b.bias_stage(1)
    b.tile_part(2)
    b.sum_other(0)
    b.target(0)
    b.sum_out(0)
    b.sum_far(1)
    b.tile_own(2)
    b.grads_x(2)
    b.sum_start(2)
    b.grads_twin(1)
    b.sum_other(1)
    b.sum_end(0)
    b.target(1)
    b.sum_out(1)
    b.sum_far(2)
    b.tile_part(3)
    b.sum_other(2)
    b.grads_twin(2)
    b.sum_end(1)
    b.tile_own(3)
    b.sum_start(3)
    b.gather_line(0, 1)
    b.sum_out(2)
    b.target(2)
    b.sum_end(2)
    b.gather_x(1, 0)
    b.gather_line(1, 1)
    b.gather_line(0, 2)
    b.sum_far(3)
    b.gather_line(1, 2)
    b.gather_x(0, 1)
    b.gather_line(0, 3)
    b.gather_y(0, 0)
    b.gather_line(2, 2)
    b.target_own(0)
    b.sum_other(3)
    b.gather_line(2, 1)
    b.gather_y(2, 0)
    b.sum_out(3)
    b.gather_y(0, 1)
    b.sum_end(3)
    b.twin_own(0)
    b.gather_x(1, 1)
    b.target_own(2)
    b.gather_line(2, 3)
    b.gather_x(0, 0)
    b.gather_y(1, 1)
    b.gather_line(1, 3)
    b.gather_x(0, 3)
    b.target_own(3)
    b.gather_line(3, 2)
    b.back(3)
    b.target_own(1)
    b.back(0)
    b.gather_line(3, 1)
    b.back(1)
    b.gather_y(0, 3)
    b.gather_x(0, 2)
    b.gather_line(3, 3)
    b.gather_x(3, 2)
    b.gather_x(1, 2)
    b.back(2)
    b.gather_y(2, 1)
    b.gather_y(1, 3)
    b.gather_x(1, 3)
    b.gather_y(0, 2)
    b.gather_y(3, 0)
    b.gather_x(3, 0)
    b.gather_x(3, 3)
    b.twin_own(1)
    b.gather_y(1, 2)
    b.gather_y(2, 2)
    b.gather_x(2, 0)
    b.gather_y(3, 2)
    b.twin_corner(0)
    b.twin_x(0)
    b.gather_y(1, 0)
    b.gather_x(2, 2)
    b.gather_x(3, 1)
    b.gather_x(2, 3)
    b.twin_x(3)
    b.twin_x(1)
    b.twin_own(2)
    b.twin_own(3)
    b.twin_y(0)
    b.gather_y(3, 3)
    b.gather_y(3, 1)
    b.gather_x(2, 1)
    b.gather_y(2, 3)
    b.bias_stage(2)
    b.twin_x(2)
    b.twin_y(1)
    b.twin_y(2)
    b.through()
    b.twin_corner(3)
    b.twin_y(3)
    b.bias_stage(3)
    b.twin_corner(1)
    b.twin_corner(2)
    b.gather_twin()


def fetch(s, names):
    copies = [pltpu.make_async_copy(getattr(s.r, name + "_far"), getattr(s.r, name), getattr(s.r, name + "_sem")) for name in names]
    for copy in copies:
        copy.start()
    return copies


def prepare(s):
    plan, r = s.plan, s.r
    for c in range(plan.cols):
        cols = pl.ds(c * NODE, NODE)
        part = jnp.where(r.mask[:, cols] > 0, r.lists[:, cols], -1)
        r.codes[:, cols] = part
        ones = jnp.sum(jnp.where(part >= 0, 1.0, 0.0), axis=0, keepdims=True)
        r.count[c] = jnp.broadcast_to(ones, (8, NODE))
    for start in range(0, plan.feat, NODE):
        r.x_t[start : start + NODE, :] = r.x[:, start : start + NODE].T


def opening(s):
    met = greet(s.to_z + s.to_y + s.to_x + [s.twin] + s.to_far)
    lists, mask, x, bias, s.r.cot_copy = fetch(s, ("lists", "mask", "x", "bias", "cot"))
    for copy in s.weight_copies():
        copy.start()
    for copy in (lists, mask, x, bias):
        copy.wait()
    prepare(s)
    met()


def whole_kernel(plan, names, *refs):
    s = Step(plan, Refs(names, refs))
    opening(s)
    schedule(ForwardHalf(s), BackwardHalf(s))
    s.send.settle(0)


def forward_kernel(plan, names, *refs):
    s = Step(plan, Refs(names, refs))
    opening(s)
    schedule(ForwardHalf(s), Skip())
    s.send.settle(0)


def backward_kernel(plan, names, *refs):
    s = Step(plan, Refs(names, refs))
    for copy in s.weight_copies():
        copy.start()
    greet(s.to_z + s.to_y + s.to_x + [s.twin])()
    half = BackwardHalf(s)
    for chunk in range(CHUNKS):
        rows = s.r.w.at[pl.ds(chunk * plan.slice, plan.slice)]
        pltpu.make_async_copy(rows, rows, s.r.w_sem.at[chunk]).wait()
    schedule(Skip(), half)
    s.send.settle(0)


def cast_kernel(low, act_in, fg_in, bias_in, out, act_out, fg_out, bias_out, wide, sems):
    copies = [
        pltpu.make_async_copy(src, dst, sems.at[i])
        for i, (src, dst) in enumerate(((act_in, act_out), (fg_in, fg_out), (bias_in, bias_out)))
    ]
    for copy in copies:
        copy.start()
    count, rows, _ = wide.shape
    for i in range(count):
        wide[i] = low[i * rows : (i + 1) * rows, :].astype(F32)
        copy = pltpu.make_async_copy(wide.at[i], out.at[pl.ds(i * rows, rows)], sems.at[3 + i])
        copy.start()
        copies.append(copy)
    for copy in copies:
        copy.wait()


def shaped(*items):
    return jax.ShapeDtypeStruct(*items)


def forward_scratch(plan):
    c, nz, fs = len(FINE), plan.nz, plan.slice
    v = pltpu.VMEM
    return dict(
        x=v((NODE, plan.feat), BF16),
        x_sem=DMA(()),
        lists=v((plan.slots, plan.block), I32),
        lists_sem=DMA(()),
        mask=v((plan.slots, plan.block), I32),
        mask_sem=DMA(()),
        bias=v((1, plan.feat), F32),
        bias_sem=DMA(()),
        cot=v((NODE, plan.feat), BF16),
        codes=v((plan.slots, plan.block), I32),
        x_t=v((plan.feat, NODE), BF16),
        gathered=v((plan.slice, plan.columns), BF16),
        line_codes=v((nz, plan.slots, plan.block), I32),
        count=v((plan.cols, 8, NODE), F32),
        degrees=v((plan.cols, 8, NODE), F32),
        half_send=v((fs, plan.half), BF16),
        half_recv=v((fs, plan.half), BF16),
        x_send=v((fs, plan.half), BF16),
        x_recv=v((plan.nx - 1, fs, plan.third), BF16),
        own=v((fs, plan.half), F32),
        total=v((fs, plan.third), BF16),
        summed=v((plan.feat, NODE), BF16),
        agg_rows=v((NODE, plan.feat), BF16),
        preact=v((NODE, plan.feat), F32),
        cot_sem=DMA(()),
        codes_sem=DMA((nz,)),
        degree_sem=DMA(()),
        slice_sem=DMA((c, nz)),
        line_sem=DMA((c, plan.ny - 1)),
        half_sem=DMA((c,)),
        third_sem=DMA((c, plan.nx - 1)),
        back_sem=DMA((c,)),
    )


def backward_scratch(plan):
    nz, ny, nx, w = plan.nz, plan.ny, plan.nx, plan.wide
    v = pltpu.VMEM
    return dict(
        agg_all=v((plan.fa, plan.depth), BF16),
        pg_all=v((plan.depth, plan.fp), BF16),
        grads=v((plan.line, plan.slice), BF16),
        tile_send=v((w, plan.fh, plan.fw), BF16),
        tile_recv=v((w, plan.fh, plan.fw), BF16),
        tile=v((w, plan.fh, plan.fw), F32),
        sum_send=v((w, 3, plan.fz, plan.fw), BF16),
        sum_recv=v((w, 5, plan.fz, plan.fw), BF16),
        final=v((w, plan.fz, plan.fw), BF16),
        y_send=v((BACK, ny - 1, plan.group, plan.wb), BF16),
        y_recv=v((BACK, ny - 1, plan.group, plan.wb), BF16),
        target=v((BACK, plan.group, plan.wb), F32),
        back=v((BACK, plan.group, plan.wb), BF16),
        returned=v((NODE, plan.feat), BF16),
        bias_k=v((CORES, 1, plan.feat), F32),
        bias_x=v((nx, 1, plan.feat), F32),
        bias_y=v((ny, 1, plan.feat), F32),
        bias_z=v((nz, 1, plan.feat), F32),
        local_sem=DMA((w,)),
        agg_x_sem=DMA((len(FINE), nx - 1)),
        agg_y_sem=DMA((ny - 1,)),
        pg_y_sem=DMA((w, ny - 1)),
        pg_x_sem=DMA((w, nx - 1)),
        grads_z_sem=DMA((BACK,)),
        grads_x_sem=DMA((BACK, nx - 1)),
        grads_k_sem=DMA((BACK,)),
        tile_sem=DMA((w,)),
        sum_sem=DMA((w, 5)),
        gather_z_sem=DMA((w, nz)),
        gather_x_sem=DMA((w, nz, nx - 1)),
        gather_y_sem=DMA((w, nz, ny - 1)),
        corner_sem=DMA((w, ny - 1, nx - 1)),
        twin_sem=DMA(()),
        y_sem=DMA((BACK, ny - 1)),
        returned_sem=DMA((BACK,)),
        total_sem=DMA((4,)),
    )


def call(body, plan, name, identity, inputs, outputs, scratch, vmem=127 << 19):
    scratch = dict(scratch, w=pltpu.VMEM((plan.feat, plan.feat), BF16), w_sem=DMA((CHUNKS,)), sems=DMA((RING,)))
    names = list(inputs) + list(outputs) + list(scratch)
    return pl.pallas_call(
        functools.partial(body, plan, names),
        name=name,
        out_shape=[pltpu.VMEM(shape, kind) if plan.merged else shaped(shape, kind) for shape, kind, _ in outputs.values()],
        in_specs=[pl.BlockSpec(memory_space=space) for _, space in inputs.values()],
        out_specs=[pl.BlockSpec(memory_space=space) for _, _, space in outputs.values()],
        scratch_shapes=list(scratch.values()),
        compiler_params=pltpu.CompilerParams(
            collective_id=identity, has_side_effects=True, vmem_limit_bytes=vmem
        ),
    )(*[array for array, _ in inputs.values()])


def on_device(plan, features, neighbours, edge_mask, weight, bias, cotangent):
    feat, v, far = plan.feat, pltpu.VMEM, pl.ANY
    arguments = dict(
        x_far=(features, far),
        lists_far=(neighbours.T, far),
        mask_far=(edge_mask.T, far),
        w_hbm=(weight, far),
        bias_far=(bias.reshape(1, -1), far),
        cot_far=(cotangent, far),
    )
    between = dict(
        pg=((NODE, feat), BF16),
        scaled=((NODE, feat), BF16),
        agg=((feat, NODE), BF16),
        adj=((plan.columns, plan.line), BF16),
        bias_sum=((1, feat), F32),
    )
    act = dict(act=((NODE, feat), BF16, v))
    results = dict(fg=((NODE, feat), F32, v), low=((feat, feat), BF16, far), bias_grad=((1, feat), F32, v))
    if plan.merged:
        scratch = dict(forward_scratch(plan), **backward_scratch(plan))
        scratch.update({name: v(*item) for name, item in between.items()})
        activations, feature_grad, low, bias_grad = call(
            whole_kernel, plan, "layer", 0, arguments, dict(act, **results), scratch,
            46 << 20,
        )
    else:
        activations, *kept = call(
            forward_kernel, plan, "forward", 0, arguments,
            dict(act, **{name: item + (v,) for name, item in between.items()}),
            forward_scratch(plan),
        )
        feature_grad, low, bias_grad = call(
            backward_kernel, plan, "backward", 1,
            dict({name: (array, v) for name, array in zip(between, kept)}, w_hbm=(weight, far)),
            results, backward_scratch(plan),
        )
    parts = 8
    vmem, hbm = pl.BlockSpec(memory_space=v), pl.BlockSpec(memory_space=far)
    weight_grad, activations, feature_grad, bias_grad = pl.pallas_call(
        cast_kernel,
        name="cast",
        out_shape=[shaped(low.shape, F32)] + [shaped(a.shape, a.dtype) for a in (activations, feature_grad, bias_grad)],
        in_specs=[vmem] * 4,
        out_specs=[hbm] * 4,
        scratch_shapes=[v((parts, feat // parts, feat), F32), DMA((3 + parts,))],
        compiler_params=pltpu.CompilerParams(vmem_limit_bytes=30 << 20),
    )(low, activations, feature_grad, bias_grad)
    return activations, feature_grad, weight_grad, bias_grad.reshape(-1)


def solution(mesh):
    placed = (
        P(("row", "col"), None),
        P("row", "col"),
        P("row", "col"),
        P(),
        P(),
        P(("row", "col"), None),
    )

    def run(*args):
        plan = Plan(mesh, args[0].shape[1], args[1].shape[1] // mesh.shape["col"])
        return jax.shard_map(
            functools.partial(on_device, plan),
            mesh=mesh,
            in_specs=placed,
            out_specs=(P(("row", "col"), None), P(("row", "col"), None), P(), P()),
            check_vma=False,
        )(*args)

    return run
```

```python
import functools

import jax
import jax.numpy as jnp
from jax import lax
from jax.experimental import pallas as pl
from jax.experimental.pallas import tpu as pltpu
from jax.sharding import PartitionSpec as P

MESH = pl.DeviceIdType.MESH
BF16, F32, I32 = jnp.bfloat16, jnp.float32, jnp.int32
DMA = pltpu.SemaphoreType.DMA
NODE = 128
SPLIT = 4
CORES = 2
CHUNKS = 4
FINE = (4, 4, 4, 4)
WIDE = 4
BACK = 4
RING = 32


class Plan:
    def __init__(self, mesh, feat, slots):
        rows, cols = mesh.shape["row"], mesh.shape["col"]
        self.rows, self.cols, self.feat, self.slots = rows, cols, feat, slots
        self.nz, self.ny, self.nx = SPLIT, rows // SPLIT, cols // CORES
        self.slice = feat // self.nz
        self.width = self.slice // CHUNKS
        sizes = [self.slice // share for share in FINE]
        self.fine = [(sum(sizes[:i]), size) for i, size in enumerate(sizes)]
        self.columns = rows * NODE
        self.block = cols * NODE
        self.line = self.nz * self.block
        self.half = self.line // CORES
        self.third = self.half // self.nx
        self.fa, self.fp = feat // self.nx, feat // self.ny
        self.wide = min(WIDE, self.fp // NODE)
        self.fh, self.fw = self.fa // CORES, self.fp // self.wide
        self.fz = self.fh // self.nz
        self.group = self.nz * NODE
        self.wb = self.slice // BACK
        self.depth = self.ny * self.nx * NODE
        self.merged = self.columns * self.line <= 1 << 22

    def place(self):
        row, col = lax.axis_index("row"), lax.axis_index("col")
        return row // self.ny, lax.rem(row, self.ny), col // CORES, lax.rem(col, CORES)

    def device(self, z, y, x, k):
        return (z * self.ny + y, x * CORES + k)


class Refs:
    def __init__(self, names, refs):
        self.__dict__.update(zip(names, refs, strict=True))


def guarded(when, act):
    if when is None:
        act()
    else:
        pl.when(when)(act)


class Sends:
    def __init__(self, sems):
        self.sems, self.started, self.settled = sems, [], 0

    def __call__(self, src, dst, recv, device, when=None):
        self.settle(RING - 1)
        copy = pltpu.make_async_remote_copy(
            src_ref=src,
            dst_ref=dst,
            send_sem=self.sems.at[len(self.started) % RING],
            recv_sem=recv,
            device_id=device,
            device_id_type=MESH,
        )
        guarded(when, copy.start)
        self.started.append((copy, when))

    def settle(self, keep):
        while len(self.started) - self.settled > keep:
            copy, when = self.started[self.settled]
            guarded(when, copy.wait_send)
            self.settled += 1


def others(index, count):
    return [lax.rem(index + step, count) for step in range(1, count)]


def seen(i, count):
    return count - 2 - i


def at(start, size):
    return pl.ds(pl.multiple_of(start, size), size)


def span(start, size):
    return pl.ds(pl.multiple_of(start, 16), size)


def loop(count, step):
    if count <= 4:
        for i in range(count):
            step(i)
    else:

        def body(i, carry):
            step(i)
            return carry

        lax.fori_loop(0, count, body, 0)


def greet(devices):
    barrier = pltpu.get_barrier_semaphore()
    for device in devices:
        pl.semaphore_signal(barrier, inc=1, device_id=device, device_id_type=MESH)
    return lambda: pl.semaphore_wait(barrier, len(devices))


class Step:
    def __init__(self, plan, refs):
        self.plan, self.r = plan, refs
        self.z, self.y, self.x, self.k = z, y, x, k = plan.place()
        self.zs, self.ys, self.xs = others(z, plan.nz), others(y, plan.ny), others(x, plan.nx)
        self.here, self.twin = plan.device(z, y, x, k), plan.device(z, y, x, 1 - k)
        self.to_z = [plan.device(a, y, x, k) for a in self.zs]
        self.to_y = [plan.device(z, b, x, k) for b in self.ys]
        self.to_x = [plan.device(z, y, a, k) for a in self.xs]
        self.to_far = [plan.device(z, y, a, 1 - k) for a in self.xs]
        self.send = Sends(refs.sems)

    def arrived(self, ref, sem):
        pltpu.make_async_remote_copy(
            src_ref=ref, dst_ref=ref, send_sem=sem, recv_sem=sem, device_id=self.here, device_id_type=MESH
        ).wait_recv()

    def weight_copies(self):
        plan, r = self.plan, self.r
        copies = []
        for chunk in range(CHUNKS):
            for a in range(plan.nz):
                i = chunk * plan.nz + a
                copies.append(
                    pltpu.make_async_copy(
                        r.w_hbm.at[pl.ds(a * plan.slice + chunk * plan.width, plan.width)],
                        r.w.at[pl.ds(i * plan.width, plan.width)],
                        r.w_sem.at[chunk],
                    )
                )
        return copies


def of_part(task):
    def run(half, part, *where):
        if part < half.s.plan.wide:
            task(half, part, *where)

    return run


class ForwardHalf:
    def __init__(self, s):
        self.s = s
        plan, r, x, k = s.plan, s.r, s.x, s.k
        self.mates = s.to_x + [s.twin] + s.to_far
        self.mate_cols = [a * CORES + k for a in s.xs] + [x * CORES + 1 - k] + [a * CORES + 1 - k for a in s.xs]

    def block_of(self, a, b):
        return at((b * self.s.plan.nz + a) * NODE, NODE)

    def send_codes(self):
        s, r = self.s, self.s.r
        for device in s.to_z:
            s.send(r.codes, r.line_codes.at[s.z], r.codes_sem.at[s.z], device)

    def send_counts(self):
        s, r = self.s, self.s.r
        col = s.x * CORES + s.k
        for device, c in zip(self.mates, self.mate_cols):
            s.send(r.count.at[c], r.degrees.at[col], r.degree_sem, device)
        r.degrees[col] = r.count[col]

    def send_slices(self, chunk):
        s, r, plan = self.s, self.s.r, self.s.plan
        start, size = plan.fine[chunk]
        rows, mine = pl.ds(start, size), self.block_of(s.z, s.y)
        for a, device in zip(s.zs, s.to_z):
            source = r.x_t.at[span(a * plan.slice + start, size)]
            s.send(source, r.gathered.at[rows, mine], r.slice_sem.at[chunk, s.z], device)
        own = span(s.z * plan.slice + start, size)
        for i, device in enumerate(s.to_y):
            s.send(r.x_t.at[own], r.gathered.at[rows, mine], r.line_sem.at[chunk, seen(i, plan.ny)], device)
        r.gathered[rows, mine] = r.x_t[own, :]

    def build(self, i):
        s = self.s
        plan, r, nz, ny = s.plan, s.r, s.plan.nz, s.plan.ny
        a = ([s.z] + s.zs)[i]
        source = r.codes if i == 0 else r.line_codes.at[a]
        if i > 0:
            s.arrived(source, r.codes_sem.at[a])
        groups, strip = (plan.rows + 3) // 4, 32
        for c in range(plan.cols):
            columns = at((((c % CORES) * plan.nx + c // CORES) * nz + a) * NODE, NODE)
            part = source[:, c * NODE : (c + 1) * NODE]
            low = jnp.where(part >= 0, part % NODE, -1)
            high = jnp.where(part >= 0, part // NODE, -1)
            adds = [
                sum(jnp.where(high == 4 * g + j, 1 << (8 * j), 0) for j in range(4) if 4 * g + j < plan.rows)
                for g in range(groups)
            ]
            for start in range(0, NODE, strip):
                lanes = lax.broadcasted_iota(I32, (strip, NODE), 0) + start
                packed = [jnp.zeros((strip, NODE), I32) for _ in range(groups)]
                for slot in range(plan.slots):
                    hit = low[slot : slot + 1, :] == lanes
                    packed = [p + jnp.where(hit, v[slot : slot + 1, :], 0) for p, v in zip(packed, adds)]
                for row in range(plan.rows):
                    start_row = ((row % ny) * nz + row // ny) * NODE + start
                    number = (packed[row // 4] >> (8 * (row % 4))) & 255
                    r.adj[start_row : start_row + strip, columns] = number.astype(F32).astype(BF16)

    def pass_on(self, chunk, i):
        s, r, a = self.s, self.s.r, self.s.zs[i]
        piece = r.gathered.at[pl.ds(*s.plan.fine[chunk]), self.block_of(a, s.y)]
        s.arrived(piece, r.slice_sem.at[chunk, a])
        for j, device in enumerate(s.to_y):
            s.send(piece, piece, r.line_sem.at[chunk, seen(j, s.plan.ny)], device)

    def product(self, chunk, columns_from, store):
        r, plan, tile = self.s.r, self.s.plan, 256
        rows = pl.ds(*plan.fine[chunk])

        def step(i):
            columns = r.adj[:, at(columns_from + i * tile, tile)]
            store(at(i * tile, tile), jnp.dot(r.gathered[rows, :], columns, preferred_element_type=F32))

        loop(plan.half // tile, step)

    def first(self, chunk):
        s, r, plan = self.s, self.s.r, self.s.plan
        rows = pl.ds(*plan.fine[chunk])
        for i in range(plan.ny - 1):
            s.arrived(r.gathered.at[rows, pl.ds(0, plan.group)], r.line_sem.at[chunk, i])

        def to_half(cols, value):
            r.half_send[rows, cols] = value.astype(BF16)

        self.product(chunk, (1 - s.k) * plan.half, to_half)
        s.send(r.half_send.at[rows], r.half_recv.at[rows], r.half_sem.at[chunk], s.twin)

    def own(self, chunk):
        r, rows = self.s.r, pl.ds(*self.s.plan.fine[chunk])

        def to_own(cols, value):
            r.own[rows, cols] = value

        self.product(chunk, self.s.k * self.s.plan.half, to_own)

    def second(self, chunk):
        s, r, third = self.s, self.s.r, self.s.plan.third
        rows = pl.ds(*s.plan.fine[chunk])
        s.arrived(r.half_recv.at[rows], r.half_sem.at[chunk])
        for i, (a, device) in enumerate(zip(s.xs, s.to_x)):
            cols, there = at(a * third, third), seen(i, s.plan.nx)
            r.x_send[rows, cols] = (r.own[rows, cols] + r.half_recv[rows, cols].astype(F32)).astype(BF16)
            s.send(r.x_send.at[rows, cols], r.x_recv.at[there, rows], r.third_sem.at[chunk, there], device)

    def last(self, chunk):
        s, r, plan = self.s, self.s.r, self.s.plan
        start, size = plan.fine[chunk]
        rows, cols = pl.ds(start, size), at(s.x * plan.third, plan.third)
        value = r.own[rows, cols] + r.half_recv[rows, cols].astype(F32)
        for i in range(plan.nx - 1):
            s.arrived(r.x_recv.at[i, rows], r.third_sem.at[chunk, i])
            value = value + r.x_recv[i, rows].astype(F32)
        r.total[rows] = value.astype(BF16)
        there = span(s.z * plan.slice + start, size)
        for a, device in zip(s.zs, s.to_z):
            s.send(r.total.at[rows, at(a * NODE, NODE)], r.summed.at[there], r.back_sem.at[chunk], device)
        r.summed[there, :] = r.total[rows, at(s.z * NODE, NODE)]

    def scale(self):
        s, r = self.s, self.s.r
        s.arrived(r.degrees.at[pl.ds(0, s.plan.cols - 1)], r.degree_sem)
        degree = r.degrees[0]
        for c in range(1, s.plan.cols):
            degree = degree + r.degrees[c]
        self.row = 1.0 / (degree[0:1, :] + 1.0)
        self.column = jnp.broadcast_to(self.row, (NODE, NODE)).T[:, 0:1]

    def combine(self, chunk):
        s, r, plan = self.s, self.s.r, self.s.plan
        nz, fs, width = plan.nz, plan.slice, plan.width
        start, size = plan.fine[chunk]
        s.arrived(r.summed.at[pl.ds(0, (nz - 1) * size)], r.back_sem.at[chunk])
        for a in range(nz):
            rows = pl.ds(a * fs + start, size)
            value = self.row * (r.summed[rows, :].astype(F32) + 2.0 * r.x_t[rows, :].astype(F32))
            r.agg[rows, :] = value.astype(BF16)
        end = start + size
        for begin in range(end // width * width - (width if end % width == 0 else 0), end - width + 1, width):
            for a in range(nz):
                place = begin * nz + a * width
                r.agg_rows[:, place : place + width] = r.agg[a * fs + begin : a * fs + begin + width, :].T

    def await_weight(self, chunk):
        r = self.s.r
        rows = r.w.at[pl.ds(chunk * self.s.plan.slice, self.s.plan.slice)]
        pltpu.make_async_copy(rows, rows, r.w_sem.at[chunk]).wait()

    def part_of(self, chunk, cols):
        r = self.s.r
        rows = pl.ds(chunk * self.s.plan.slice, self.s.plan.slice)
        return jnp.dot(r.agg_rows[:, rows], r.w[rows, cols], preferred_element_type=F32)

    def add(self, chunk):
        r = self.s.r
        self.await_weight(chunk)

        def step(i):
            cols = at(i * 512, 512)
            if chunk == 0:
                r.preact[:, cols] = self.part_of(chunk, cols)
            else:
                r.preact[:, cols] += self.part_of(chunk, cols)

        loop(self.s.plan.feat // 512, step)

    @of_part
    def layer(self, part):
        plan = self.s.plan
        if part == 0:
            self.await_weight(CHUNKS - 1)
            self.s.r.cot_copy.wait()
        loop(plan.ny, lambda b: self.layer_columns(at(b * plan.fp + part * plan.fw, plan.fw)))

    def layer_columns(self, cols):
        r = self.s.r
        pre = r.preact[:, cols] + self.part_of(CHUNKS - 1, cols) + r.bias[:, cols]
        square = pre * pre
        slope = 0.7978845608028654
        t = jnp.tanh(slope * pre * (1.0 + 0.044715 * square))
        r.act[:, cols] = (0.5 * pre * (1.0 + t)).astype(BF16)
        grad = 0.5 * (1.0 + t) + 0.5 * pre * (1.0 - t * t) * (slope * (1.0 + 3.0 * 0.044715 * square))
        low = (r.cot[:, cols].astype(F32) * grad).astype(BF16)
        r.pg[:, cols] = low
        wide = low.astype(F32)
        r.scaled[:, cols] = (self.column * wide).astype(BF16)
        r.bias_sum[:, cols] = jnp.sum(wide, axis=0, keepdims=True)


class BackwardHalf:
    def __init__(self, s):
        self.s = s
        plan = s.plan
        self.pair = s.z + 1 - 2 * lax.rem(s.z, 2)
        self.other = plan.nz - 1 - s.z
        self.middle = lax.rem(s.z, 3) > 0
        self.end = lax.rem(s.z, 3) == 0
        self.tile = min(256, plan.fh)
        self.copies = {}

    def nodes(self, b, a):
        return at((b * self.s.plan.nx + a) * NODE, NODE)

    def line_rows(self, c, a):
        return at((c * self.s.plan.nx + a) * self.s.plan.group, self.s.plan.group)

    def wide_cols(self, b, part):
        return at(b * self.s.plan.fp + part * self.s.plan.fw, self.s.plan.fw)

    def agg_blocks(self, chunk, part):
        plan = self.s.plan
        begin, size = plan.fine[chunk]
        for i in range(plan.nz // plan.nx):
            start = i * plan.slice + begin
            yield span(part * plan.fa + start, size), pl.ds(start, size)

    def agg_send(self, chunk):
        s, r = self.s, self.s.r
        mine = self.nodes(s.y, s.x)
        for j, (a, device) in enumerate(zip(s.xs, s.to_x)):
            for source, rows in self.agg_blocks(chunk, a):
                s.send(r.agg.at[source], r.agg_all.at[rows, mine], r.agg_x_sem.at[chunk, seen(j, s.plan.nx)], device)
        for source, rows in self.agg_blocks(chunk, s.x):
            for j, device in enumerate(s.to_y):
                s.send(r.agg.at[source], r.agg_all.at[rows, mine], r.agg_y_sem.at[seen(j, s.plan.ny)], device)
            r.agg_all[rows, mine] = r.agg[source, :]

    @of_part
    def pg_x(self, part):
        s, r, fw = self.s, self.s.r, self.s.plan.fw
        mine, cols = self.nodes(s.y, s.x), pl.ds(part * fw, fw)
        for j, device in enumerate(s.to_x):
            source = r.pg.at[:, self.wide_cols(s.y, part)]
            s.send(source, r.pg_all.at[mine, cols], r.pg_x_sem.at[part, seen(j, s.plan.nx)], device)
        r.pg_all[mine, cols] = r.pg[:, self.wide_cols(s.y, part)]

    @of_part
    def pg_y(self, part):
        s, r, fw = self.s, self.s.r, self.s.plan.fw
        mine, cols = self.nodes(s.y, s.x), pl.ds(part * fw, fw)
        for j, (b, device) in enumerate(zip(s.ys, s.to_y)):
            source = r.pg.at[:, self.wide_cols(b, part)]
            s.send(source, r.pg_all.at[mine, cols], r.pg_y_sem.at[part, seen(j, s.plan.ny)], device)

    def pass_agg(self, chunk):
        s, r, plan = self.s, self.s.r, self.s.plan
        size = plan.fine[chunk][1] * (plan.nz // plan.nx)
        for i, a in enumerate(s.xs):
            s.arrived(r.agg_all.at[pl.ds(0, size), self.nodes(s.y, a)], r.agg_x_sem.at[chunk, i])
            for _, rows in self.agg_blocks(chunk, s.x):
                ref = r.agg_all.at[rows, self.nodes(s.y, a)]
                for j, device in enumerate(s.to_y):
                    s.send(ref, ref, r.agg_y_sem.at[seen(j, plan.ny)], device)

    @of_part
    def pass_pg(self, part):
        s, r, plan = self.s, self.s.r, self.s.plan
        for i, b in enumerate(s.ys):
            ref = r.pg_all.at[self.nodes(b, s.x), pl.ds(part * plan.fw, plan.fw)]
            s.arrived(ref, r.pg_y_sem.at[part, i])
            for j, device in enumerate(s.to_x):
                s.send(ref, ref, r.pg_x_sem.at[part, seen(j, plan.nx)], device)

    def await_agg(self):
        s, r = self.s, self.s.r
        for i in range(s.plan.ny - 1):
            s.arrived(r.agg_all.at[:, pl.ds(0, s.plan.nx * NODE)], r.agg_y_sem.at[i])

    def tile_product(self, part, rows_from, store):
        r, plan, tile = self.s.r, self.s.plan, self.tile
        cols = pl.ds(part * plan.fw, plan.fw)

        def step(i):
            rows = r.agg_all[at(rows_from + i * tile, tile), :]
            store(at(i * tile, tile), jnp.dot(rows, r.pg_all[:, cols], preferred_element_type=F32))

        loop(plan.fh // tile, step)

    @of_part
    def tile_part(self, part):
        s, r, plan = self.s, self.s.r, self.s.plan
        for i in range(plan.nx - 1):
            s.arrived(r.pg_all.at[pl.ds(0, plan.ny * NODE), pl.ds(part * plan.fw, plan.fw)], r.pg_x_sem.at[part, i])

        def to_half(rows, value):
            r.tile_send[part, rows, :] = value.astype(BF16)

        self.tile_product(part, (1 - s.k) * plan.fh, to_half)
        s.send(r.tile_send.at[part], r.tile_recv.at[part], r.tile_sem.at[part], s.twin)

    @of_part
    def tile_own(self, part):
        r = self.s.r

        def to_own(rows, value):
            r.tile[part, rows, :] = value

        self.tile_product(part, self.s.k * self.s.plan.fh, to_own)

    def own_part(self, part, a):
        r, fz = self.s.r, self.s.plan.fz
        rows = at(a * fz, fz)
        return r.tile[part, rows, :] + r.tile_recv[part, rows, :].astype(F32)

    @of_part
    def sum_start(self, part):
        s, r = self.s, self.s.r
        s.arrived(r.tile_recv.at[part], r.tile_sem.at[part])
        pair, other = self.pair, self.other
        targets = [other, s.plan.nz - 1 - pair, pair]

        @pl.when(self.end)
        def _():
            for i, a in enumerate(targets):
                r.sum_send[part, i] = self.own_part(part, a).astype(BF16)

        for i in range(3):
            s.send(
                r.sum_send.at[part, i], r.sum_recv.at[part, i], r.sum_sem.at[part, i],
                s.plan.device(pair, s.y, s.x, s.k), self.end,
            )

    def sum_step(self, part, i, into, slot, a, to):
        s, r = self.s, self.s.r

        @pl.when(self.middle)
        def _():
            s.arrived(r.sum_recv.at[part, i], r.sum_sem.at[part, i])
            r.sum_send[part, slot] = (self.own_part(part, a) + r.sum_recv[part, i].astype(F32)).astype(BF16)

        s.send(
            r.sum_send.at[part, slot], r.sum_recv.at[part, into], r.sum_sem.at[part, into],
            s.plan.device(to, s.y, s.x, s.k), self.middle,
        )

    @of_part
    def sum_far(self, part):
        self.sum_step(part, 0, 3, 0, self.s.plan.nz - 1 - self.pair, self.other)

    @of_part
    def sum_other(self, part):
        self.sum_step(part, 1, 4, 1, self.other, self.other)

    @of_part
    def sum_out(self, part):
        self.sum_step(part, 3, 0, 2, self.pair, self.pair)

    @of_part
    def sum_end(self, part):
        s, r = self.s, self.s.r
        mine = self.own_part(part, s.z)

        @pl.when(self.middle)
        def _():
            s.arrived(r.sum_recv.at[part, 2], r.sum_sem.at[part, 2])
            s.arrived(r.sum_recv.at[part, 4], r.sum_sem.at[part, 4])
            r.final[part] = (mine + r.sum_recv[part, 2].astype(F32) + r.sum_recv[part, 4].astype(F32)).astype(BF16)

        @pl.when(self.end)
        def _():
            s.arrived(r.sum_recv.at[part, 0], r.sum_sem.at[part, 0])
            r.final[part] = (mine + r.sum_recv[part, 0].astype(F32)).astype(BF16)

        copy = pltpu.make_async_copy(r.final.at[part], self.piece(part, s.z, s.y, s.x), r.local_sem.at[part])
        copy.start()
        self.copies[part] = copy
        self.spread(r.final.at[part], part, s.z)
        self.along(r.final.at[part], part, s.z, self.pair, None)
        self.along(r.final.at[part], part, s.z, self.other, self.middle)

    def block(self, part, a_y, a_x):
        plan = self.s.plan
        return self.s.r.low.at[at(a_x * plan.fa + self.s.k * plan.fh, plan.fh), self.wide_cols(a_y, part)]

    def piece(self, part, a_z, a_y, a_x):
        plan = self.s.plan
        rows = at(a_x * plan.fa + self.s.k * plan.fh + a_z * plan.fz, plan.fz)
        return self.s.r.low.at[rows, self.wide_cols(a_y, part)]

    def along(self, source, part, a_z, to, when):
        s = self.s
        device = s.plan.device(to, s.y, s.x, s.k)
        s.send(source, self.piece(part, a_z, s.y, s.x), s.r.gather_z_sem.at[part, a_z], device, when)

    def spread(self, source, part, a_z):
        s, r = self.s, self.s.r
        target = self.piece(part, a_z, s.y, s.x)
        for i, device in enumerate(s.to_x):
            s.send(source, target, r.gather_x_sem.at[part, a_z, seen(i, s.plan.nx)], device)
        for i, device in enumerate(s.to_y):
            s.send(source, target, r.gather_y_sem.at[part, a_z, seen(i, s.plan.ny)], device)

    def line_order(self):
        return [self.s.z, self.pair, 2 - self.s.z // 2, 3 - 3 * (self.s.z // 2)]

    @of_part
    def gather_line(self, part, i):
        s = self.s
        a_z = self.line_order()[i]
        piece = self.piece(part, a_z, s.y, s.x)
        s.arrived(piece, s.r.gather_z_sem.at[part, a_z])
        self.along(piece, part, a_z, self.other if i == 1 else self.pair, self.middle)
        self.spread(piece, part, a_z)

    @of_part
    def gather_x(self, part, i):
        s, r, plan = self.s, self.s.r, self.s.plan
        a_z = self.line_order()[i]
        for j, a_x in enumerate(s.xs):
            piece = self.piece(part, a_z, s.y, a_x)
            s.arrived(piece, r.gather_x_sem.at[part, a_z, j])
            for m, device in enumerate(s.to_y):
                s.send(piece, piece, r.corner_sem.at[part, seen(m, plan.ny), j], device, lax.rem(a_z, 2) == 0)

    @of_part
    def gather_y(self, part, i):
        s, r, plan = self.s, self.s.r, self.s.plan
        a_z = self.line_order()[i]
        for j, a_y in enumerate(s.ys):
            piece = self.piece(part, a_z, a_y, s.x)
            s.arrived(piece, r.gather_y_sem.at[part, a_z, j])
            for m, device in enumerate(s.to_x):
                s.send(piece, piece, r.corner_sem.at[part, j, seen(m, plan.nx)], device, lax.rem(a_z, 2) == 1)

    def to_twin(self, part, a_y, a_x):
        s = self.s
        block = self.block(part, a_y, a_x)
        s.send(block, block, s.r.twin_sem, s.twin)

    @of_part
    def twin_own(self, part):
        self.copies[part].wait()
        self.to_twin(part, self.s.y, self.s.x)

    @of_part
    def twin_x(self, part):
        for a_x in self.s.xs:
            self.to_twin(part, self.s.y, a_x)

    @of_part
    def twin_y(self, part):
        for a_y in self.s.ys:
            self.to_twin(part, a_y, self.s.x)

    @of_part
    def twin_corner(self, part):
        s = self.s
        for j, a_y in enumerate(s.ys):
            for i, a_x in enumerate(s.xs):
                s.arrived(self.block(part, a_y, a_x), s.r.corner_sem.at[part, j, i])
                self.to_twin(part, a_y, a_x)

    def gather_twin(self):
        s, feat = self.s, self.s.plan.feat
        s.send.settle(16)
        s.arrived(s.r.low.at[pl.ds(0, feat // CORES)], s.r.twin_sem)

    def grads_start(self, part):
        s, r, plan = self.s, self.s.r, self.s.plan
        fs, wb = plan.slice, plan.wb
        mine, cols = at(((s.k * plan.nx + s.x) * plan.nz + s.z) * NODE, NODE), pl.ds(part * wb, wb)
        for a, device in zip(s.zs, s.to_z):
            s.send(r.scaled.at[:, at(a * fs + part * wb, wb)], r.grads.at[mine, cols], r.grads_z_sem.at[part], device)
        r.grads[mine, cols] = r.scaled[:, at(s.z * fs + part * wb, wb)]

    def grads_x(self, part):
        s, r, plan = self.s, self.s.r, self.s.plan
        cols = pl.ds(part * plan.wb, plan.wb)
        s.arrived(r.grads.at[pl.ds(0, (plan.nz - 1) * NODE), cols], r.grads_z_sem.at[part])
        ref = r.grads.at[self.line_rows(s.k, s.x), cols]
        for i, device in enumerate(s.to_x):
            s.send(ref, ref, r.grads_x_sem.at[part, seen(i, plan.nx)], device)
        s.send(ref, ref, r.grads_k_sem.at[part], s.twin)

    def grads_twin(self, part):
        s, r, plan = self.s, self.s.r, self.s.plan
        for i, a in enumerate(s.xs):
            ref = r.grads.at[self.line_rows(s.k, a), pl.ds(part * plan.wb, plan.wb)]
            s.arrived(ref, r.grads_x_sem.at[part, i])
            s.send(ref, ref, r.grads_k_sem.at[part], s.twin)

    def target_product(self, part, b, store):
        r, plan = self.s.r, self.s.plan
        cols = pl.ds(part * plan.wb, plan.wb)

        def step(i):
            rows = r.adj[at(b * plan.group + i * 256, 256), :]
            store(at(i * 256, 256), jnp.dot(rows, r.grads[:, cols], preferred_element_type=F32))

        loop(plan.group // 256, step)

    def target(self, part):
        s, r, plan = self.s, self.s.r, self.s.plan
        s.arrived(r.grads.at[pl.ds(0, plan.line // CORES), pl.ds(part * plan.wb, plan.wb)], r.grads_k_sem.at[part])
        for i, (b, device) in enumerate(zip(s.ys, s.to_y)):

            def to_y(rows, value):
                r.y_send[part, i, rows, :] = value.astype(BF16)

            self.target_product(part, b, to_y)
            there = seen(i, plan.ny)
            s.send(r.y_send.at[part, i], r.y_recv.at[part, there], r.y_sem.at[part, there], device)

    def target_own(self, part):
        r = self.s.r

        def to_target(rows, value):
            r.target[part, rows, :] = value

        self.target_product(part, self.s.y, to_target)

    def back(self, part):
        s, r, plan = self.s, self.s.r, self.s.plan
        value = r.target[part]
        for i in range(plan.ny - 1):
            s.arrived(r.y_recv.at[part, i], r.y_sem.at[part, i])
            value = value + r.y_recv[part, i].astype(F32)
        r.back[part] = value.astype(BF16)
        cols = at(s.z * plan.slice + part * plan.wb, plan.wb)
        for a, device in zip(s.zs, s.to_z):
            s.send(r.back.at[part, at(a * NODE, NODE)], r.returned.at[:, cols], r.returned_sem.at[part], device)
        r.returned[:, cols] = r.back[part, at(s.z * NODE, NODE), :]

    def through(self):
        s, r, plan = self.s, self.s.r, self.s.plan
        for part in range(BACK):
            s.arrived(r.returned.at[:, pl.ds(0, (plan.nz - 1) * plan.wb)], r.returned_sem.at[part])
        r.returned[...] = (r.returned[...].astype(F32) + 2.0 * r.scaled[...].astype(F32)).astype(BF16)
        for chunk in range(CHUNKS):
            rows = pl.ds(chunk * plan.slice, plan.slice)
            value = lax.dot_general(
                r.returned[...], r.w[rows, :], (((1,), (1,)), ((), ())), preferred_element_type=F32
            )
            for a in range(plan.nz):
                cols = pl.ds(a * plan.slice + chunk * plan.width, plan.width)
                r.fg[:, cols] = value[:, a * plan.width : (a + 1) * plan.width]

    def bias_start(self):
        s, r = self.s, self.s.r
        s.send(r.bias_sum, r.bias_k.at[s.k], r.total_sem.at[0], s.twin)
        r.bias_k[s.k] = r.bias_sum[...]

    def bias_stage(self, stage):
        s, r, plan = self.s, self.s.r, self.s.plan
        ref, count = ((r.bias_k, CORES), (r.bias_x, plan.nx), (r.bias_y, plan.ny), (r.bias_z, plan.nz))[stage]
        s.arrived(ref.at[pl.ds(0, count - 1)], r.total_sem.at[stage])
        value = ref[0]
        for a in range(1, count):
            value = value + ref[a]
        if stage == 3:
            r.bias_grad[...] = value
            return
        ref, index, devices = ((r.bias_x, s.x, s.to_x), (r.bias_y, s.y, s.to_y), (r.bias_z, s.z, s.to_z))[stage]
        ref[index] = value
        for device in devices:
            s.send(ref.at[index], ref.at[index], r.total_sem.at[stage + 1], device)


class Skip:
    def __getattr__(self, name):
        return lambda *where: None


def schedule(f, b):
    f.send_slices(0)
    f.build(0)
    f.send_codes()
    f.pass_on(0, 1)
    f.send_slices(1)
    f.pass_on(0, 0)
    f.pass_on(0, 2)
    f.build(2)
    f.send_slices(2)
    f.build(1)
    f.send_slices(3)
    f.pass_on(1, 0)
    f.pass_on(1, 2)
    f.pass_on(1, 1)
    f.build(3)
    f.first(0)
    f.send_counts()
    f.pass_on(2, 2)
    f.own(0)
    f.pass_on(2, 0)
    f.second(0)
    f.pass_on(2, 1)
    f.first(1)
    f.pass_on(3, 2)
    f.pass_on(3, 0)
    f.pass_on(3, 1)
    f.own(1)
    f.second(1)
    f.first(2)
    f.own(2)
    f.last(0)
    f.first(3)
    f.second(2)
    f.own(3)
    f.last(1)
    f.second(3)
    f.scale()
    f.combine(0)
    f.last(2)
    b.agg_send(0)
    f.add(0)
    f.combine(1)
    b.agg_send(1)
    f.last(3)
    b.pass_agg(0)
    f.add(1)
    f.combine(2)
    b.agg_send(2)
    f.add(2)
    b.pass_agg(1)
    f.combine(3)
    b.agg_send(3)
    f.layer(0)
    f.layer(1)
    f.layer(2)
    b.pg_x(1)
    f.layer(3)
    b.grads_start(3)
    b.pg_y(0)
    b.pass_agg(2)
    b.pg_x(2)
    b.pass_agg(3)
    b.pg_x(0)
    b.grads_start(0)
    b.grads_start(2)
    b.pass_pg(0)
    b.pg_y(1)
    b.pg_y(2)
    b.grads_x(3)
    b.await_agg()
    b.grads_start(1)
    b.bias_start()
    b.tile_part(0)
    b.pass_pg(1)
    b.pg_y(3)
    b.grads_x(0)
    b.tile_own(0)
    b.sum_start(0)
    b.grads_twin(3)
    b.pass_pg(2)
    b.grads_x(2)
    b.tile_part(1)
    b.tile_own(1)
    b.bias_stage(0)
    b.pg_x(3)
    b.target(3)
    b.sum_far(0)
    b.sum_start(1)
    b.grads_twin(0)
    b.sum_other(0)
    b.tile_part(2)
    b.target(0)
    b.sum_out(0)
    b.sum_far(1)
    b.pass_pg(3)
    b.tile_own(2)
    b.sum_start(2)
    b.bias_stage(1)
    b.grads_twin(2)
    b.sum_other(1)
    b.grads_x(1)
    b.sum_end(0)
    b.target(2)
    b.sum_out(1)
    b.tile_part(3)
    b.sum_far(2)
    b.tile_own(3)
    b.sum_other(2)
    b.sum_end(1)
    b.gather_y(0, 0)
    b.grads_twin(1)
    b.target_own(0)
    b.sum_start(3)
    b.gather_line(0, 1)
    b.sum_out(2)
    b.target(1)
    b.sum_end(2)
    b.gather_line(1, 1)
    b.gather_line(0, 2)
    b.gather_line(0, 3)
    b.twin_own(0)
    b.gather_x(0, 1)
    b.sum_far(3)
    b.sum_other(3)
    b.gather_x(0, 0)
    b.gather_line(2, 2)
    b.gather_line(1, 2)
    b.gather_line(2, 1)
    b.gather_line(1, 3)
    b.sum_out(3)
    b.gather_x(0, 3)
    b.sum_end(3)
    b.gather_x(2, 0)
    b.target_own(3)
    b.gather_y(0, 2)
    b.gather_line(2, 3)
    b.gather_y(0, 3)
    b.target_own(2)
    b.gather_line(3, 2)
    b.back(0)
    b.gather_y(0, 1)
    b.target_own(1)
    b.gather_x(1, 1)
    b.back(3)
    b.twin_own(1)
    b.gather_x(0, 2)
    b.bias_stage(2)
    b.gather_line(3, 1)
    b.gather_y(1, 3)
    b.gather_y(1, 0)
    b.back(1)
    b.gather_line(3, 3)
    b.gather_x(2, 1)
    b.gather_x(1, 0)
    b.gather_y(1, 1)
    b.twin_y(0)
    b.gather_y(1, 2)
    b.gather_x(1, 2)
    b.back(2)
    b.gather_x(3, 1)
    b.twin_corner(0)
    b.gather_y(3, 1)
    b.gather_x(1, 3)
    b.gather_y(2, 1)
    b.gather_x(2, 2)
    b.gather_y(3, 0)
    b.bias_stage(3)
    b.gather_x(2, 3)
    b.twin_x(0)
    b.twin_y(1)
    b.twin_own(2)
    b.gather_y(2, 2)
    b.gather_x(3, 0)
    b.gather_x(3, 2)
    b.gather_y(2, 3)
    b.gather_y(2, 0)
    b.gather_x(3, 3)
    b.twin_y(2)
    b.gather_y(3, 2)
    b.gather_y(3, 3)
    b.twin_y(3)
    b.twin_own(3)
    b.twin_x(2)
    b.twin_x(3)
    b.twin_x(1)
    b.through()
    b.twin_corner(2)
    b.twin_corner(1)
    b.twin_corner(3)
    b.gather_twin()


def fetch(s, names):
    copies = [pltpu.make_async_copy(getattr(s.r, name + "_far"), getattr(s.r, name), getattr(s.r, name + "_sem")) for name in names]
    for copy in copies:
        copy.start()
    return copies


def prepare(s):
    plan, r = s.plan, s.r
    for c in range(plan.cols):
        cols = pl.ds(c * NODE, NODE)
        part = jnp.where(r.mask[:, cols] > 0, r.lists[:, cols], -1)
        r.codes[:, cols] = part
        ones = jnp.sum(jnp.where(part >= 0, 1.0, 0.0), axis=0, keepdims=True)
        r.count[c] = jnp.broadcast_to(ones, (8, NODE))
    for start in range(0, plan.feat, NODE):
        r.x_t[start : start + NODE, :] = r.x[:, start : start + NODE].T


def opening(s):
    met = greet(s.to_z + s.to_y + s.to_x + [s.twin] + s.to_far)
    lists, mask, x, bias, s.r.cot_copy = fetch(s, ("lists", "mask", "x", "bias", "cot"))
    for copy in s.weight_copies():
        copy.start()
    for copy in (lists, mask, x, bias):
        copy.wait()
    prepare(s)
    met()


def whole_kernel(plan, names, *refs):
    s = Step(plan, Refs(names, refs))
    opening(s)
    schedule(ForwardHalf(s), BackwardHalf(s))
    s.send.settle(0)


def forward_kernel(plan, names, *refs):
    s = Step(plan, Refs(names, refs))
    opening(s)
    schedule(ForwardHalf(s), Skip())
    s.send.settle(0)


def backward_kernel(plan, names, *refs):
    s = Step(plan, Refs(names, refs))
    for copy in s.weight_copies():
        copy.start()
    greet(s.to_z + s.to_y + s.to_x + [s.twin])()
    half = BackwardHalf(s)
    for chunk in range(CHUNKS):
        rows = s.r.w.at[pl.ds(chunk * plan.slice, plan.slice)]
        pltpu.make_async_copy(rows, rows, s.r.w_sem.at[chunk]).wait()
    schedule(Skip(), half)
    s.send.settle(0)


def cast_kernel(low, act_in, fg_in, bias_in, out, act_out, fg_out, bias_out, wide, sems):
    copies = [
        pltpu.make_async_copy(src, dst, sems.at[i])
        for i, (src, dst) in enumerate(((act_in, act_out), (fg_in, fg_out), (bias_in, bias_out)))
    ]
    for copy in copies:
        copy.start()
    count, rows, _ = wide.shape
    for i in range(count):
        wide[i] = low[i * rows : (i + 1) * rows, :].astype(F32)
        copy = pltpu.make_async_copy(wide.at[i], out.at[pl.ds(i * rows, rows)], sems.at[3 + i])
        copy.start()
        copies.append(copy)
    for copy in copies:
        copy.wait()


def shaped(*items):
    return jax.ShapeDtypeStruct(*items)


def forward_scratch(plan):
    c, nz, fs = len(FINE), plan.nz, plan.slice
    v = pltpu.VMEM
    return dict(
        x=v((NODE, plan.feat), BF16),
        x_sem=DMA(()),
        lists=v((plan.slots, plan.block), I32),
        lists_sem=DMA(()),
        mask=v((plan.slots, plan.block), I32),
        mask_sem=DMA(()),
        bias=v((1, plan.feat), F32),
        bias_sem=DMA(()),
        cot=v((NODE, plan.feat), BF16),
        codes=v((plan.slots, plan.block), I32),
        x_t=v((plan.feat, NODE), BF16),
        gathered=v((plan.slice, plan.columns), BF16),
        line_codes=v((nz, plan.slots, plan.block), I32),
        count=v((plan.cols, 8, NODE), F32),
        degrees=v((plan.cols, 8, NODE), F32),
        half_send=v((fs, plan.half), BF16),
        half_recv=v((fs, plan.half), BF16),
        x_send=v((fs, plan.half), BF16),
        x_recv=v((plan.nx - 1, fs, plan.third), BF16),
        own=v((fs, plan.half), F32),
        total=v((fs, plan.third), BF16),
        summed=v((plan.feat, NODE), BF16),
        agg_rows=v((NODE, plan.feat), BF16),
        preact=v((NODE, plan.feat), F32),
        cot_sem=DMA(()),
        codes_sem=DMA((nz,)),
        degree_sem=DMA(()),
        slice_sem=DMA((c, nz)),
        line_sem=DMA((c, plan.ny - 1)),
        half_sem=DMA((c,)),
        third_sem=DMA((c, plan.nx - 1)),
        back_sem=DMA((c,)),
    )


def backward_scratch(plan):
    nz, ny, nx, w = plan.nz, plan.ny, plan.nx, plan.wide
    v = pltpu.VMEM
    return dict(
        agg_all=v((plan.fa, plan.depth), BF16),
        pg_all=v((plan.depth, plan.fp), BF16),
        grads=v((plan.line, plan.slice), BF16),
        tile_send=v((w, plan.fh, plan.fw), BF16),
        tile_recv=v((w, plan.fh, plan.fw), BF16),
        tile=v((w, plan.fh, plan.fw), F32),
        sum_send=v((w, 3, plan.fz, plan.fw), BF16),
        sum_recv=v((w, 5, plan.fz, plan.fw), BF16),
        final=v((w, plan.fz, plan.fw), BF16),
        y_send=v((BACK, ny - 1, plan.group, plan.wb), BF16),
        y_recv=v((BACK, ny - 1, plan.group, plan.wb), BF16),
        target=v((BACK, plan.group, plan.wb), F32),
        back=v((BACK, plan.group, plan.wb), BF16),
        returned=v((NODE, plan.feat), BF16),
        bias_k=v((CORES, 1, plan.feat), F32),
        bias_x=v((nx, 1, plan.feat), F32),
        bias_y=v((ny, 1, plan.feat), F32),
        bias_z=v((nz, 1, plan.feat), F32),
        local_sem=DMA((w,)),
        agg_x_sem=DMA((len(FINE), nx - 1)),
        agg_y_sem=DMA((ny - 1,)),
        pg_y_sem=DMA((w, ny - 1)),
        pg_x_sem=DMA((w, nx - 1)),
        grads_z_sem=DMA((BACK,)),
        grads_x_sem=DMA((BACK, nx - 1)),
        grads_k_sem=DMA((BACK,)),
        tile_sem=DMA((w,)),
        sum_sem=DMA((w, 5)),
        gather_z_sem=DMA((w, nz)),
        gather_x_sem=DMA((w, nz, nx - 1)),
        gather_y_sem=DMA((w, nz, ny - 1)),
        corner_sem=DMA((w, ny - 1, nx - 1)),
        twin_sem=DMA(()),
        y_sem=DMA((BACK, ny - 1)),
        returned_sem=DMA((BACK,)),
        total_sem=DMA((4,)),
    )


def call(body, plan, name, identity, inputs, outputs, scratch, vmem=127 << 19):
    scratch = dict(scratch, w=pltpu.VMEM((plan.feat, plan.feat), BF16), w_sem=DMA((CHUNKS,)), sems=DMA((RING,)))
    names = list(inputs) + list(outputs) + list(scratch)
    return pl.pallas_call(
        functools.partial(body, plan, names),
        name=name,
        out_shape=[pltpu.VMEM(shape, kind) if plan.merged else shaped(shape, kind) for shape, kind, _ in outputs.values()],
        in_specs=[pl.BlockSpec(memory_space=space) for _, space in inputs.values()],
        out_specs=[pl.BlockSpec(memory_space=space) for _, _, space in outputs.values()],
        scratch_shapes=list(scratch.values()),
        compiler_params=pltpu.CompilerParams(
            collective_id=identity, has_side_effects=True, vmem_limit_bytes=vmem
        ),
    )(*[array for array, _ in inputs.values()])


def on_device(plan, features, neighbours, edge_mask, weight, bias, cotangent):
    feat, v, far = plan.feat, pltpu.VMEM, pl.ANY
    arguments = dict(
        x_far=(features, far),
        lists_far=(neighbours.T, far),
        mask_far=(edge_mask.T, far),
        w_hbm=(weight, far),
        bias_far=(bias.reshape(1, -1), far),
        cot_far=(cotangent, far),
    )
    between = dict(
        pg=((NODE, feat), BF16),
        scaled=((NODE, feat), BF16),
        agg=((feat, NODE), BF16),
        adj=((plan.columns, plan.line), BF16),
        bias_sum=((1, feat), F32),
    )
    act = dict(act=((NODE, feat), BF16, v))
    results = dict(fg=((NODE, feat), F32, v), low=((feat, feat), BF16, far), bias_grad=((1, feat), F32, v))
    if plan.merged:
        scratch = dict(forward_scratch(plan), **backward_scratch(plan))
        scratch.update({name: v(*item) for name, item in between.items()})
        activations, feature_grad, low, bias_grad = call(
            whole_kernel, plan, "layer", 0, arguments, dict(act, **results), scratch,
            46 << 20,
        )
    else:
        activations, *kept = call(
            forward_kernel, plan, "forward", 0, arguments,
            dict(act, **{name: item + (v,) for name, item in between.items()}),
            forward_scratch(plan),
        )
        feature_grad, low, bias_grad = call(
            backward_kernel, plan, "backward", 1,
            dict({name: (array, v) for name, array in zip(between, kept)}, w_hbm=(weight, far)),
            results, backward_scratch(plan),
        )
    parts = 8
    vmem, hbm = pl.BlockSpec(memory_space=v), pl.BlockSpec(memory_space=far)
    weight_grad, activations, feature_grad, bias_grad = pl.pallas_call(
        cast_kernel,
        name="cast",
        out_shape=[shaped(low.shape, F32)] + [shaped(a.shape, a.dtype) for a in (activations, feature_grad, bias_grad)],
        in_specs=[vmem] * 4,
        out_specs=[hbm] * 4,
        scratch_shapes=[v((parts, feat // parts, feat), F32), DMA((3 + parts,))],
        compiler_params=pltpu.CompilerParams(vmem_limit_bytes=30 << 20),
    )(low, activations, feature_grad, bias_grad)
    return activations, feature_grad, weight_grad, bias_grad.reshape(-1)


def solution(mesh):
    placed = (
        P(("row", "col"), None),
        P("row", "col"),
        P("row", "col"),
        P(),
        P(),
        P(("row", "col"), None),
    )

    def run(*args):
        plan = Plan(mesh, args[0].shape[1], args[1].shape[1] // mesh.shape["col"])
        return jax.shard_map(
            functools.partial(on_device, plan),
            mesh=mesh,
            in_specs=placed,
            out_specs=(P(("row", "col"), None), P(("row", "col"), None), P(), P()),
            check_vma=False,
        )(*args)

    return run
```

```python
import functools

import jax
import jax.numpy as jnp
from jax import lax
from jax.experimental import pallas as pl
from jax.experimental.pallas import tpu as pltpu
from jax.sharding import PartitionSpec as P

MESH = pl.DeviceIdType.MESH
BF16, F32, I32 = jnp.bfloat16, jnp.float32, jnp.int32
DMA = pltpu.SemaphoreType.DMA
NODE = 128
SPLIT = 4
CORES = 2
CHUNKS = 4
FINE = (4, 4, 4, 4)
WIDE = 4
BACK = 4
RING = 32


class Plan:
    def __init__(self, mesh, feat, slots):
        rows, cols = mesh.shape["row"], mesh.shape["col"]
        self.rows, self.cols, self.feat, self.slots = rows, cols, feat, slots
        self.nz, self.ny, self.nx = SPLIT, rows // SPLIT, cols // CORES
        self.slice = feat // self.nz
        self.width = self.slice // CHUNKS
        sizes = [self.slice // share for share in FINE]
        self.fine = [(sum(sizes[:i]), size) for i, size in enumerate(sizes)]
        self.columns = rows * NODE
        self.block = cols * NODE
        self.line = self.nz * self.block
        self.half = self.line // CORES
        self.third = self.half // self.nx
        self.fa, self.fp = feat // self.nx, feat // self.ny
        self.wide = min(WIDE, self.fp // NODE)
        self.fh, self.fw = self.fa // CORES, self.fp // self.wide
        self.fz = self.fh // self.nz
        self.group = self.nz * NODE
        self.wb = self.slice // BACK
        self.depth = self.ny * self.nx * NODE
        self.merged = self.columns * self.line <= 1 << 22

    def place(self):
        row, col = lax.axis_index("row"), lax.axis_index("col")
        return row // self.ny, lax.rem(row, self.ny), col // CORES, lax.rem(col, CORES)

    def device(self, z, y, x, k):
        return (z * self.ny + y, x * CORES + k)


class Refs:
    def __init__(self, names, refs):
        self.__dict__.update(zip(names, refs, strict=True))


def guarded(when, act):
    if when is None:
        act()
    else:
        pl.when(when)(act)


class Sends:
    def __init__(self, sems):
        self.sems, self.started, self.settled = sems, [], 0

    def __call__(self, src, dst, recv, device, when=None):
        self.settle(RING - 1)
        copy = pltpu.make_async_remote_copy(
            src_ref=src,
            dst_ref=dst,
            send_sem=self.sems.at[len(self.started) % RING],
            recv_sem=recv,
            device_id=device,
            device_id_type=MESH,
        )
        guarded(when, copy.start)
        self.started.append((copy, when))

    def settle(self, keep):
        while len(self.started) - self.settled > keep:
            copy, when = self.started[self.settled]
            guarded(when, copy.wait_send)
            self.settled += 1


def others(index, count):
    return [lax.rem(index + step, count) for step in range(1, count)]


def seen(i, count):
    return count - 2 - i


def at(start, size):
    return pl.ds(pl.multiple_of(start, size), size)


def span(start, size):
    return pl.ds(pl.multiple_of(start, 16), size)


def loop(count, step):
    if count <= 4:
        for i in range(count):
            step(i)
    else:

        def body(i, carry):
            step(i)
            return carry

        lax.fori_loop(0, count, body, 0)


def greet(devices):
    barrier = pltpu.get_barrier_semaphore()
    for device in devices:
        pl.semaphore_signal(barrier, inc=1, device_id=device, device_id_type=MESH)
    return lambda: pl.semaphore_wait(barrier, len(devices))


class Step:
    def __init__(self, plan, refs):
        self.plan, self.r = plan, refs
        self.z, self.y, self.x, self.k = z, y, x, k = plan.place()
        self.zs, self.ys, self.xs = others(z, plan.nz), others(y, plan.ny), others(x, plan.nx)
        self.here, self.twin = plan.device(z, y, x, k), plan.device(z, y, x, 1 - k)
        self.to_z = [plan.device(a, y, x, k) for a in self.zs]
        self.to_y = [plan.device(z, b, x, k) for b in self.ys]
        self.to_x = [plan.device(z, y, a, k) for a in self.xs]
        self.to_far = [plan.device(z, y, a, 1 - k) for a in self.xs]
        self.send = Sends(refs.sems)

    def arrived(self, ref, sem):
        pltpu.make_async_remote_copy(
            src_ref=ref, dst_ref=ref, send_sem=sem, recv_sem=sem, device_id=self.here, device_id_type=MESH
        ).wait_recv()

    def weight_copies(self):
        plan, r = self.plan, self.r
        copies = []
        for chunk in range(CHUNKS):
            for a in range(plan.nz):
                i = chunk * plan.nz + a
                copies.append(
                    pltpu.make_async_copy(
                        r.w_hbm.at[pl.ds(a * plan.slice + chunk * plan.width, plan.width)],
                        r.w.at[pl.ds(i * plan.width, plan.width)],
                        r.w_sem.at[chunk],
                    )
                )
        return copies


def of_part(task):
    def run(half, part, *where):
        if part < half.s.plan.wide:
            task(half, part, *where)

    return run


class ForwardHalf:
    def __init__(self, s):
        self.s = s
        plan, r, x, k = s.plan, s.r, s.x, s.k
        self.mates = s.to_x + [s.twin] + s.to_far
        self.mate_cols = [a * CORES + k for a in s.xs] + [x * CORES + 1 - k] + [a * CORES + 1 - k for a in s.xs]

    def block_of(self, a, b):
        return at((b * self.s.plan.nz + a) * NODE, NODE)

    def send_codes(self):
        s, r = self.s, self.s.r
        for device in s.to_z:
            s.send(r.codes, r.line_codes.at[s.z], r.codes_sem.at[s.z], device)

    def send_counts(self):
        s, r = self.s, self.s.r
        col = s.x * CORES + s.k
        for device, c in zip(self.mates, self.mate_cols):
            s.send(r.count.at[c], r.degrees.at[col], r.degree_sem, device)
        r.degrees[col] = r.count[col]

    def send_slices(self, chunk):
        s, r, plan = self.s, self.s.r, self.s.plan
        start, size = plan.fine[chunk]
        rows, mine = pl.ds(start, size), self.block_of(s.z, s.y)
        for a, device in zip(s.zs, s.to_z):
            source = r.x_t.at[span(a * plan.slice + start, size)]
            s.send(source, r.gathered.at[rows, mine], r.slice_sem.at[chunk, s.z], device)
        own = span(s.z * plan.slice + start, size)
        for i, device in enumerate(s.to_y):
            s.send(r.x_t.at[own], r.gathered.at[rows, mine], r.line_sem.at[chunk, seen(i, plan.ny)], device)
        r.gathered[rows, mine] = r.x_t[own, :]

    def build(self, i):
        s = self.s
        plan, r, nz, ny = s.plan, s.r, s.plan.nz, s.plan.ny
        a = ([s.z] + s.zs)[i]
        source = r.codes if i == 0 else r.line_codes.at[a]
        if i > 0:
            s.arrived(source, r.codes_sem.at[a])
        groups, strip = (plan.rows + 3) // 4, 32
        for c in range(plan.cols):
            columns = at((((c % CORES) * plan.nx + c // CORES) * nz + a) * NODE, NODE)
            part = source[:, c * NODE : (c + 1) * NODE]
            low = jnp.where(part >= 0, part % NODE, -1)
            high = jnp.where(part >= 0, part // NODE, -1)
            adds = [
                sum(jnp.where(high == 4 * g + j, 1 << (8 * j), 0) for j in range(4) if 4 * g + j < plan.rows)
                for g in range(groups)
            ]
            for start in range(0, NODE, strip):
                lanes = lax.broadcasted_iota(I32, (strip, NODE), 0) + start
                packed = [jnp.zeros((strip, NODE), I32) for _ in range(groups)]
                for slot in range(plan.slots):
                    hit = low[slot : slot + 1, :] == lanes
                    packed = [p + jnp.where(hit, v[slot : slot + 1, :], 0) for p, v in zip(packed, adds)]
                for row in range(plan.rows):
                    start_row = ((row % ny) * nz + row // ny) * NODE + start
                    number = (packed[row // 4] >> (8 * (row % 4))) & 255
                    r.adj[start_row : start_row + strip, columns] = number.astype(F32).astype(BF16)

    def pass_on(self, chunk, i):
        s, r, a = self.s, self.s.r, self.s.zs[i]
        piece = r.gathered.at[pl.ds(*s.plan.fine[chunk]), self.block_of(a, s.y)]
        s.arrived(piece, r.slice_sem.at[chunk, a])
        for j, device in enumerate(s.to_y):
            s.send(piece, piece, r.line_sem.at[chunk, seen(j, s.plan.ny)], device)

    def product(self, chunk, columns_from, store):
        r, plan, tile = self.s.r, self.s.plan, 256
        rows = pl.ds(*plan.fine[chunk])

        def step(i):
            columns = r.adj[:, at(columns_from + i * tile, tile)]
            store(at(i * tile, tile), jnp.dot(r.gathered[rows, :], columns, preferred_element_type=F32))

        loop(plan.half // tile, step)

    def first(self, chunk):
        s, r, plan = self.s, self.s.r, self.s.plan
        rows = pl.ds(*plan.fine[chunk])
        for i in range(plan.ny - 1):
            s.arrived(r.gathered.at[rows, pl.ds(0, plan.group)], r.line_sem.at[chunk, i])

        def to_half(cols, value):
            r.half_send[rows, cols] = value.astype(BF16)

        self.product(chunk, (1 - s.k) * plan.half, to_half)
        s.send(r.half_send.at[rows], r.half_recv.at[rows], r.half_sem.at[chunk], s.twin)

    def own(self, chunk):
        r, rows = self.s.r, pl.ds(*self.s.plan.fine[chunk])

        def to_own(cols, value):
            r.own[rows, cols] = value

        self.product(chunk, self.s.k * self.s.plan.half, to_own)

    def second(self, chunk):
        s, r, third = self.s, self.s.r, self.s.plan.third
        rows = pl.ds(*s.plan.fine[chunk])
        s.arrived(r.half_recv.at[rows], r.half_sem.at[chunk])
        for i, (a, device) in enumerate(zip(s.xs, s.to_x)):
            cols, there = at(a * third, third), seen(i, s.plan.nx)
            r.x_send[rows, cols] = (r.own[rows, cols] + r.half_recv[rows, cols].astype(F32)).astype(BF16)
            s.send(r.x_send.at[rows, cols], r.x_recv.at[there, rows], r.third_sem.at[chunk, there], device)

    def last(self, chunk):
        s, r, plan = self.s, self.s.r, self.s.plan
        start, size = plan.fine[chunk]
        rows, cols = pl.ds(start, size), at(s.x * plan.third, plan.third)
        value = r.own[rows, cols] + r.half_recv[rows, cols].astype(F32)
        for i in range(plan.nx - 1):
            s.arrived(r.x_recv.at[i, rows], r.third_sem.at[chunk, i])
            value = value + r.x_recv[i, rows].astype(F32)
        r.total[rows] = value.astype(BF16)
        there = span(s.z * plan.slice + start, size)
        for a, device in zip(s.zs, s.to_z):
            s.send(r.total.at[rows, at(a * NODE, NODE)], r.summed.at[there], r.back_sem.at[chunk], device)
        r.summed[there, :] = r.total[rows, at(s.z * NODE, NODE)]

    def scale(self):
        s, r = self.s, self.s.r
        s.arrived(r.degrees.at[pl.ds(0, s.plan.cols - 1)], r.degree_sem)
        degree = r.degrees[0]
        for c in range(1, s.plan.cols):
            degree = degree + r.degrees[c]
        self.row = 1.0 / (degree[0:1, :] + 1.0)
        self.column = jnp.broadcast_to(self.row, (NODE, NODE)).T[:, 0:1]

    def combine(self, chunk):
        s, r, plan = self.s, self.s.r, self.s.plan
        nz, fs, width = plan.nz, plan.slice, plan.width
        start, size = plan.fine[chunk]
        s.arrived(r.summed.at[pl.ds(0, (nz - 1) * size)], r.back_sem.at[chunk])
        for a in range(nz):
            rows = pl.ds(a * fs + start, size)
            value = self.row * (r.summed[rows, :].astype(F32) + 2.0 * r.x_t[rows, :].astype(F32))
            r.agg[rows, :] = value.astype(BF16)
        end = start + size
        for begin in range(end // width * width - (width if end % width == 0 else 0), end - width + 1, width):
            for a in range(nz):
                place = begin * nz + a * width
                r.agg_rows[:, place : place + width] = r.agg[a * fs + begin : a * fs + begin + width, :].T

    def await_weight(self, chunk):
        r = self.s.r
        rows = r.w.at[pl.ds(chunk * self.s.plan.slice, self.s.plan.slice)]
        pltpu.make_async_copy(rows, rows, r.w_sem.at[chunk]).wait()

    def part_of(self, chunk, cols):
        r = self.s.r
        rows = pl.ds(chunk * self.s.plan.slice, self.s.plan.slice)
        return jnp.dot(r.agg_rows[:, rows], r.w[rows, cols], preferred_element_type=F32)

    def add(self, chunk):
        r = self.s.r
        self.await_weight(chunk)

        def step(i):
            cols = at(i * 512, 512)
            if chunk == 0:
                r.preact[:, cols] = self.part_of(chunk, cols)
            else:
                r.preact[:, cols] += self.part_of(chunk, cols)

        loop(self.s.plan.feat // 512, step)

    @of_part
    def layer(self, part):
        plan = self.s.plan
        if part == 0:
            self.await_weight(CHUNKS - 1)
            self.s.r.cot_copy.wait()
        loop(plan.ny, lambda b: self.layer_columns(at(b * plan.fp + part * plan.fw, plan.fw)))

    def layer_columns(self, cols):
        r = self.s.r
        pre = r.preact[:, cols] + self.part_of(CHUNKS - 1, cols) + r.bias[:, cols]
        square = pre * pre
        slope = 0.7978845608028654
        t = jnp.tanh(slope * pre * (1.0 + 0.044715 * square))
        r.act[:, cols] = (0.5 * pre * (1.0 + t)).astype(BF16)
        grad = 0.5 * (1.0 + t) + 0.5 * pre * (1.0 - t * t) * (slope * (1.0 + 3.0 * 0.044715 * square))
        low = (r.cot[:, cols].astype(F32) * grad).astype(BF16)
        r.pg[:, cols] = low
        wide = low.astype(F32)
        r.scaled[:, cols] = (self.column * wide).astype(BF16)
        r.bias_sum[:, cols] = jnp.sum(wide, axis=0, keepdims=True)


class BackwardHalf:
    def __init__(self, s):
        self.s = s
        plan = s.plan
        self.pair = s.z + 1 - 2 * lax.rem(s.z, 2)
        self.other = plan.nz - 1 - s.z
        self.middle = lax.rem(s.z, 3) > 0
        self.end = lax.rem(s.z, 3) == 0
        self.tile = min(256, plan.fh)
        self.copies = {}

    def nodes(self, b, a):
        return at((b * self.s.plan.nx + a) * NODE, NODE)

    def line_rows(self, c, a):
        return at((c * self.s.plan.nx + a) * self.s.plan.group, self.s.plan.group)

    def wide_cols(self, b, part):
        return at(b * self.s.plan.fp + part * self.s.plan.fw, self.s.plan.fw)

    def agg_blocks(self, chunk, part):
        plan = self.s.plan
        begin, size = plan.fine[chunk]
        for i in range(plan.nz // plan.nx):
            start = i * plan.slice + begin
            yield span(part * plan.fa + start, size), pl.ds(start, size)

    def agg_send(self, chunk):
        s, r = self.s, self.s.r
        mine = self.nodes(s.y, s.x)
        for j, (a, device) in enumerate(zip(s.xs, s.to_x)):
            for source, rows in self.agg_blocks(chunk, a):
                s.send(r.agg.at[source], r.agg_all.at[rows, mine], r.agg_x_sem.at[chunk, seen(j, s.plan.nx)], device)
        for source, rows in self.agg_blocks(chunk, s.x):
            for j, device in enumerate(s.to_y):
                s.send(r.agg.at[source], r.agg_all.at[rows, mine], r.agg_y_sem.at[seen(j, s.plan.ny)], device)
            r.agg_all[rows, mine] = r.agg[source, :]

    @of_part
    def pg_x(self, part):
        s, r, fw = self.s, self.s.r, self.s.plan.fw
        mine, cols = self.nodes(s.y, s.x), pl.ds(part * fw, fw)
        for j, device in enumerate(s.to_x):
            source = r.pg.at[:, self.wide_cols(s.y, part)]
            s.send(source, r.pg_all.at[mine, cols], r.pg_x_sem.at[part, seen(j, s.plan.nx)], device)
        r.pg_all[mine, cols] = r.pg[:, self.wide_cols(s.y, part)]

    @of_part
    def pg_y(self, part):
        s, r, fw = self.s, self.s.r, self.s.plan.fw
        mine, cols = self.nodes(s.y, s.x), pl.ds(part * fw, fw)
        for j, (b, device) in enumerate(zip(s.ys, s.to_y)):
            source = r.pg.at[:, self.wide_cols(b, part)]
            s.send(source, r.pg_all.at[mine, cols], r.pg_y_sem.at[part, seen(j, s.plan.ny)], device)

    def pass_agg(self, chunk):
        s, r, plan = self.s, self.s.r, self.s.plan
        size = plan.fine[chunk][1] * (plan.nz // plan.nx)
        for i, a in enumerate(s.xs):
            s.arrived(r.agg_all.at[pl.ds(0, size), self.nodes(s.y, a)], r.agg_x_sem.at[chunk, i])
            for _, rows in self.agg_blocks(chunk, s.x):
                ref = r.agg_all.at[rows, self.nodes(s.y, a)]
                for j, device in enumerate(s.to_y):
                    s.send(ref, ref, r.agg_y_sem.at[seen(j, plan.ny)], device)

    @of_part
    def pass_pg(self, part):
        s, r, plan = self.s, self.s.r, self.s.plan
        for i, b in enumerate(s.ys):
            ref = r.pg_all.at[self.nodes(b, s.x), pl.ds(part * plan.fw, plan.fw)]
            s.arrived(ref, r.pg_y_sem.at[part, i])
            for j, device in enumerate(s.to_x):
                s.send(ref, ref, r.pg_x_sem.at[part, seen(j, plan.nx)], device)

    def await_agg(self):
        s, r = self.s, self.s.r
        for i in range(s.plan.ny - 1):
            s.arrived(r.agg_all.at[:, pl.ds(0, s.plan.nx * NODE)], r.agg_y_sem.at[i])

    def tile_product(self, part, rows_from, store):
        r, plan, tile = self.s.r, self.s.plan, self.tile
        cols = pl.ds(part * plan.fw, plan.fw)

        def step(i):
            rows = r.agg_all[at(rows_from + i * tile, tile), :]
            store(at(i * tile, tile), jnp.dot(rows, r.pg_all[:, cols], preferred_element_type=F32))

        loop(plan.fh // tile, step)

    @of_part
    def tile_part(self, part):
        s, r, plan = self.s, self.s.r, self.s.plan
        for i in range(plan.nx - 1):
            s.arrived(r.pg_all.at[pl.ds(0, plan.ny * NODE), pl.ds(part * plan.fw, plan.fw)], r.pg_x_sem.at[part, i])

        def to_half(rows, value):
            r.tile_send[part, rows, :] = value.astype(BF16)

        self.tile_product(part, (1 - s.k) * plan.fh, to_half)
        s.send(r.tile_send.at[part], r.tile_recv.at[part], r.tile_sem.at[part], s.twin)

    @of_part
    def tile_own(self, part):
        r = self.s.r

        def to_own(rows, value):
            r.tile[part, rows, :] = value

        self.tile_product(part, self.s.k * self.s.plan.fh, to_own)

    def own_part(self, part, a):
        r, fz = self.s.r, self.s.plan.fz
        rows = at(a * fz, fz)
        return r.tile[part, rows, :] + r.tile_recv[part, rows, :].astype(F32)

    @of_part
    def sum_start(self, part):
        s, r = self.s, self.s.r
        s.arrived(r.tile_recv.at[part], r.tile_sem.at[part])
        pair, other = self.pair, self.other
        targets = [other, s.plan.nz - 1 - pair, pair]

        @pl.when(self.end)
        def _():
            for i, a in enumerate(targets):
                r.sum_send[part, i] = self.own_part(part, a).astype(BF16)

        for i in range(3):
            s.send(
                r.sum_send.at[part, i], r.sum_recv.at[part, i], r.sum_sem.at[part, i],
                s.plan.device(pair, s.y, s.x, s.k), self.end,
            )

    def sum_step(self, part, i, into, slot, a, to):
        s, r = self.s, self.s.r

        @pl.when(self.middle)
        def _():
            s.arrived(r.sum_recv.at[part, i], r.sum_sem.at[part, i])
            r.sum_send[part, slot] = (self.own_part(part, a) + r.sum_recv[part, i].astype(F32)).astype(BF16)

        s.send(
            r.sum_send.at[part, slot], r.sum_recv.at[part, into], r.sum_sem.at[part, into],
            s.plan.device(to, s.y, s.x, s.k), self.middle,
        )

    @of_part
    def sum_far(self, part):
        self.sum_step(part, 0, 3, 0, self.s.plan.nz - 1 - self.pair, self.other)

    @of_part
    def sum_other(self, part):
        self.sum_step(part, 1, 4, 1, self.other, self.other)

    @of_part
    def sum_out(self, part):
        self.sum_step(part, 3, 0, 2, self.pair, self.pair)

    @of_part
    def sum_end(self, part):
        s, r = self.s, self.s.r
        mine = self.own_part(part, s.z)

        @pl.when(self.middle)
        def _():
            s.arrived(r.sum_recv.at[part, 2], r.sum_sem.at[part, 2])
            s.arrived(r.sum_recv.at[part, 4], r.sum_sem.at[part, 4])
            r.final[part] = (mine + r.sum_recv[part, 2].astype(F32) + r.sum_recv[part, 4].astype(F32)).astype(BF16)

        @pl.when(self.end)
        def _():
            s.arrived(r.sum_recv.at[part, 0], r.sum_sem.at[part, 0])
            r.final[part] = (mine + r.sum_recv[part, 0].astype(F32)).astype(BF16)

        copy = pltpu.make_async_copy(r.final.at[part], self.piece(part, s.z, s.y, s.x), r.local_sem.at[part])
        copy.start()
        self.copies[part] = copy
        self.spread(r.final.at[part], part, s.z)
        self.along(r.final.at[part], part, s.z, self.pair, None)
        self.along(r.final.at[part], part, s.z, self.other, self.middle)

    def block(self, part, a_y, a_x):
        plan = self.s.plan
        return self.s.r.low.at[at(a_x * plan.fa + self.s.k * plan.fh, plan.fh), self.wide_cols(a_y, part)]

    def piece(self, part, a_z, a_y, a_x):
        plan = self.s.plan
        rows = at(a_x * plan.fa + self.s.k * plan.fh + a_z * plan.fz, plan.fz)
        return self.s.r.low.at[rows, self.wide_cols(a_y, part)]

    def along(self, source, part, a_z, to, when):
        s = self.s
        device = s.plan.device(to, s.y, s.x, s.k)
        s.send(source, self.piece(part, a_z, s.y, s.x), s.r.gather_z_sem.at[part, a_z], device, when)

    def spread(self, source, part, a_z):
        s, r = self.s, self.s.r
        target = self.piece(part, a_z, s.y, s.x)
        for i, device in enumerate(s.to_x):
            s.send(source, target, r.gather_x_sem.at[part, a_z, seen(i, s.plan.nx)], device)
        for i, device in enumerate(s.to_y):
            s.send(source, target, r.gather_y_sem.at[part, a_z, seen(i, s.plan.ny)], device)

    def line_order(self):
        return [self.s.z, self.pair, 2 - self.s.z // 2, 3 - 3 * (self.s.z // 2)]

    @of_part
    def gather_line(self, part, i):
        s = self.s
        a_z = self.line_order()[i]
        piece = self.piece(part, a_z, s.y, s.x)
        s.arrived(piece, s.r.gather_z_sem.at[part, a_z])
        self.along(piece, part, a_z, self.other if i == 1 else self.pair, self.middle)
        self.spread(piece, part, a_z)

    @of_part
    def gather_x(self, part, i):
        s, r, plan = self.s, self.s.r, self.s.plan
        a_z = self.line_order()[i]
        for j, a_x in enumerate(s.xs):
            piece = self.piece(part, a_z, s.y, a_x)
            s.arrived(piece, r.gather_x_sem.at[part, a_z, j])
            for m, device in enumerate(s.to_y):
                s.send(piece, piece, r.corner_sem.at[part, seen(m, plan.ny), j], device, lax.rem(a_z, 2) == 0)

    @of_part
    def gather_y(self, part, i):
        s, r, plan = self.s, self.s.r, self.s.plan
        a_z = self.line_order()[i]
        for j, a_y in enumerate(s.ys):
            piece = self.piece(part, a_z, a_y, s.x)
            s.arrived(piece, r.gather_y_sem.at[part, a_z, j])
            for m, device in enumerate(s.to_x):
                s.send(piece, piece, r.corner_sem.at[part, j, seen(m, plan.nx)], device, lax.rem(a_z, 2) == 1)

    def to_twin(self, part, a_y, a_x):
        s = self.s
        block = self.block(part, a_y, a_x)
        s.send(block, block, s.r.twin_sem, s.twin)

    @of_part
    def twin_own(self, part):
        self.copies[part].wait()
        self.to_twin(part, self.s.y, self.s.x)

    @of_part
    def twin_x(self, part):
        for a_x in self.s.xs:
            self.to_twin(part, self.s.y, a_x)

    @of_part
    def twin_y(self, part):
        for a_y in self.s.ys:
            self.to_twin(part, a_y, self.s.x)

    @of_part
    def twin_corner(self, part):
        s = self.s
        for j, a_y in enumerate(s.ys):
            for i, a_x in enumerate(s.xs):
                s.arrived(self.block(part, a_y, a_x), s.r.corner_sem.at[part, j, i])
                self.to_twin(part, a_y, a_x)

    def gather_twin(self):
        s, feat = self.s, self.s.plan.feat
        s.send.settle(16)
        s.arrived(s.r.low.at[pl.ds(0, feat // CORES)], s.r.twin_sem)

    def grads_start(self, part):
        s, r, plan = self.s, self.s.r, self.s.plan
        fs, wb = plan.slice, plan.wb
        mine, cols = at(((s.k * plan.nx + s.x) * plan.nz + s.z) * NODE, NODE), pl.ds(part * wb, wb)
        for a, device in zip(s.zs, s.to_z):
            s.send(r.scaled.at[:, at(a * fs + part * wb, wb)], r.grads.at[mine, cols], r.grads_z_sem.at[part], device)
        r.grads[mine, cols] = r.scaled[:, at(s.z * fs + part * wb, wb)]

    def grads_x(self, part):
        s, r, plan = self.s, self.s.r, self.s.plan
        cols = pl.ds(part * plan.wb, plan.wb)
        s.arrived(r.grads.at[pl.ds(0, (plan.nz - 1) * NODE), cols], r.grads_z_sem.at[part])
        ref = r.grads.at[self.line_rows(s.k, s.x), cols]
        for i, device in enumerate(s.to_x):
            s.send(ref, ref, r.grads_x_sem.at[part, seen(i, plan.nx)], device)
        s.send(ref, ref, r.grads_k_sem.at[part], s.twin)

    def grads_twin(self, part):
        s, r, plan = self.s, self.s.r, self.s.plan
        for i, a in enumerate(s.xs):
            ref = r.grads.at[self.line_rows(s.k, a), pl.ds(part * plan.wb, plan.wb)]
            s.arrived(ref, r.grads_x_sem.at[part, i])
            s.send(ref, ref, r.grads_k_sem.at[part], s.twin)

    def target_product(self, part, b, store):
        r, plan = self.s.r, self.s.plan
        cols = pl.ds(part * plan.wb, plan.wb)

        def step(i):
            rows = r.adj[at(b * plan.group + i * 256, 256), :]
            store(at(i * 256, 256), jnp.dot(rows, r.grads[:, cols], preferred_element_type=F32))

        loop(plan.group // 256, step)

    def target(self, part):
        s, r, plan = self.s, self.s.r, self.s.plan
        s.arrived(r.grads.at[pl.ds(0, plan.line // CORES), pl.ds(part * plan.wb, plan.wb)], r.grads_k_sem.at[part])
        for i, (b, device) in enumerate(zip(s.ys, s.to_y)):

            def to_y(rows, value):
                r.y_send[part, i, rows, :] = value.astype(BF16)

            self.target_product(part, b, to_y)
            there = seen(i, plan.ny)
            s.send(r.y_send.at[part, i], r.y_recv.at[part, there], r.y_sem.at[part, there], device)

    def target_own(self, part):
        r = self.s.r

        def to_target(rows, value):
            r.target[part, rows, :] = value

        self.target_product(part, self.s.y, to_target)

    def back(self, part):
        s, r, plan = self.s, self.s.r, self.s.plan
        value = r.target[part]
        for i in range(plan.ny - 1):
            s.arrived(r.y_recv.at[part, i], r.y_sem.at[part, i])
            value = value + r.y_recv[part, i].astype(F32)
        r.back[part] = value.astype(BF16)
        cols = at(s.z * plan.slice + part * plan.wb, plan.wb)
        for a, device in zip(s.zs, s.to_z):
            s.send(r.back.at[part, at(a * NODE, NODE)], r.returned.at[:, cols], r.returned_sem.at[part], device)
        r.returned[:, cols] = r.back[part, at(s.z * NODE, NODE), :]

    def through(self):
        s, r, plan = self.s, self.s.r, self.s.plan
        for part in range(BACK):
            s.arrived(r.returned.at[:, pl.ds(0, (plan.nz - 1) * plan.wb)], r.returned_sem.at[part])
        r.returned[...] = (r.returned[...].astype(F32) + 2.0 * r.scaled[...].astype(F32)).astype(BF16)
        for chunk in range(CHUNKS):
            rows = pl.ds(chunk * plan.slice, plan.slice)
            value = lax.dot_general(
                r.returned[...], r.w[rows, :], (((1,), (1,)), ((), ())), preferred_element_type=F32
            )
            for a in range(plan.nz):
                cols = pl.ds(a * plan.slice + chunk * plan.width, plan.width)
                r.fg[:, cols] = value[:, a * plan.width : (a + 1) * plan.width]

    def bias_start(self):
        s, r = self.s, self.s.r
        s.send(r.bias_sum, r.bias_k.at[s.k], r.total_sem.at[0], s.twin)
        r.bias_k[s.k] = r.bias_sum[...]

    def bias_stage(self, stage):
        s, r, plan = self.s, self.s.r, self.s.plan
        ref, count = ((r.bias_k, CORES), (r.bias_x, plan.nx), (r.bias_y, plan.ny), (r.bias_z, plan.nz))[stage]
        s.arrived(ref.at[pl.ds(0, count - 1)], r.total_sem.at[stage])
        value = ref[0]
        for a in range(1, count):
            value = value + ref[a]
        if stage == 3:
            r.bias_grad[...] = value
            return
        ref, index, devices = ((r.bias_x, s.x, s.to_x), (r.bias_y, s.y, s.to_y), (r.bias_z, s.z, s.to_z))[stage]
        ref[index] = value
        for device in devices:
            s.send(ref.at[index], ref.at[index], r.total_sem.at[stage + 1], device)


class Skip:
    def __getattr__(self, name):
        return lambda *where: None


def schedule(f, b):
    f.send_slices(0)
    f.build(0)
    f.send_codes()
    f.pass_on(0, 1)
    f.send_slices(1)
    f.pass_on(0, 0)
    f.pass_on(0, 2)
    f.build(2)
    f.send_slices(2)
    f.build(1)
    f.send_slices(3)
    f.pass_on(1, 0)
    f.pass_on(1, 2)
    f.pass_on(1, 1)
    f.build(3)
    f.first(0)
    f.send_counts()
    f.pass_on(2, 2)
    f.own(0)
    f.pass_on(2, 0)
    f.second(0)
    f.pass_on(2, 1)
    f.first(1)
    f.pass_on(3, 2)
    f.pass_on(3, 0)
    f.pass_on(3, 1)
    f.own(1)
    f.second(1)
    f.first(2)
    f.own(2)
    f.last(0)
    f.first(3)
    f.second(2)
    f.own(3)
    f.last(1)
    f.second(3)
    f.scale()
    f.combine(0)
    f.last(2)
    b.agg_send(0)
    f.add(0)
    f.combine(1)
    b.agg_send(1)
    f.last(3)
    b.pass_agg(0)
    f.add(1)
    f.combine(2)
    b.agg_send(2)
    f.add(2)
    b.pass_agg(1)
    f.combine(3)
    b.agg_send(3)
    f.layer(0)
    f.layer(1)
    f.layer(2)
    b.pg_x(1)
    f.layer(3)
    b.grads_start(3)
    b.pg_y(0)
    b.pass_agg(2)
    b.pg_x(2)
    b.pass_agg(3)
    b.pg_x(0)
    b.grads_start(0)
    b.grads_start(2)
    b.pass_pg(0)
    b.pg_y(1)
    b.pg_y(2)
    b.grads_x(3)
    b.await_agg()
    b.grads_start(1)
    b.bias_start()
    b.tile_part(0)
    b.pass_pg(1)
    b.pg_y(3)
    b.grads_x(0)
    b.tile_own(0)
    b.sum_start(0)
    b.grads_twin(3)
    b.pass_pg(2)
    b.grads_x(2)
    b.tile_part(1)
    b.tile_own(1)
    b.bias_stage(0)
    b.pg_x(3)
    b.target(3)
    b.sum_far(0)
    b.sum_start(1)
    b.grads_twin(0)
    b.sum_other(0)
    b.tile_part(2)
    b.target(0)
    b.sum_out(0)
    b.sum_far(1)
    b.pass_pg(3)
    b.tile_own(2)
    b.sum_start(2)
    b.bias_stage(1)
    b.grads_twin(2)
    b.sum_other(1)
    b.grads_x(1)
    b.sum_end(0)
    b.target(2)
    b.sum_out(1)
    b.tile_part(3)
    b.sum_far(2)
    b.tile_own(3)
    b.sum_other(2)
    b.sum_end(1)
    b.gather_y(0, 0)
    b.grads_twin(1)
    b.target_own(0)
    b.sum_start(3)
    b.gather_line(0, 1)
    b.sum_out(2)
    b.target(1)
    b.sum_end(2)
    b.gather_line(1, 1)
    b.gather_line(0, 2)
    b.gather_line(0, 3)
    b.twin_own(0)
    b.gather_x(0, 1)
    b.sum_far(3)
    b.sum_other(3)
    b.gather_x(0, 0)
    b.gather_line(2, 2)
    b.gather_line(1, 2)
    b.gather_line(2, 1)
    b.gather_line(1, 3)
    b.sum_out(3)
    b.gather_x(0, 3)
    b.sum_end(3)
    b.gather_x(2, 0)
    b.target_own(3)
    b.gather_y(0, 2)
    b.gather_line(2, 3)
    b.gather_y(0, 3)
    b.target_own(2)
    b.gather_line(3, 2)
    b.back(0)
    b.gather_y(0, 1)
    b.target_own(1)
    b.gather_x(1, 1)
    b.back(3)
    b.twin_own(1)
    b.gather_x(0, 2)
    b.bias_stage(2)
    b.gather_line(3, 1)
    b.gather_y(1, 3)
    b.gather_y(1, 0)
    b.back(1)
    b.gather_line(3, 3)
    b.gather_x(2, 1)
    b.gather_x(1, 0)
    b.gather_y(1, 1)
    b.twin_y(0)
    b.gather_y(1, 2)
    b.gather_x(1, 2)
    b.back(2)
    b.gather_x(3, 1)
    b.twin_corner(0)
    b.gather_y(3, 1)
    b.gather_x(1, 3)
    b.gather_y(2, 1)
    b.gather_x(2, 2)
    b.gather_y(3, 0)
    b.bias_stage(3)
    b.gather_x(2, 3)
    b.twin_x(0)
    b.twin_y(1)
    b.twin_own(2)
    b.gather_y(2, 2)
    b.gather_x(3, 0)
    b.gather_x(3, 2)
    b.gather_y(2, 3)
    b.gather_y(2, 0)
    b.gather_x(3, 3)
    b.twin_y(2)
    b.gather_y(3, 2)
    b.gather_y(3, 3)
    b.twin_y(3)
    b.twin_own(3)
    b.twin_x(2)
    b.twin_x(3)
    b.twin_x(1)
    b.through()
    b.twin_corner(2)
    b.twin_corner(1)
    b.twin_corner(3)
    b.gather_twin()


def fetch(s, names):
    copies = [pltpu.make_async_copy(getattr(s.r, name + "_far"), getattr(s.r, name), getattr(s.r, name + "_sem")) for name in names]
    for copy in copies:
        copy.start()
    return copies


def prepare(s):
    plan, r = s.plan, s.r
    for c in range(plan.cols):
        cols = pl.ds(c * NODE, NODE)
        part = jnp.where(r.mask[:, cols] > 0, r.lists[:, cols], -1)
        r.codes[:, cols] = part
        ones = jnp.sum(jnp.where(part >= 0, 1.0, 0.0), axis=0, keepdims=True)
        r.count[c] = jnp.broadcast_to(ones, (8, NODE))
    for start in range(0, plan.feat, NODE):
        r.x_t[start : start + NODE, :] = r.x[:, start : start + NODE].T


def opening(s):
    met = greet(s.to_z + s.to_y + s.to_x + [s.twin] + s.to_far)
    lists, mask, x, bias, s.r.cot_copy = fetch(s, ("lists", "mask", "x", "bias", "cot"))
    for copy in s.weight_copies():
        copy.start()
    for copy in (lists, mask, x, bias):
        copy.wait()
    prepare(s)
    met()


def whole_kernel(plan, names, *refs):
    s = Step(plan, Refs(names, refs))
    opening(s)
    schedule(ForwardHalf(s), BackwardHalf(s))
    s.send.settle(0)


def forward_kernel(plan, names, *refs):
    s = Step(plan, Refs(names, refs))
    opening(s)
    schedule(ForwardHalf(s), Skip())
    s.send.settle(0)


def backward_kernel(plan, names, *refs):
    s = Step(plan, Refs(names, refs))
    for copy in s.weight_copies():
        copy.start()
    greet(s.to_z + s.to_y + s.to_x + [s.twin])()
    half = BackwardHalf(s)
    for chunk in range(CHUNKS):
        rows = s.r.w.at[pl.ds(chunk * plan.slice, plan.slice)]
        pltpu.make_async_copy(rows, rows, s.r.w_sem.at[chunk]).wait()
    schedule(Skip(), half)
    s.send.settle(0)


def cast_kernel(low, act_in, fg_in, bias_in, out, act_out, fg_out, bias_out, wide, sems):
    copies = [
        pltpu.make_async_copy(src, dst, sems.at[i])
        for i, (src, dst) in enumerate(((act_in, act_out), (fg_in, fg_out), (bias_in, bias_out)))
    ]
    for copy in copies:
        copy.start()
    count, rows, _ = wide.shape
    for i in range(count):
        wide[i] = low[i * rows : (i + 1) * rows, :].astype(F32)
        copy = pltpu.make_async_copy(wide.at[i], out.at[pl.ds(i * rows, rows)], sems.at[3 + i])
        copy.start()
        copies.append(copy)
    for copy in copies:
        copy.wait()


def shaped(*items):
    return jax.ShapeDtypeStruct(*items)


def forward_scratch(plan):
    c, nz, fs = len(FINE), plan.nz, plan.slice
    v = pltpu.VMEM
    return dict(
        x=v((NODE, plan.feat), BF16),
        x_sem=DMA(()),
        lists=v((plan.slots, plan.block), I32),
        lists_sem=DMA(()),
        mask=v((plan.slots, plan.block), I32),
        mask_sem=DMA(()),
        bias=v((1, plan.feat), F32),
        bias_sem=DMA(()),
        cot=v((NODE, plan.feat), BF16),
        codes=v((plan.slots, plan.block), I32),
        x_t=v((plan.feat, NODE), BF16),
        gathered=v((plan.slice, plan.columns), BF16),
        line_codes=v((nz, plan.slots, plan.block), I32),
        count=v((plan.cols, 8, NODE), F32),
        degrees=v((plan.cols, 8, NODE), F32),
        half_send=v((fs, plan.half), BF16),
        half_recv=v((fs, plan.half), BF16),
        x_send=v((fs, plan.half), BF16),
        x_recv=v((plan.nx - 1, fs, plan.third), BF16),
        own=v((fs, plan.half), F32),
        total=v((fs, plan.third), BF16),
        summed=v((plan.feat, NODE), BF16),
        agg_rows=v((NODE, plan.feat), BF16),
        preact=v((NODE, plan.feat), F32),
        cot_sem=DMA(()),
        codes_sem=DMA((nz,)),
        degree_sem=DMA(()),
        slice_sem=DMA((c, nz)),
        line_sem=DMA((c, plan.ny - 1)),
        half_sem=DMA((c,)),
        third_sem=DMA((c, plan.nx - 1)),
        back_sem=DMA((c,)),
    )


def backward_scratch(plan):
    nz, ny, nx, w = plan.nz, plan.ny, plan.nx, plan.wide
    v = pltpu.VMEM
    return dict(
        agg_all=v((plan.fa, plan.depth), BF16),
        pg_all=v((plan.depth, plan.fp), BF16),
        grads=v((plan.line, plan.slice), BF16),
        tile_send=v((w, plan.fh, plan.fw), BF16),
        tile_recv=v((w, plan.fh, plan.fw), BF16),
        tile=v((w, plan.fh, plan.fw), F32),
        sum_send=v((w, 3, plan.fz, plan.fw), BF16),
        sum_recv=v((w, 5, plan.fz, plan.fw), BF16),
        final=v((w, plan.fz, plan.fw), BF16),
        y_send=v((BACK, ny - 1, plan.group, plan.wb), BF16),
        y_recv=v((BACK, ny - 1, plan.group, plan.wb), BF16),
        target=v((BACK, plan.group, plan.wb), F32),
        back=v((BACK, plan.group, plan.wb), BF16),
        returned=v((NODE, plan.feat), BF16),
        bias_k=v((CORES, 1, plan.feat), F32),
        bias_x=v((nx, 1, plan.feat), F32),
        bias_y=v((ny, 1, plan.feat), F32),
        bias_z=v((nz, 1, plan.feat), F32),
        local_sem=DMA((w,)),
        agg_x_sem=DMA((len(FINE), nx - 1)),
        agg_y_sem=DMA((ny - 1,)),
        pg_y_sem=DMA((w, ny - 1)),
        pg_x_sem=DMA((w, nx - 1)),
        grads_z_sem=DMA((BACK,)),
        grads_x_sem=DMA((BACK, nx - 1)),
        grads_k_sem=DMA((BACK,)),
        tile_sem=DMA((w,)),
        sum_sem=DMA((w, 5)),
        gather_z_sem=DMA((w, nz)),
        gather_x_sem=DMA((w, nz, nx - 1)),
        gather_y_sem=DMA((w, nz, ny - 1)),
        corner_sem=DMA((w, ny - 1, nx - 1)),
        twin_sem=DMA(()),
        y_sem=DMA((BACK, ny - 1)),
        returned_sem=DMA((BACK,)),
        total_sem=DMA((4,)),
    )


def call(body, plan, name, identity, inputs, outputs, scratch, vmem=127 << 19):
    scratch = dict(scratch, w=pltpu.VMEM((plan.feat, plan.feat), BF16), w_sem=DMA((CHUNKS,)), sems=DMA((RING,)))
    names = list(inputs) + list(outputs) + list(scratch)
    return pl.pallas_call(
        functools.partial(body, plan, names),
        name=name,
        out_shape=[pltpu.VMEM(shape, kind) if plan.merged else shaped(shape, kind) for shape, kind, _ in outputs.values()],
        in_specs=[pl.BlockSpec(memory_space=space) for _, space in inputs.values()],
        out_specs=[pl.BlockSpec(memory_space=space) for _, _, space in outputs.values()],
        scratch_shapes=list(scratch.values()),
        compiler_params=pltpu.CompilerParams(
            collective_id=identity, has_side_effects=True, vmem_limit_bytes=vmem
        ),
    )(*[array for array, _ in inputs.values()])


def on_device(plan, features, neighbours, edge_mask, weight, bias, cotangent):
    feat, v, far = plan.feat, pltpu.VMEM, pl.ANY
    arguments = dict(
        x_far=(features, far),
        lists_far=(neighbours.T, far),
        mask_far=(edge_mask.T, far),
        w_hbm=(weight, far),
        bias_far=(bias.reshape(1, -1), far),
        cot_far=(cotangent, far),
    )
    between = dict(
        pg=((NODE, feat), BF16),
        scaled=((NODE, feat), BF16),
        agg=((feat, NODE), BF16),
        adj=((plan.columns, plan.line), BF16),
        bias_sum=((1, feat), F32),
    )
    act = dict(act=((NODE, feat), BF16, v))
    results = dict(fg=((NODE, feat), F32, v), low=((feat, feat), BF16, far), bias_grad=((1, feat), F32, v))
    if plan.merged:
        scratch = dict(forward_scratch(plan), **backward_scratch(plan))
        scratch.update({name: v(*item) for name, item in between.items()})
        activations, feature_grad, low, bias_grad = call(
            whole_kernel, plan, "layer", 0, arguments, dict(act, **results), scratch,
            46 << 20,
        )
    else:
        activations, *kept = call(
            forward_kernel, plan, "forward", 0, arguments,
            dict(act, **{name: item + (v,) for name, item in between.items()}),
            forward_scratch(plan),
        )
        feature_grad, low, bias_grad = call(
            backward_kernel, plan, "backward", 1,
            dict({name: (array, v) for name, array in zip(between, kept)}, w_hbm=(weight, far)),
            results, backward_scratch(plan),
        )
    parts = 16
    vmem, hbm = pl.BlockSpec(memory_space=v), pl.BlockSpec(memory_space=far)
    weight_grad, activations, feature_grad, bias_grad = pl.pallas_call(
        cast_kernel,
        name="cast",
        out_shape=[shaped(low.shape, F32)] + [shaped(a.shape, a.dtype) for a in (activations, feature_grad, bias_grad)],
        in_specs=[vmem] * 4,
        out_specs=[hbm] * 4,
        scratch_shapes=[v((parts, feat // parts, feat), F32), DMA((3 + parts,))],
        compiler_params=pltpu.CompilerParams(vmem_limit_bytes=30 << 20),
    )(low, activations, feature_grad, bias_grad)
    return activations, feature_grad, weight_grad, bias_grad.reshape(-1)


def solution(mesh):
    placed = (
        P(("row", "col"), None),
        P("row", "col"),
        P("row", "col"),
        P(),
        P(),
        P(("row", "col"), None),
    )

    def run(*args):
        plan = Plan(mesh, args[0].shape[1], args[1].shape[1] // mesh.shape["col"])
        return jax.shard_map(
            functools.partial(on_device, plan),
            mesh=mesh,
            in_specs=placed,
            out_specs=(P(("row", "col"), None), P(("row", "col"), None), P(), P()),
            check_vma=False,
        )(*args)

    return run
```
